32 devices in a mesh: row: 8 (over z, y), col: 4 (over x, core).
Axes of the slice: x: 2, y: 2, z: 4, core: 2. Of those that a mesh axis runs over, the one named last changes fastest.
Arguments:
- tokens: bfloat16 [16384, 1024], P(('row', 'col')), may hold values from -6 to 6
- cotangent: bfloat16 [16384, 1024], P(('row', 'col')), may hold values from -6 to 6
- dest_slot: int32 [16384], replicated, may hold values from 0 to 16383, as said below
- lengths: int32 [32, 4], P(('row', 'col')), may hold values from 1 to 256, 512 in all within a row
- pad_mask: int32 [16384], P(('row', 'col')), may hold values 0 or 1
- based_gain: float32 [1024], replicated, may hold values from 0.1 to 1.9
- based_query: bfloat16 [1024, 256], P('row', 'col'), may hold values from -0.1875 to 0.1875
- based_key: bfloat16 [1024, 256], P('row', 'col'), may hold values from -0.1875 to 0.1875
- based_value: bfloat16 [1024, 1024], P('row', 'col'), may hold values from -0.1875 to 0.1875
- based_output: bfloat16 [1024, 1024], P('row', 'col'), may hold values from -1.5 to 1.5
- mlp_gain_one: float32 [1024], replicated, may hold values from 0.1 to 1.9
- mlp_gate_one: bfloat16 [1024, 2752], P('row', 'col'), may hold values from -0.1875 to 0.1875
- mlp_up_one: bfloat16 [1024, 2752], P('row', 'col'), may hold values from -0.1875 to 0.1875
- mlp_down_one: bfloat16 [2752, 1024], P('row', 'col'), may hold values from -0.109375 to 0.109375
- window_gain: float32 [1024], replicated, may hold values from 0.1 to 1.9
- window_query: bfloat16 [1024, 1024], P('row', 'col'), may hold values from -0.1875 to 0.1875
- window_key: bfloat16 [1024, 1024], P('row', 'col'), may hold values from -0.1875 to 0.1875
- window_value: bfloat16 [1024, 1024], P('row', 'col'), may hold values from -0.1875 to 0.1875
- window_output: bfloat16 [1024, 1024], P('row', 'col'), may hold values from -1 to 1
- mlp_gain_two: float32 [1024], replicated, may hold values from 0.1 to 1.9
- mlp_gate_two: bfloat16 [1024, 2752], P('row', 'col'), may hold values from -0.1875 to 0.1875
- mlp_up_two: bfloat16 [1024, 2752], P('row', 'col'), may hold values from -0.1875 to 0.1875
- mlp_down_two: bfloat16 [2752, 1024], P('row', 'col'), may hold values from -0.109375 to 0.109375
Outputs:
- output: bfloat16 [16384, 1024], P(('row', 'col'))
- tokens_grad: bfloat16 [16384, 1024], P(('row', 'col'))
- grad_based_gain: float32 [1024], replicated
- grad_based_query: float32 [1024, 256], P('row', 'col')
- grad_based_key: float32 [1024, 256], P('row', 'col')
- grad_based_value: float32 [1024, 1024], P('row', 'col')
- grad_based_output: float32 [1024, 1024], P('row', 'col')
- grad_mlp_gain_one: float32 [1024], replicated
- grad_mlp_gate_one: float32 [1024, 2752], P('row', 'col')
- grad_mlp_up_one: float32 [1024, 2752], P('row', 'col')
- grad_mlp_down_one: float32 [2752, 1024], P('row', 'col')
- grad_window_gain: float32 [1024], replicated
- grad_window_query: float32 [1024, 1024], P('row', 'col')
- grad_window_key: float32 [1024, 1024], P('row', 'col')
- grad_window_value: float32 [1024, 1024], P('row', 'col')
- grad_window_output: float32 [1024, 1024], P('row', 'col')
- grad_mlp_gain_two: float32 [1024], replicated
- grad_mlp_gate_two: float32 [1024, 2752], P('row', 'col')
- grad_mlp_up_two: float32 [1024, 2752], P('row', 'col')
- grad_mlp_down_two: float32 [2752, 1024], P('row', 'col')
The draws below stay inside these ranges and needn't reach their ends.
Inputs may be any that keep to these rules, and one draw needn't show every extreme that they name: dest_slot is a permutation. Blocks of 512 rows are numbered in order; block b sends its tokens only to blocks b2 with b2 % 4 == b % 4, exactly 64 to each such block, itself included. `lengths`: row b lists the sequences of packed block b in order; each row sums to 512.
All inputs are finite; a program needn't handle non-finite values. No bound on the sum of `pad_mask` on one device may be relied on, other than what follows from the above.
Results may differ from the reference program's by a relative error of at most 0.025.
Values may be sent and summed in bfloat16 or wider, within the bound.
No kernel may reach another device: no remote copies, remote signals or barrier semaphores. Data moves between devices by JAX's collectives and lax.ppermute only.
A program may use at most 256 MiB of HBM per device.

```python
import math
import jax
import jax.numpy as jnp
import numpy as np
from jax import lax

D = 1024
FF = 2752
HEADS = 16
FEAT = 16
HEAD_DIM = 64
WINDOW = 64
MAX_LEN = 256
QUERY_BLOCK_SIZE = 512
TOK_DEV = 512
SEQS = 4
GROUPS = 4
SHARE = 64
TOKENS = 16384
DEVICES = 32


def shuffle_one(one_key):
    return jax.random.permutation(one_key, TOK_DEV).astype(jnp.int32)


def draw_dest_slot(key, part):
    row_count = TOKENS // (TOK_DEV * GROUPS)
    send_key, place_key = jax.random.split(key)
    send_keys = jax.random.split(send_key, row_count * GROUPS)
    place_keys = jax.random.split(place_key, row_count * GROUPS)
    sending = jax.vmap(shuffle_one)(send_keys).reshape(row_count, GROUPS, TOK_DEV)
    placing = jax.vmap(shuffle_one)(place_keys).reshape(row_count, GROUPS, TOK_DEV)
    target_row = sending // SHARE
    offset = sending % SHARE
    source_row = jnp.arange(row_count, dtype=jnp.int32)[:, None, None]
    group_index = jnp.arange(GROUPS, dtype=jnp.int32)[None, :, None]
    local_slot = placing[target_row, group_index, source_row * SHARE + offset]
    slots = (target_row * GROUPS + group_index) * TOK_DEV + local_slot
    return slots.reshape(TOKENS).astype(jnp.int32)


def plant(array, rng, low, largest):
    index_at = [jax.random.randint(jax.random.fold_in(rng, axis), (), 0, length) for axis, length in enumerate(array.shape)]
    widest = array.shape.index(max(array.shape))
    next_to = index_at[:widest] + [(index_at[widest] + 1) % array.shape[widest]] + index_at[widest + 1:]
    return array.at[tuple(index_at)].set(low).at[tuple(next_to)].set(largest)


def steps_of(rng, shape, cuts, smallest, largest):
    gain, own = 1.0, jax.random.fold_in(rng, 6)
    for dim, shards_of in cuts:
        steps = jnp.exp(jax.random.uniform(jax.random.fold_in(own, dim), (shards_of,), jnp.float32, smallest / len(cuts), largest / len(cuts)))
        gain = gain * jnp.repeat(steps, shape[dim] // shards_of).reshape([-1 if axis == dim else 1 for axis in range(len(shape))])
    return gain


def length_profile(number_of, total, most, slope):
    weights = [(1 << 20) // math.isqrt(standing ** slope) + 1 for standing in range(2, number_of + 1)]
    spare, given = total - most - (number_of - 1), [1] * (number_of - 1)
    while spare > 0:
        candidates = [i for i in range(number_of - 1) if given[i] < most]
        mass, remaining = sum([weights[i] for i in candidates]), spare
        for i in candidates:
            addition = min(most - given[i], max(1, remaining * weights[i] // mass), spare)
            given[i] = given[i] + addition
            spare = spare - addition
    return np.array([most] + given)


def ragged(own_key, count, total, bound, lean):
    if count == 2:
        one = jax.random.randint(own_key, (), max(1, total - bound), min(bound, total - 1) + 1)
        return jnp.stack([one, total - one])
    sizes = jnp.asarray(length_profile(count, total, bound, lean), jnp.int32)
    pairs = (count - 1) // 2
    source_of, taker = sizes[1:1 + 2 * pairs:2], sizes[2:2 + 2 * pairs:2]
    slack = jnp.minimum(source_of - 1, bound - taker)
    shifted = jax.random.randint(jax.random.fold_in(own_key, 1), (pairs,), 0, 1 << 20) % (slack + 1)
    sizes = sizes.at[1:1 + 2 * pairs:2].set(source_of - shifted).at[2:2 + 2 * pairs:2].set(taker + shifted)
    return sizes[jax.random.permutation(jax.random.fold_in(own_key, 2), count)]


def centred(rng, shape, deviation, limit, shards=(), kind=jnp.bfloat16):
    values = jax.random.normal(rng, shape, jnp.float32) * deviation
    if len(shards) > 0:
        values = steps_of(rng, shape, shards, -0.22, 0.18) * values
    return jnp.clip(values, min=-limit, max=limit).astype(kind)


def setup_inputs(seed: int = 0) -> dict:
    splits = jax.random.split(jax.random.key(seed), 24)
    return {
        "tokens": centred(splits[0], (TOKENS, D), 1.0, 6.0, ((0, 32),)),
        "cotangent": centred(splits[1], (TOKENS, D), 1.0, 6.0, ((0, 32),)),
        "dest_slot": draw_dest_slot(jax.random.fold_in(splits[23], 71), 0),
        "lengths": jax.vmap(lambda own: ragged(own, SEQS, TOK_DEV, MAX_LEN, 2))(jax.random.split(splits[3], DEVICES)).reshape((DEVICES, SEQS)).astype(jnp.int32),
        "pad_mask": plant((jax.random.randint(splits[4], (TOKENS,), 0, 8) < 7).astype(jnp.int32), jax.random.fold_in(splits[4], 1), 0, 1),
        "based_gain": jnp.clip(1.0 + 0.18 * jax.random.normal(splits[5], (D,), jnp.float32), 0.1, 1.9),
        "based_query": centred(splits[6], (D, HEADS * FEAT), D ** -0.5, 0.1875, ((0, 8), (1, 4))),
        "based_key": centred(splits[7], (D, HEADS * FEAT), D ** -0.5, 0.1875, ((0, 8), (1, 4))),
        "based_value": centred(splits[8], (D, D), D ** -0.5, 0.1875, ((0, 8), (1, 4))),
        "based_output": centred(splits[9], (D, D), (D // 64) ** -0.5, 1.5, ((0, 8), (1, 4))),
        "mlp_gain_one": jnp.clip(1.0 + 0.18 * jax.random.normal(splits[10], (D,), jnp.float32), 0.1, 1.9),
        "mlp_gate_one": centred(splits[11], (D, FF), D ** -0.5, 0.1875, ((0, 8), (1, 4))),
        "mlp_up_one": centred(splits[12], (D, FF), D ** -0.5, 0.1875, ((0, 8), (1, 4))),
        "mlp_down_one": centred(splits[13], (FF, D), FF ** -0.5, 0.109375, ((0, 8), (1, 4))),
        "window_gain": jnp.clip(1.0 + 0.18 * jax.random.normal(splits[14], (D,), jnp.float32), 0.1, 1.9),
        "window_query": centred(splits[15], (D, D), D ** -0.5, 0.1875, ((0, 8), (1, 4))),
        "window_key": centred(splits[16], (D, D), D ** -0.5, 0.1875, ((0, 8), (1, 4))),
        "window_value": centred(splits[17], (D, D), D ** -0.5, 0.1875, ((0, 8), (1, 4))),
        "window_output": centred(splits[18], (D, D), (D // 32) ** -0.5, 1.0, ((0, 8), (1, 4))),
        "mlp_gain_two": jnp.clip(1.0 + 0.18 * jax.random.normal(splits[19], (D,), jnp.float32), 0.1, 1.9),
        "mlp_gate_two": centred(splits[20], (D, FF), D ** -0.5, 0.1875, ((0, 8), (1, 4))),
        "mlp_up_two": centred(splits[21], (D, FF), D ** -0.5, 0.1875, ((0, 8), (1, 4))),
        "mlp_down_two": centred(splits[22], (FF, D), FF ** -0.5, 0.109375, ((0, 8), (1, 4))),
    }


@jax.custom_vjp
def low(v):
    return lax.optimization_barrier(v.astype(jnp.bfloat16)).astype(jnp.float32)

@jax.custom_vjp
def lower_bound_back(v):
    return v

def low_keep(v):
    return (low(v), None)

def low_pass(kept, grad):
    return (grad,)

def back_keep(v):
    return (v, None)

def back_low(kept, grad):
    return (low(grad),)
low.defvjp(low_keep, low_pass)
lower_bound_back.defvjp(back_keep, back_low)
EPS = 1e-05
FULL_PRECISION = lax.Precision.HIGHEST

def round_both(quantity):
    return lower_bound_back(low(quantity))

def matmul(left_side, right_side):
    return jnp.dot(left_side, right_side, precision=FULL_PRECISION)

def rms_apply(residual, gain_vector):
    factor = lax.rsqrt(lax.optimization_barrier(jnp.mean(residual * residual, axis=-1, keepdims=True)) + EPS)
    return residual * factor * gain_vector

def pad_front(source, key_extent, fill_value):
    front_fill = jnp.full((key_extent,) + source.shape[1:], fill_value, source.dtype)
    return jnp.concatenate([front_fill, source], axis=0)

def key_rules(segment_pad, live_pad, block_first_row, key_extent, window_span):
    query_pos = block_first_row + jnp.arange(QUERY_BLOCK_SIZE, dtype=jnp.int32)
    key_pos = block_first_row - key_extent + jnp.arange(key_extent + QUERY_BLOCK_SIZE, dtype=jnp.int32)
    query_seg = segment_pad[block_first_row + key_extent:block_first_row + key_extent + QUERY_BLOCK_SIZE]
    key_seg = segment_pad[block_first_row:block_first_row + key_extent + QUERY_BLOCK_SIZE]
    key_live = live_pad[block_first_row:block_first_row + key_extent + QUERY_BLOCK_SIZE]
    earlier = (key_pos[None, :] <= query_pos[:, None]) & (key_pos[None, :] > query_pos[:, None] - window_span)
    same_seq = query_seg[:, None] == key_seg[None, :]
    usable = (key_live[None, :] > 0) | (key_pos[None, :] == query_pos[:, None])
    return earlier & same_seq & usable

def based_device(operands):
    query_rows, keys_in, values_in, segment, live_keys = operands
    key_extent = MAX_LEN
    logit_scale = FEAT ** (-0.5)
    padded_keys = pad_front(keys_in, key_extent, 0.0)
    values_pad = pad_front(values_in, key_extent, 0.0)
    segment_pad = pad_front(segment, key_extent, -1)
    live_pad = pad_front(live_keys, key_extent, 0)
    pieces = []
    for block_index in range(TOK_DEV // QUERY_BLOCK_SIZE):
        block_first_row = block_index * QUERY_BLOCK_SIZE
        allowed = key_rules(segment_pad, live_pad, block_first_row, key_extent, key_extent).astype(jnp.float32)
        score_matrix = lower_bound_back(jnp.einsum('nvx,ivx->vni', query_rows[block_first_row:block_first_row + QUERY_BLOCK_SIZE], padded_keys[block_first_row:block_first_row + key_extent + QUERY_BLOCK_SIZE], precision=FULL_PRECISION) * logit_scale)
        weights = (1.0 + score_matrix + 0.5 * score_matrix * score_matrix) * allowed[None]
        totals = lax.optimization_barrier(jnp.sum(weights, axis=-1))
        numerator = lower_bound_back(jnp.einsum('hqk,khe->qhe', low(weights), values_pad[block_first_row:block_first_row + key_extent + QUERY_BLOCK_SIZE], precision=FULL_PRECISION))
        pieces.append(numerator / jnp.transpose(totals)[:, :, None])
    return jnp.concatenate(pieces, axis=0)

def window_device(operands):
    query_rows, keys_in, values_in, segment, live_keys = operands
    key_extent = WINDOW
    logit_scale = HEAD_DIM ** (-0.5)
    padded_keys = pad_front(keys_in, key_extent, 0.0)
    values_pad = pad_front(values_in, key_extent, 0.0)
    segment_pad = pad_front(segment, key_extent, -1)
    live_pad = pad_front(live_keys, key_extent, 0)
    pieces = []
    for block_index in range(TOK_DEV // QUERY_BLOCK_SIZE):
        block_first_row = block_index * QUERY_BLOCK_SIZE
        allowed = key_rules(segment_pad, live_pad, block_first_row, key_extent, key_extent)
        score_matrix = lower_bound_back(jnp.einsum('nvx,ivx->vni', query_rows[block_first_row:block_first_row + QUERY_BLOCK_SIZE], padded_keys[block_first_row:block_first_row + key_extent + QUERY_BLOCK_SIZE], precision=FULL_PRECISION) * logit_scale)
        weights = jax.nn.softmax(jnp.where(allowed[None], score_matrix, -1e+30), axis=-1)
        pieces.append(jnp.einsum('hqk,khe->qhe', low(weights), values_pad[block_first_row:block_first_row + key_extent + QUERY_BLOCK_SIZE], precision=FULL_PRECISION))
    return jnp.concatenate(pieces, axis=0)

def mixer_all(device_kernel, query_rows, keys_in, values_in, segment, live_keys, feature_width):
    block_count = TOKENS // TOK_DEV
    shaped = (query_rows.reshape(block_count, TOK_DEV, HEADS, feature_width), keys_in.reshape(block_count, TOK_DEV, HEADS, feature_width), values_in.reshape(block_count, TOK_DEV, HEADS, HEAD_DIM), segment, live_keys)
    result = lax.map(jax.checkpoint(device_kernel), shaped)
    return result.reshape(TOKENS, D)

def layer_forward(residual, params, segment, live_keys, mixer_kind):
    gain_att, w_query, w_key, w_value, w_out, gain_mlp, w_gate, w_up, w_down = params
    normed = low(rms_apply(residual, gain_att))
    query_rows = round_both(matmul(normed, w_query))
    keys_in = round_both(matmul(normed, w_key))
    values_in = round_both(matmul(normed, w_value))
    if mixer_kind == 'based':
        mixed_out = low(mixer_all(based_device, query_rows, keys_in, values_in, segment, live_keys, FEAT))
    else:
        mixed_out = round_both(mixer_all(window_device, query_rows, keys_in, values_in, segment, live_keys, HEAD_DIM))
    residual = residual + lower_bound_back(matmul(mixed_out, w_out))
    normed_mlp = low(rms_apply(residual, gain_mlp))
    gate_pre = lower_bound_back(matmul(normed_mlp, w_gate))
    upward = lower_bound_back(matmul(normed_mlp, w_up))
    hidden = low(jax.nn.silu(gate_pre) * upward)
    return residual + lower_bound_back(matmul(hidden, w_down))

def reference(tokens, cotangent, dest_slot, lengths, pad_mask, based_gain, based_query, based_key, based_value, based_output, mlp_gain_one, mlp_gate_one, mlp_up_one, mlp_down_one, window_gain, window_query, window_key, window_value, window_output, mlp_gain_two, mlp_gate_two, mlp_up_two, mlp_down_two):
    route_order = jnp.argsort(dest_slot).astype(jnp.int32)
    sequence_ends = jnp.cumsum(lengths, axis=1).astype(jnp.int32)
    positions = jnp.arange(TOK_DEV, dtype=jnp.int32)
    segment = lax.optimization_barrier(jnp.sum((positions[None, :, None] >= sequence_ends[:, None, :]).astype(jnp.int32), axis=2)).astype(jnp.int32)
    live_keys = pad_mask.reshape(-1, TOK_DEV)
    start_resid = tokens[route_order].astype(jnp.float32)
    packed_cot = cotangent[route_order].astype(jnp.float32)
    first_params = tuple((weight.astype(jnp.float32) for weight in (based_gain, based_query, based_key, based_value, based_output, mlp_gain_one, mlp_gate_one, mlp_up_one, mlp_down_one)))
    second_params = tuple((weight.astype(jnp.float32) for weight in (window_gain, window_query, window_key, window_value, window_output, mlp_gain_two, mlp_gate_two, mlp_up_two, mlp_down_two)))

    def forward(residual, first_set, second_set):
        middle = layer_forward(residual, first_set, segment, live_keys, 'based')
        return layer_forward(middle, second_set, segment, live_keys, 'window')
    result, pullback = jax.vjp(forward, start_resid, first_params, second_params)
    d_start, d_first, d_second = pullback(packed_cot)
    output = result.astype(jnp.bfloat16)[dest_slot]
    tokens_grad = d_start.astype(jnp.bfloat16)[dest_slot]
    return (output, tokens_grad, d_first[0], d_first[1], d_first[2], d_first[3], d_first[4], d_first[5], d_first[6], d_first[7], d_first[8], d_second[0], d_second[1], d_second[2], d_second[3], d_second[4], d_second[5], d_second[6], d_second[7], d_second[8])
```

```python
import functools

import jax
import jax.numpy as jnp
from jax import lax
from jax.experimental import pallas as pl
from jax.experimental.pallas import tpu as pltpu
from jax.sharding import Mesh, PartitionSpec as P

HEADS = 16
FEAT = 16
HEAD_DIM = 64
WINDOW = 64
MAX_LEN = 256
D = 1024
T = 512
HALF = 256
EPS = 1e-05
NEG = -1e30
ROWS = 8
COLS = 4
FB = 344
FBP = 352
FFP = ROWS * FBP
FC = FFP // COLS

bf16, f32, i32 = jnp.bfloat16, jnp.float32, jnp.int32
NN, NT, TN = ((1,), (0,)), ((1,), (1,)), ((0,), (0,))


def dot(a, b, dims):
    return lax.dot_general(a, b, (dims, ((), ())), preferred_element_type=f32)


def call(body, grid, ins, outs, scratch=(), flops=0, prefetch=None):
    extra = 0 if prefetch is None else 1

    def spec(block, index):
        if block is None:
            return pl.BlockSpec(memory_space=pl.ANY)
        return pl.BlockSpec(block, index)

    in_specs, args = [], []
    for item in ins:
        if not isinstance(item, tuple):
            nd = item.ndim
            item = (item, item.shape, functools.partial(lambda n, *_: (0,) * n, nd))
        args.append(item[0])
        in_specs.append(spec(item[1], item[2]))
    out_specs = [spec(o[2], o[3]) for o in outs]
    out_shape = [jax.ShapeDtypeStruct(o[0], o[1]) for o in outs]
    moved = sum(a.size * a.dtype.itemsize for a in args)
    moved += sum(s.size * s.dtype.itemsize for s in out_shape)
    cost = pl.CostEstimate(flops=int(flops), bytes_accessed=int(moved), transcendentals=0)
    got = pl.pallas_call(
        body,
        out_shape=out_shape,
        grid_spec=pltpu.PrefetchScalarGridSpec(
            num_scalar_prefetch=extra,
            grid=grid,
            in_specs=in_specs,
            out_specs=out_specs,
            scratch_shapes=list(scratch),
        ),
        compiler_params=pltpu.CompilerParams(vmem_limit_bytes=56 * 2**20),
        cost_estimate=cost,
    )(*(([prefetch] if extra else []) + args))
    return got


def whole_map(*shape):
    zeros = (0,) * len(shape)
    return lambda *_: zeros


def norm_factor(h):
    return lax.rsqrt(jnp.mean(h * h, axis=-1, keepdims=True) + EPS)


def norm_proj(h, gain, weights):
    n = len(weights)

    def body(h_ref, gain_ref, *refs):
        xa_ref, outs = refs[n], refs[n + 1 :]

        @pl.when(pl.program_id(0) == 0)
        def _():
            hv = h_ref[...].astype(f32)
            xa_ref[...] = (hv * norm_factor(hv) * gain_ref[...]).astype(bf16)

        for w_ref, o_ref in zip(refs[:n], outs):
            o_ref[...] = dot(xa_ref[...], w_ref[...], NN).astype(bf16)

    ins = [h, gain.reshape(1, D)]
    outs = [((T, D), bf16, (T, D), whole_map(T, D))]
    for w in weights:
        wide = w.shape[1] // COLS
        ins.append((w, (D, wide), lambda i: (0, i)))
        outs.append(((T, w.shape[1]), bf16, (T, wide), lambda i: (0, i)))
    total = sum(w.shape[1] for w in weights)
    return call(body, (COLS,), ins, outs, flops=2 * T * D * total)


def lanes(shape, width):
    return lax.broadcasted_iota(i32, shape, len(shape) - 1) // width


def fill_mask(mask_ref, seg_q, seg_k, live_k, q_axis, window):
    q = lax.broadcasted_iota(i32, (T, T), q_axis)
    k = lax.broadcasted_iota(i32, (T, T), 1 - q_axis)
    ok = (k <= q) & (k > q - window) & (seg_q == seg_k) & ((live_k > 0) | (k == q))
    mask_ref[...] = jnp.where(ok, 1.0, 0.0)


def based_fwd(qk, v, seg_row, seg_col, live_row):
    def body(qk_ref, v_ref, sr_ref, sc_ref, lr_ref, o_ref, ou_ref, rden_ref, mask_ref):
        @pl.when(pl.program_id(0) == 0)
        def _():
            fill_mask(mask_ref, sc_ref[...], sr_ref[...], lr_ref[...], 0, MAX_LEN)

        q4, k4 = qk_ref[:, 0:64], qk_ref[:, 64:128]
        qlane = lanes((T, 64), FEAT)
        first = lanes((HALF, 128), HEAD_DIM) == 0
        scaled = q4.astype(f32) * (FEAT**-0.5)
        for pair in range(2):
            v2 = v_ref[:, pair * 128 : pair * 128 + 128]
            for tb in range(2):
                t0, s1 = tb * HALF, (tb + 1) * HALF
                got = []
                for e in range(2):
                    qm = jnp.where(qlane == pair * 2 + e, scaled, 0.0).astype(bf16)
                    a = dot(qm[t0 : t0 + HALF], k4[0:s1], NT)
                    p = (1.0 + a * (1.0 + 0.5 * a)) * mask_ref[t0 : t0 + HALF, 0:s1]
                    den = jnp.sum(p, axis=-1, keepdims=True)
                    got.append((dot(p.astype(bf16), v2[0:s1], NN), den))
                rden = 1.0 / jnp.where(first, got[0][1], got[1][1])
                ou = jnp.where(first, got[0][0], got[1][0]) * rden
                at = (slice(t0, t0 + HALF), slice(pair * 128, pair * 128 + 128))
                ou_ref[at] = ou
                rden_ref[at] = rden
                o_ref[at] = ou.astype(bf16)

    wide = (T, 256)
    col = lambda c: (0, c)
    return call(
        body,
        (4,),
        [(qk, (T, 128), col), (v, wide, col), seg_row, seg_col, live_row],
        [((T, D), bf16, wide, col), ((T, D), f32, wide, col), ((T, D), f32, wide, col)],
        scratch=[pltpu.VMEM((T, T), f32)],
        flops=HEADS * T * T * 2 * 192,
    )


def based_bwd(qk, v, dou, ou, rden, seg_row, seg_col, live_col):
    def body(qk_ref, v_ref, dou_ref, ou_ref, rden_ref, sr_ref, sc_ref, lc_ref, dqk_ref, dv_ref, mask_ref, dk_ref, dva_ref):
        @pl.when(pl.program_id(0) == 0)
        def _():
            fill_mask(mask_ref, sr_ref[...], sc_ref[...], lc_ref[...], 1, MAX_LEN)

        q4, k4 = qk_ref[:, 0:64], qk_ref[:, 64:128]
        qlane = lanes((T, 64), FEAT)
        q_scaled = q4.astype(f32) * (FEAT**-0.5)
        k_scaled = k4.astype(f32) * (FEAT**-0.5)
        vlane = lanes((T, 128), HEAD_DIM)
        dnum_f = dou_ref[...] * rden_ref[...]
        term = dnum_f * ou_ref[...]
        high = term.astype(bf16)
        low = (term - high.astype(f32)).astype(bf16)
        pick = jnp.where(
            lax.broadcasted_iota(i32, (8, 256), 0) == lanes((8, 256), HEAD_DIM), 1.0, 0.0
        ).astype(bf16)
        dden = -(dot(pick, high, NT) + dot(pick, low, NT))
        dk_ref[...] = jnp.zeros((T, 64), f32)
        dva_ref[...] = jnp.zeros((T, 256), f32)
        dq = [jnp.zeros((HALF, 64), f32), jnp.zeros((HALF, 64), f32)]
        for pair in range(2):
            cols = slice(pair * 128, pair * 128 + 128)
            v2 = v_ref[:, cols]
            for e in range(2):
                head = pair * 2 + e
                qm = jnp.where(qlane == head, q_scaled, 0.0).astype(bf16)
                km = jnp.where(qlane == head, k_scaled, 0.0).astype(bf16)
                dn = jnp.where(vlane == e, dnum_f[:, cols], 0.0).astype(bf16)
                for tb in range(2):
                    t0, s1 = tb * HALF, (tb + 1) * HALF
                    at = slice(t0, t0 + HALF)
                    a = dot(k4[0:s1], qm[at], NT)
                    m = mask_ref[0:s1, at]
                    p = (1.0 + a * (1.0 + 0.5 * a)) * m
                    dp = dot(v2[0:s1], dn[at], NT) + dden[head : head + 1, at]
                    da = (dp * m * (1.0 + a)).astype(bf16)
                    dk_ref[0:s1, :] += dot(da, qm[at], NN)
                    dva_ref[0:s1, cols] += dot(p.astype(bf16), dn[at], NN)
                    dq[tb] += dot(da, km[0:s1], TN)
        for tb in range(2):
            at = slice(tb * HALF, tb * HALF + HALF)
            dqk_ref[at, 0:64] = dq[tb].astype(bf16)
        dqk_ref[:, 64:128] = dk_ref[...].astype(bf16)
        dv_ref[...] = dva_ref[...].astype(bf16)

    wide = (T, 256)
    col = lambda c: (0, c)
    return call(
        body,
        (4,),
        [(qk, (T, 128), col), (v, wide, col), (dou, wide, col), (ou, wide, col), (rden, wide, col), seg_row, seg_col, live_col],
        [((T, 512), bf16, (T, 128), col), ((T, D), bf16, wide, col)],
        scratch=[pltpu.VMEM((T, T), f32), pltpu.VMEM((T, 64), f32), pltpu.VMEM((T, 256), f32)],
        flops=HEADS * T * T * 2 * 480,
    )


SPAN = ((0, HALF), (HALF - WINDOW, T))


def window_fwd(q, k, v, seg_row, seg_col, live_row):
    def body(q_ref, k_ref, v_ref, sr_ref, sc_ref, lr_ref, o_ref, mask_ref):
        @pl.when(pl.program_id(0) == 0)
        def _():
            fill_mask(mask_ref, sc_ref[...], sr_ref[...], lr_ref[...], 0, WINDOW)

        first = lanes((HALF, 128), HEAD_DIM) == 0
        qlane = lanes((T, 128), HEAD_DIM)
        scaled = q_ref[...].astype(f32) * (HEAD_DIM**-0.5)
        for tb in range(2):
            t0 = tb * HALF
            s0, s1 = SPAN[tb]
            ok = mask_ref[t0 : t0 + HALF, s0:s1] > 0.5
            got = []
            for e in range(2):
                qm = jnp.where(qlane == e, scaled, 0.0).astype(bf16)
                c = dot(qm[t0 : t0 + HALF], k_ref[s0:s1, :], NT)
                c = jnp.where(ok, c, NEG)
                w = jnp.exp(c - jnp.max(c, axis=-1, keepdims=True))
                w = w * (1.0 / jnp.sum(w, axis=-1, keepdims=True))
                got.append(dot(w.astype(bf16), v_ref[s0:s1, :], NN))
            o_ref[t0 : t0 + HALF, :] = jnp.where(first, got[0], got[1]).astype(bf16)

    blk = (T, 128)
    col = lambda c: (0, c)
    return call(
        body,
        (8,),
        [(q, blk, col), (k, blk, col), (v, blk, col), seg_row, seg_col, live_row],
        [((T, D), bf16, blk, col)],
        scratch=[pltpu.VMEM((T, T), f32)],
        flops=HEADS * T * T * 2 * 192,
    )[0]


def window_bwd(q, k, v, dor, seg_row, seg_col, live_col):
    def body(q_ref, k_ref, v_ref, do_ref, sr_ref, sc_ref, lc_ref, dq_ref, dk_ref, dv_ref, mask_ref, dka_ref, dva_ref):
        @pl.when(pl.program_id(0) == 0)
        def _():
            fill_mask(mask_ref, sr_ref[...], sc_ref[...], lc_ref[...], 1, WINDOW)

        lane = lanes((T, 128), HEAD_DIM)
        q_scaled = q_ref[...].astype(f32) * (HEAD_DIM**-0.5)
        k_scaled = k_ref[...].astype(f32) * (HEAD_DIM**-0.5)
        do = do_ref[...]
        dka_ref[...] = jnp.zeros((T, 128), f32)
        dva_ref[...] = jnp.zeros((T, 128), f32)
        for tb in range(2):
            at = slice(tb * HALF, tb * HALF + HALF)
            s0, s1 = SPAN[tb]
            ok = mask_ref[s0:s1, at] > 0.5
            dq = jnp.zeros((HALF, 128), f32)
            for e in range(2):
                qm = jnp.where(lane == e, q_scaled, 0.0).astype(bf16)
                km = jnp.where(lane == e, k_scaled, 0.0).astype(bf16)
                dm = jnp.where(lane == e, do, jnp.zeros_like(do))
                c = dot(k_ref[s0:s1, :], qm[at], NT)
                c = jnp.where(ok, c, NEG)
                w = jnp.exp(c - jnp.max(c, axis=0, keepdims=True))
                w = w * (1.0 / jnp.sum(w, axis=0, keepdims=True))
                dw = dot(v_ref[s0:s1, :], dm[at], NT)
                ds = (w * (dw - jnp.sum(w * dw, axis=0, keepdims=True))).astype(bf16)
                dka_ref[s0:s1, :] += dot(ds, qm[at], NN)
                dva_ref[s0:s1, :] += dot(w.astype(bf16), dm[at], NN)
                dq += dot(ds, km[s0:s1], TN)
            dq_ref[at, :] = dq.astype(bf16)
        dk_ref[...] = dka_ref[...].astype(bf16)
        dv_ref[...] = dva_ref[...].astype(bf16)

    blk = (T, 128)
    col = lambda c: (0, c)
    return call(
        body,
        (8,),
        [(q, blk, col), (k, blk, col), (v, blk, col), (dor, blk, col), seg_row, seg_col, live_col],
        [((T, D), bf16, blk, col)] * 3,
        scratch=[pltpu.VMEM((T, T), f32), pltpu.VMEM((T, 128), f32), pltpu.VMEM((T, 128), f32)],
        flops=HEADS * T * T * 2 * 480,
    )


def attn_out(h, o, w_out, gain):
    def body(h_ref, o_ref, w_ref, gain_ref, hm_ref, xf_ref):
        hm = h_ref[...].astype(f32) + dot(o_ref[...], w_ref[...], NN)
        hm_ref[...] = hm
        xf_ref[...] = (hm * norm_factor(hm) * gain_ref[...]).astype(bf16)

    full = whole_map(T, D)
    return call(
        body,
        (1,),
        [h, o, w_out, gain.reshape(1, D)],
        [((T, D), f32, (T, D), full), ((T, D), bf16, (T, D), full)],
        flops=2 * T * D * D,
    )


def gate_up(xf, w_gate, w_up):
    def body(xf_ref, wg_ref, wu_ref, g_ref, u_ref, hid_ref):
        xfv = xf_ref[...]
        g = dot(wg_ref[...], xfv, NT)
        u = dot(wu_ref[...], xfv, NT)
        g_ref[...] = g.astype(bf16)
        u_ref[...] = u.astype(bf16)
        hid_ref[...] = (g * (1.0 / (1.0 + jnp.exp(-g))) * u).astype(bf16)

    wblk, oblk, row = (FC, D), (FC, T), lambda i: (i, 0)
    return call(
        body,
        (COLS,),
        [xf, (w_gate, wblk, row), (w_up, wblk, row)],
        [((FFP, T), bf16, oblk, row)] * 3,
        flops=4 * T * D * FFP,
    )


def down(hm, hid, w_down):
    def body(hm_ref, hid_ref, w_ref, h_ref):
        part = dot(hid_ref[...], w_ref[...], TN)

        @pl.when(pl.program_id(0) == 0)
        def _():
            h_ref[...] = hm_ref[...] + part

        @pl.when(pl.program_id(0) > 0)
        def _():
            h_ref[...] += part

    row = lambda i: (i, 0)
    return call(
        body,
        (COLS,),
        [hm, (hid, (FC, T), row), (w_down, (FC, D), row)],
        [((T, D), f32, (T, D), whole_map(T, D))],
        flops=2 * T * D * FFP,
    )[0]


def relative(me, z, y, x, core):
    return z ^ me[0], y ^ me[1], x ^ me[2], core ^ me[3]


def down_bwd(me, bd, w_down, hid, g, u):
    def body(me_ref, bd_ref, w_ref, hid_ref, g_ref, u_ref, dg_ref, du_ref, p1_ref, p2_ref):
        bdv = bd_ref[...]
        gwd = dot(hid_ref[...], bdv, NN).astype(bf16)
        for x in range(2):
            for core in range(2):
                _, _, xr, cr = relative(me_ref, 0, 0, x, core)
                at = (x * 2 + core) * 256
                p1_ref[cr, xr, 0, 0] = gwd[:, at : at + 128]
                p2_ref[cr, 0, xr, 0] = gwd[:, at + 128 : at + 256]
        dhid = dot(w_ref[...], bdv, NT)
        gv, uv = g_ref[...].astype(f32), u_ref[...].astype(f32)
        sig = 1.0 / (1.0 + jnp.exp(-gv))
        act = gv * sig
        du_ref[...] = (dhid * act).astype(bf16)
        dg_ref[...] = (dhid * uv * (sig + act * (1.0 - sig))).astype(bf16)

    row = lambda i, me: (i, 0)
    hblk = (FBP, T)
    return call(
        body,
        (ROWS,),
        [bd, (w_down, (FBP, D), row), (hid, hblk, row), (g, hblk, row), (u, hblk, row)],
        [
            ((FFP, T), bf16, hblk, row),
            ((FFP, T), bf16, hblk, row),
            ((2, 2, 2, 4, FBP, 128), bf16, (2, 2, 1, 1, FBP, 128), lambda i, me: (0, 0, (i % 2) ^ me[1], (i // 2) ^ me[0], 0, 0)),
            ((2, 2, 2, 4, FBP, 128), bf16, (2, 1, 2, 1, FBP, 128), lambda i, me: (0, (i % 2) ^ me[1], 0, (i // 2) ^ me[0], 0, 0)),
        ],
        flops=4 * T * D * FFP,
        prefetch=me,
    )


def store_col(me_ref, out_ref, swapped, tile, rows, at):
    for z in range(4):
        for y in range(2):
            zr, yr, _, _ = relative(me_ref, z, y, 0, 0)
            r = (z * 2 + y) * 128
            part = tile[r : r + 128]
            if swapped:
                out_ref[0, yr, 0, zr, at : at + rows] = part
            else:
                out_ref[0, 0, yr, zr, at : at + rows] = part


def gate_up_bwd(me, xf, dg, du):
    def body(me_ref, xf_ref, dg_ref, du_ref, p1_ref, p2_ref):
        xfv = xf_ref[...]
        gwg = dot(dg_ref[...], xfv, NN).astype(bf16)
        gwu = dot(du_ref[...], xfv, NN).astype(bf16)
        for z in range(4):
            for y in range(2):
                zr, yr, _, _ = relative(me_ref, z, y, 0, 0)
                r = (z * 2 + y) * 128
                p1_ref[0, 0, yr, zr] = gwg[:, r : r + 128]
                p2_ref[0, yr, 0, zr] = gwu[:, r : r + 128]

    row = lambda i, me: (i, 0)
    return call(
        body,
        (COLS,),
        [xf, (dg, (FC, T), row), (du, (FC, T), row)],
        [
            ((2, 2, 2, 4, FC, 128), bf16, (1, 1, 2, 4, FC, 128), lambda i, me: ((i % 2) ^ me[3], (i // 2) ^ me[2], 0, 0, 0, 0)),
            ((2, 2, 2, 4, FC, 128), bf16, (1, 2, 1, 4, FC, 128), lambda i, me: ((i % 2) ^ me[3], 0, (i // 2) ^ me[2], 0, 0, 0)),
        ],
        flops=4 * T * D * FFP,
        prefetch=me,
    )


def norm_bwd(dx, h, gain, g):
    rf = norm_factor(h)
    hr = h * rf
    dgain = jnp.sum(dx * hr, axis=0, keepdims=True)
    gd = gain * dx
    mean = jnp.sum(gd * hr, axis=-1, keepdims=True) * (1.0 / D)
    return dgain, g + rf * (gd - hr * mean)


def mlp_dx(dg, du, w_gate, w_up, hm, gain, g):
    def body(dg_ref, du_ref, wg_ref, wu_ref, hm_ref, gain_ref, g_ref, gm_ref, bo_ref, gg_ref):
        part = dot(dg_ref[...], wg_ref[...], TN) + dot(du_ref[...], wu_ref[...], TN)
        i = pl.program_id(0)

        @pl.when(i == 0)
        def _():
            gm_ref[...] = part

        @pl.when((i > 0) & (i < COLS - 1))
        def _():
            gm_ref[...] += part

        @pl.when(i == COLS - 1)
        def _():
            gg, gm = norm_bwd(gm_ref[...] + part, hm_ref[...], gain_ref[...], g_ref[...].astype(f32))
            gg_ref[...] = gg
            gm_ref[...] = gm
            bo_ref[...] = gm.astype(bf16)

    row = lambda i: (i, 0)
    full = whole_map(T, D)
    return call(
        body,
        (COLS,),
        [(dg, (FC, T), row), (du, (FC, T), row), (w_gate, (FC, D), row), (w_up, (FC, D), row), hm, gain.reshape(1, D), g],
        [((T, D), f32, (T, D), full), ((T, D), bf16, (T, D), full), ((1, D), f32, (1, D), full)],
        flops=4 * T * D * FFP,
    )


def attn_dout(bo, w_out, kind):
    def body(bo_ref, w_ref, dou_ref):
        dou_ref[...] = dot(bo_ref[...], w_ref[...], NT).astype(kind)

    return call(
        body,
        (COLS,),
        [bo, (w_out, (256, D), lambda i: (i, 0))],
        [((T, D), kind, (T, 256), lambda i: (0, i))],
        flops=2 * T * D * D,
    )[0]


def attn_bwd(me, xa, grads, weights, o, bo, h, gain, gm, halves):
    n = len(grads)
    first, second = halves

    def body(me_ref, xa_ref, o_ref, h_ref, gain_ref, gm_ref, bo_ref, *refs):
        d_refs, w_refs = refs[:n], refs[n : 2 * n]
        p1_ref, p2_ref, g_ref, gg_ref = refs[2 * n :]
        xav = xa_ref[...]
        tiles = [dot(xav, d[...], TN).astype(bf16) for d in d_refs]
        tiles.append(dot(o_ref[...], bo_ref[...], TN).astype(bf16))
        for ref, strips, swapped in ((p1_ref, first, False), (p2_ref, second, True)):
            for j, (which, at) in enumerate(strips):
                store_col(me_ref, ref, swapped, tiles[which][:, at : at + 128], 128, j * 128)
        part = dot(d_refs[0][...], w_refs[0][...], NT)
        for d, w in zip(d_refs[1:], w_refs[1:]):
            part += dot(d[...], w[...], NT)
        i = pl.program_id(0)

        @pl.when(i == 0)
        def _():
            g_ref[...] = part

        @pl.when((i > 0) & (i < COLS - 1))
        def _():
            g_ref[...] += part

        @pl.when(i == COLS - 1)
        def _():
            gg, g = norm_bwd(g_ref[...] + part, h_ref[...].astype(f32), gain_ref[...], gm_ref[...])
            gg_ref[...] = gg
            g_ref[...] = g

    col = lambda i, me: (0, i)
    full = whole_map(T, D)
    n1, n2 = 128 * len(first), 128 * len(second)
    ins = [xa, o, h, gain.reshape(1, D), gm, (bo, (T, 256), col)]
    ins += [(d, (T, d.shape[1] // COLS), col) for d in grads]
    ins += [(w, (D, w.shape[1] // COLS), col) for w in weights]
    total = sum(w.shape[1] for w in weights)
    return call(
        body,
        (COLS,),
        ins,
        [
            ((2, 2, 2, 4, n1, 128), bf16, (1, 1, 2, 4, n1, 128), lambda i, me: ((i % 2) ^ me[3], (i // 2) ^ me[2], 0, 0, 0, 0)),
            ((2, 2, 2, 4, n2, 128), bf16, (1, 2, 1, 4, n2, 128), lambda i, me: ((i % 2) ^ me[3], 0, (i // 2) ^ me[2], 0, 0, 0)),
            ((T, D), f32, (T, D), full),
            ((1, D), f32, (1, D), full),
        ],
        flops=4 * T * D * total + 2 * T * D * D,
        prefetch=me,
    )


def assemble(me, bufs, jobs, shapes):
    n_out = len(shapes)

    def body(me_ref, *refs):
        halves = (refs[0:4], refs[4:8])
        outs, sems = refs[8 : 8 + n_out], refs[8 + n_out]
        for core_rel in range(2):
            for hi in range(2):

                @pl.loop(0, 8)
                def _(i):
                    lo, zr = i // 4, i % 4
                    for half, src, rows, out, rs, cs, cb in jobs:
                        yr, xr = (hi, lo) if half == 0 else (lo, hi)
                        z, y, x, core = relative(me_ref, zr, yr, xr, core_rel)
                        r, c = z * 2 + y, x * 2 + core
                        r0 = pl.multiple_of(r * rs[0] + c * rs[1], 16)
                        c0 = pl.multiple_of(r * cs[0] + c * cs[1] + cb, 128)
                        pltpu.make_async_copy(
                            halves[half][core_rel * 2 + hi].at[lo, zr, pl.ds(src, rows)],
                            outs[out].at[pl.ds(r0, rows), pl.ds(c0, 128)],
                            sems.at[out],
                        ).start()
        for j in range(n_out):
            pltpu.make_async_copy(outs[j], outs[j], sems.at[j]).wait()

    ins = [(b, None, None) for half in bufs for b in half]
    outs = [(s, bf16, None, None) for s in shapes]
    return call(body, (1,), ins, outs, scratch=[pltpu.SemaphoreType.DMA((n_out,))], prefetch=me)


HALVES_ONE = (((1, 0), (1, 128)), ((0, 0), (2, 0), (2, 128)))
HALVES_TWO = (((0, 0), (0, 128), (1, 0), (1, 128)), ((2, 0), (2, 128), (3, 0), (3, 128)))


def attn_jobs(halves, widths):
    jobs = []
    for half, strips in enumerate(halves):
        for j, (which, at) in enumerate(strips):
            jobs.append((half, j * 128, 128, which, (128, 0), (0, widths[which]), at))
    return jobs


GU_JOBS = [(0, 0, FC, 0, (0, FC), (128, 0), 0), (1, 0, FC, 1, (0, FC), (128, 0), 0)]
DOWN_JOBS = [(0, 0, FBP, 0, (FBP, 0), (0, 256), 0), (1, 0, FBP, 0, (FBP, 0), (0, 256), 128)]


def pad_hidden(w):
    k = w.shape[0]
    return jnp.pad(w.reshape(k, -1, FB), ((0, 0), (0, 0), (0, FBP - FB))).reshape(k, -1).T


def pad_rows(w):
    n = w.shape[1]
    return jnp.pad(w.reshape(-1, FB, n), ((0, 0), (0, FBP - FB), (0, 0))).reshape(-1, n)


def strips_of(blocks, halves):
    return tuple(
        jnp.concatenate([blocks[which][:, at : at + 128] for which, at in strips], axis=0) for strips in halves
    )


class Ring:
    def __init__(self):
        self.axes = ("row", "col")

    def swap(self, value, axis, by=1):
        pairs = []
        for i in range(32):
            z, y, x, c = i >> 3, (i >> 2) & 1, (i >> 1) & 1, i & 1
            if axis == "z":
                z ^= by
            elif axis == "y":
                y ^= 1
            elif axis == "x":
                x ^= 1
            else:
                c ^= 1
            pairs.append((i, (z << 3) | (y << 2) | (x << 1) | c))
        return lax.ppermute(value, self.axes, pairs)

    def gather(self, one, two):
        n1 = one.shape[0]
        both = jnp.concatenate([one, two], axis=0)
        near = [both] + [self.swap(both, "z", by) for by in (1, 2, 3)]
        full = []
        for part, (lo, hi) in ((slice(0, n1), "xy"), (slice(n1, None), "yx")):
            mine = jnp.stack([b[part] for b in near])
            own = jnp.stack([mine, self.swap(mine, lo)])
            far = self.swap(own, hi)
            full.append([own, far, self.swap(own, "core"), self.swap(far, "core")])
        return full

    def reduce(self, one, two):
        done = []
        for g, (lo, hi) in ((one, "xy"), (two, "yx")):
            h = g[0] + self.swap(g[1], "core")
            h = h[0] + self.swap(h[1], lo)
            h = h[0] + self.swap(h[1], hi)
            done.append(h)
        n1 = done[0].shape[1]
        both = jnp.concatenate(done, axis=1)
        total = both[0].astype(f32)
        for by in (1, 2, 3):
            total = total + self.swap(both[by], "z", by).astype(f32)
        return total[:n1], total[n1:]


def fetch_ring(ring, me, shards, halves):
    *attn, gate, up, dn = shards
    widths = [w.shape[1] for w in attn]
    a = ring.gather(*strips_of(attn, halves))
    attn_full = assemble(me, a, attn_jobs(halves, widths), [(D, w * COLS) for w in widths])
    gu = ring.gather(pad_hidden(gate), pad_hidden(up))
    gu_full = assemble(me, gu, GU_JOBS, [(FFP, D)] * 2)
    dp = pad_rows(dn)
    d = ring.gather(dp[:, 0:128], dp[:, 128:256])
    d_full = assemble(me, d, DOWN_JOBS, [(FFP, D)])
    return list(attn_full) + list(gu_full) + list(d_full)


def fetch_any(shards):
    full = [
        lax.all_gather(lax.all_gather(w, "col", axis=1, tiled=True), "row", axis=0, tiled=True) for w in shards
    ]
    return full[:-3] + [pad_hidden(full[-3]), pad_hidden(full[-2]), pad_rows(full[-1])]


def unpad_hidden(g):
    k = g.shape[1]
    return g.reshape(-1, FBP, k)[:, :FB].reshape(-1, k).T


def unpad_rows(g):
    n = g.shape[1]
    return g.reshape(-1, FBP, n)[:, :FB].reshape(-1, n)


def whole_grad(p, swapped):
    if swapped:
        p = jnp.swapaxes(p, 1, 2)
    core, x, y, z, n, w = p.shape
    return p.transpose(3, 2, 1, 0, 4, 5).reshape(z * y, x * core, n, w)


def join_strips(one, two, halves, widths):
    out = []
    for which, width in enumerate(widths):
        got = {}
        for src, strips in ((one, halves[0]), (two, halves[1])):
            for j, (w, at) in enumerate(strips):
                if w == which:
                    got[at] = src[..., j * 128 : j * 128 + 128, :]
        out.append(jnp.concatenate([got[a] for a in sorted(got)], axis=-1))
    return out


def scatter_any(w):
    part = lax.psum_scatter(w, "row", scatter_dimension=0, tiled=True)
    return lax.psum_scatter(part, "col", scatter_dimension=1, tiled=True).astype(f32)


def natural(blocks):
    r, c, n, w = blocks.shape
    return blocks.transpose(0, 2, 1, 3).reshape(r * n, c * w)


def sum_down(ring, one, two):
    if ring:
        a, b = ring.reduce(one, two)
        return unpad_rows(jnp.concatenate([a, b], axis=1))
    whole = jnp.concatenate([whole_grad(one, False), whole_grad(two, True)], axis=-1)
    return scatter_any(unpad_rows(natural(whole)))


def sum_gate_up(ring, one, two):
    if ring:
        a, b = ring.reduce(one, two)
        return unpad_hidden(a), unpad_hidden(b)
    out = []
    for g, swapped in ((one, False), (two, True)):
        whole = whole_grad(g, swapped).transpose(1, 2, 0, 3).reshape(FFP, D)
        out.append(scatter_any(unpad_hidden(whole)))
    return tuple(out)


def sum_attn(ring, one, two, halves, widths):
    if ring:
        a, b = ring.reduce(one, two)
        return join_strips(a, b, halves, widths)
    blocks = join_strips(whole_grad(one, False), whole_grad(two, True), halves, widths)
    return [scatter_any(natural(b)) for b in blocks]


def join_qk(q, k, parts):
    n = q.shape[0]
    both = jnp.concatenate([q.reshape(n, parts, -1), k.reshape(n, parts, -1)], axis=2)
    return both.reshape(n, -1)


def route_plan(dest_slot, block_tokens):
    row_count = lax.axis_size("row")
    col_count = lax.axis_size("col")
    per_peer = block_tokens // row_count
    row_at = lax.axis_index("row")
    col_at = lax.axis_index("col")
    slot_table = dest_slot.reshape(row_count, col_count, block_tokens)
    column = lax.dynamic_index_in_dim(slot_table, col_at, 1, False)
    own_slots = lax.dynamic_index_in_dim(column, row_at, 0, False)
    send_order = jnp.argsort(own_slots)
    arrived = jnp.sort(column, axis=1)
    incoming = lax.dynamic_slice_in_dim(arrived, row_at * per_peer, per_peer, 1)
    local_slots = incoming.reshape(-1) - (row_at * col_count + col_at) * block_tokens
    placing = jnp.argsort(local_slots)
    return (send_order, local_slots, placing)


def exchange(rows, row_count):
    n, width = rows.shape
    got = lax.all_to_all(rows.reshape(row_count, n // row_count, width), "row", split_axis=0, concat_axis=0, tiled=True)
    return got.reshape(n, width)


def body(tokens, cotangent, dest_slot, lengths, pad_mask, *params):
    n_rows, n_cols = lax.axis_size("row"), lax.axis_size("col")
    ring = Ring() if (n_rows, n_cols) == (ROWS, COLS) else None
    gain_a1, bq, bk, bv, bo_w, gain_m1, wg1, wu1, wd1 = params[:9]
    gain_a2, wq, wk, wv, wo2, gain_m2, wg2, wu2, wd2 = params[9:]
    if ring:
        row, col = lax.axis_index("row"), lax.axis_index("col")
        me = jnp.stack([row // 2, row % 2, col // 2, col % 2]).astype(i32)
        one = fetch_ring(ring, me, [join_qk(bq, bk, 1), bv, bo_w, wg1, wu1, wd1], HALVES_ONE)
        two = fetch_ring(ring, me, [wq, wk, wv, wo2, wg2, wu2, wd2], HALVES_TWO)
    else:
        me = jnp.zeros((4,), i32)
        got = fetch_any([bq, bk, bv, bo_w, wg1, wu1, wd1])
        one = [join_qk(got[0], got[1], COLS)] + got[2:]
        two = fetch_any([wq, wk, wv, wo2, wg2, wu2, wd2])
    send_order, local_slots, placing = route_plan(dest_slot, T)
    start = exchange(tokens[send_order], n_rows)[placing]
    cot = exchange(cotangent[send_order], n_rows)[placing]
    position = jnp.arange(T, dtype=i32)
    segment, end = jnp.zeros((T,), i32), jnp.zeros((), i32)
    for j in range(lengths.shape[1]):
        end = end + lengths[0, j]
        segment = segment + (position >= end).astype(i32)
    seg_row, seg_col = segment.reshape(1, T), segment.reshape(T, 1)
    live_row, live_col = pad_mask.reshape(1, T), pad_mask.reshape(T, 1)

    w_qk, w_v, w_o, w_g, w_u, w_d = one
    xa1, qk1, v1 = norm_proj(start, gain_a1, [w_qk, w_v])
    o1, ou1, rden1 = based_fwd(qk1, v1, seg_row, seg_col, live_row)
    hm1, xf1 = attn_out(start, o1, w_o, gain_m1)
    g1, u1, hid1 = gate_up(xf1, w_g, w_u)
    h1 = down(hm1, hid1, w_d)
    v_q, v_k, v_v, v_o, v_g, v_u, v_d = two
    xa2, q2, k2, v2 = norm_proj(h1, gain_a2, [v_q, v_k, v_v])
    o2 = window_fwd(q2, k2, v2, seg_row, seg_col, live_row)
    hm2, xf2 = attn_out(h1, o2, v_o, gain_m2)
    g2, u2, hid2 = gate_up(xf2, v_g, v_u)
    h2 = down(hm2, hid2, v_d)
    dg2, du2, *pd2 = down_bwd(me, cot, v_d, hid2, g2, u2)
    sum_d2 = sum_down(ring, *pd2)
    pgu2 = gate_up_bwd(me, xf2, dg2, du2)
    sum_g2, sum_u2 = sum_gate_up(ring, *pgu2)
    gm2, bo2, gg_m2 = mlp_dx(dg2, du2, v_g, v_u, hm2, gain_m2, cot)
    dor2 = attn_dout(bo2, v_o, bf16)
    dq2, dk2, dv2 = window_bwd(q2, k2, v2, dor2, seg_row, seg_col, live_col)
    *pa2, gh1, gg_a2 = attn_bwd(me, xa2, [dq2, dk2, dv2], [v_q, v_k, v_v], o2, bo2, h1, gain_a2, gm2, HALVES_TWO)
    sum_q2, sum_k2, sum_v2, sum_o2 = sum_attn(ring, *pa2, HALVES_TWO, [256] * 4)
    dg1, du1, *pd1 = down_bwd(me, gh1.astype(bf16), w_d, hid1, g1, u1)
    sum_d1 = sum_down(ring, *pd1)
    pgu1 = gate_up_bwd(me, xf1, dg1, du1)
    sum_g1, sum_u1 = sum_gate_up(ring, *pgu1)
    gm1, bo1, gg_m1 = mlp_dx(dg1, du1, w_g, w_u, hm1, gain_m1, gh1)
    dou1 = attn_dout(bo1, w_o, f32)
    dqk1, dv1 = based_bwd(qk1, v1, dou1, ou1, rden1, seg_row, seg_col, live_col)
    *pa1, g0, gg_a1 = attn_bwd(me, xa1, [dqk1, dv1], [w_qk, w_v], o1, bo1, start, gain_a1, gm1, HALVES_ONE)
    sums = sum_attn(ring, *pa1, HALVES_ONE, [128, 256, 256])
    if ring:
        sum_q1, sum_k1 = sums[0][:, :64], sums[0][:, 64:]
    else:
        wide = sums[0].shape[1] // 2
        sum_q1, sum_k1 = sums[0][:, :wide], sums[0][:, wide:]
    sum_v1, sum_o1 = sums[1:]

    gains = lax.psum(jnp.concatenate([gg_a1, gg_m1, gg_a2, gg_m2], axis=0), ("row", "col"))
    restore = jnp.argsort(send_order)
    output = exchange(h2.astype(bf16)[local_slots], n_rows)[restore]
    tokens_grad = exchange(g0.astype(bf16)[local_slots], n_rows)[restore]
    return (
        output, tokens_grad,
        gains[0], sum_q1, sum_k1, sum_v1, sum_o1, gains[1], sum_g1, sum_u1, sum_d1,
        gains[2], sum_q2, sum_k2, sum_v2, sum_o2, gains[3], sum_g2, sum_u2, sum_d2,
    )


def solution(mesh):
    block, weight = P(("row", "col"), None), P("row", "col")
    layer_in = (P(),) + (weight,) * 4 + (P(),) + (weight,) * 3
    return jax.shard_map(
        body,
        mesh=mesh,
        in_specs=(block, block, P(), block, P(("row", "col"))) + layer_in * 2,
        out_specs=(block, block) + layer_in * 2,
        check_vma=False,
    )
```

```python
import functools

import jax
import jax.numpy as jnp
from jax import lax
from jax.experimental import pallas as pl
from jax.experimental.pallas import tpu as pltpu
from jax.sharding import Mesh, PartitionSpec as P

HEADS = 16
FEAT = 16
HEAD_DIM = 64
WINDOW = 64
MAX_LEN = 256
D = 1024
T = 512
HALF = 256
EPS = 1e-05
NEG = -1e30
ROWS = 8
COLS = 4
FB = 344
FBP = 352
FFP = ROWS * FBP
FC = FFP // COLS

bf16, f32, i32 = jnp.bfloat16, jnp.float32, jnp.int32
NN, NT, TN = ((1,), (0,)), ((1,), (1,)), ((0,), (0,))


def dot(a, b, dims):
    return lax.dot_general(a, b, (dims, ((), ())), preferred_element_type=f32)


def call(body, grid, ins, outs, scratch=(), flops=0, prefetch=None):
    extra = 0 if prefetch is None else 1

    def spec(block, index):
        if block is None:
            return pl.BlockSpec(memory_space=pl.ANY)
        return pl.BlockSpec(block, index)

    in_specs, args = [], []
    for item in ins:
        if not isinstance(item, tuple):
            nd = item.ndim
            item = (item, item.shape, functools.partial(lambda n, *_: (0,) * n, nd))
        args.append(item[0])
        in_specs.append(spec(item[1], item[2]))
    out_specs = [spec(o[2], o[3]) for o in outs]
    out_shape = [jax.ShapeDtypeStruct(o[0], o[1]) for o in outs]
    moved = sum(a.size * a.dtype.itemsize for a in args)
    moved += sum(s.size * s.dtype.itemsize for s in out_shape)
    cost = pl.CostEstimate(flops=int(flops), bytes_accessed=int(moved), transcendentals=0)
    got = pl.pallas_call(
        body,
        out_shape=out_shape,
        grid_spec=pltpu.PrefetchScalarGridSpec(
            num_scalar_prefetch=extra,
            grid=grid,
            in_specs=in_specs,
            out_specs=out_specs,
            scratch_shapes=list(scratch),
        ),
        compiler_params=pltpu.CompilerParams(vmem_limit_bytes=56 * 2**20),
        cost_estimate=cost,
    )(*(([prefetch] if extra else []) + args))
    return got


def whole_map(*shape):
    zeros = (0,) * len(shape)
    return lambda *_: zeros


def norm_factor(h):
    return lax.rsqrt(jnp.mean(h * h, axis=-1, keepdims=True) + EPS)


class Strips:
    def __init__(self, half, swapped, at, n):
        self.bufs, self.swapped, self.at, self.n = half, swapped, at, n

    def ins(self):
        return [(b, None, None) for b in self.bufs]

    def scratch(self):
        return [pltpu.VMEM((2, 2, 2, 4, self.n, 128), bf16), pltpu.SemaphoreType.DMA((2, 2, 2))]

    def start(self, refs, box, sems):
        order = [(core, x, y) for core in range(2) for x in range(2) for y in range(2)]
        for core, x, y in order:
            hi, lo = (x, y) if self.swapped else (y, x)
            src = refs[core * 2 + hi].at[lo]
            if self.n != self.bufs[0].shape[2]:
                src = src.at[:, pl.ds(self.at, self.n)]
            pltpu.make_async_copy(src, box.at[core, hi, lo], sems.at[core, hi, lo]).start()

    def wait(self, box, sems, core, x):
        for y in range(2):
            hi, lo = (x, y) if self.swapped else (y, x)
            there = box.at[core, hi, lo]
            pltpu.make_async_copy(there, there, sems.at[core, hi, lo]).wait()

    def wait_all(self, box, sems):
        for core in range(2):
            for x in range(2):
                self.wait(box, sems, core, x)

    def piece(self, box, z, y, x, core):
        return box.at[core, x, y, z] if self.swapped else box.at[core, y, x, z]


BLOCKS = [(z, y) for z in range(4) for y in range(2)]
PLACES = [(x, core) for x in range(2) for core in range(2)]


def step_place(i):
    return i % 2, i // 2


def step_col(i, me):
    return ((i % 2) * 2 + i // 2) ^ me[1]


def regroup(dst_ref, src_ref, count, me):
    width = D // count
    for j in range(count):
        at = pl.multiple_of((j ^ me) * width, 128)
        dst_ref[:, j * width : (j + 1) * width] = src_ref[:, pl.ds(at, width)]


class Kernel:
    def __init__(self, n_in, strips, n_out):
        self.n_in, self.strips, self.n_out = n_in, strips, n_out

    def split(self, refs):
        n, m = self.n_in, len(self.strips)
        ins, refs = refs[:n], refs[n:]
        srcs, refs = refs[: 4 * m], refs[4 * m :]
        outs, refs = refs[: self.n_out], refs[self.n_out :]
        boxes, rest = refs[: 2 * m], refs[2 * m :]
        hold = [(s, srcs[4 * j : 4 * j + 4], boxes[2 * j], boxes[2 * j + 1]) for j, s in enumerate(self.strips)]
        return ins, hold, outs, rest

    def ins(self):
        return [i for s in self.strips for i in s.ins()]

    def scratch(self):
        return [i for s in self.strips for i in s.scratch()]


def start_all(hold):
    for s, srcs, box, sems in hold:
        s.start(srcs, box, sems)


def col_block(s, box, x, core):
    strips = []
    for j in range(s.n // 128):
        strips.append(jnp.concatenate([s.piece(box, z, y, x, core)[j * 128 : (j + 1) * 128, :] for z, y in BLOCKS], axis=0))
    return strips[0] if len(strips) == 1 else jnp.concatenate(strips, axis=1)


def norm_proj(me, h, gain, strips):
    n = len(strips)
    kern = Kernel(2, strips, n + 1)

    def body(me_ref, *refs):
        (h_ref, gain_ref), hold, (xa_ref, *outs), (xr_ref,) = kern.split(refs)
        i = pl.program_id(0)

        @pl.when(i == 0)
        def _():
            start_all(hold)
            hv = h_ref[...].astype(f32)
            xa_ref[...] = (hv * norm_factor(hv) * gain_ref[...]).astype(bf16)
            regroup(xr_ref, xa_ref, ROWS, me_ref[0])

        x, core = step_place(i)
        for (s, _, box, sems), o_ref in zip(hold, outs):
            s.wait(box, sems, core, x)
            o_ref[...] = dot(xr_ref[...], col_block(s, box, x, core), NN).astype(bf16)

    outs = [((T, D), bf16, (T, D), whole_map(T, D))]
    for s in strips:
        outs.append(((T, s.n * COLS), bf16, (T, s.n), lambda i, me: (0, step_col(i, me))))
    total = sum(s.n * COLS for s in strips)
    return call(
        body, (COLS,), [h, gain.reshape(1, D)] + kern.ins(), outs,
        scratch=kern.scratch() + [pltpu.VMEM((T, D), bf16)], flops=2 * T * D * total, prefetch=me,
    )


def lanes(shape, width):
    return lax.broadcasted_iota(i32, shape, len(shape) - 1) // width


def fill_mask(mask_ref, seg_q, seg_k, live_k, q_axis, window):
    q = lax.broadcasted_iota(i32, (T, T), q_axis)
    k = lax.broadcasted_iota(i32, (T, T), 1 - q_axis)
    ok = (k <= q) & (k > q - window) & (seg_q == seg_k) & ((live_k > 0) | (k == q))
    mask_ref[...] = jnp.where(ok, 1.0, 0.0)


def based_fwd(qk, v, seg_row, seg_col, live_row):
    def body(qk_ref, v_ref, sr_ref, sc_ref, lr_ref, o_ref, ou_ref, rden_ref, mask_ref):
        @pl.when(pl.program_id(0) == 0)
        def _():
            fill_mask(mask_ref, sc_ref[...], sr_ref[...], lr_ref[...], 0, MAX_LEN)

        q4, k4 = qk_ref[:, 0:64], qk_ref[:, 64:128]
        qlane = lanes((T, 64), FEAT)
        first = lanes((HALF, 128), HEAD_DIM) == 0
        scaled = q4.astype(f32) * (FEAT**-0.5)
        for pair in range(2):
            v2 = v_ref[:, pair * 128 : pair * 128 + 128]
            for tb in range(2):
                t0, s1 = tb * HALF, (tb + 1) * HALF
                got = []
                for e in range(2):
                    qm = jnp.where(qlane == pair * 2 + e, scaled, 0.0).astype(bf16)
                    a = dot(qm[t0 : t0 + HALF], k4[0:s1], NT)
                    p = (1.0 + a * (1.0 + 0.5 * a)) * mask_ref[t0 : t0 + HALF, 0:s1]
                    den = jnp.sum(p, axis=-1, keepdims=True)
                    got.append((dot(p.astype(bf16), v2[0:s1], NN), den))
                rden = 1.0 / jnp.where(first, got[0][1], got[1][1])
                ou = jnp.where(first, got[0][0], got[1][0]) * rden
                at = (slice(t0, t0 + HALF), slice(pair * 128, pair * 128 + 128))
                ou_ref[at] = ou
                rden_ref[at] = rden
                o_ref[at] = ou.astype(bf16)

    wide = (T, 256)
    col = lambda c: (0, c)
    return call(
        body,
        (4,),
        [(qk, (T, 128), col), (v, wide, col), seg_row, seg_col, live_row],
        [((T, D), bf16, wide, col), ((T, D), f32, wide, col), ((T, D), f32, wide, col)],
        scratch=[pltpu.VMEM((T, T), f32)],
        flops=HEADS * T * T * 2 * 192,
    )


def based_bwd(qk, v, dou, ou, rden, seg_row, seg_col, live_col):
    def body(qk_ref, v_ref, dou_ref, ou_ref, rden_ref, sr_ref, sc_ref, lc_ref, dqk_ref, dv_ref, mask_ref, dk_ref, dva_ref):
        @pl.when(pl.program_id(0) == 0)
        def _():
            fill_mask(mask_ref, sr_ref[...], sc_ref[...], lc_ref[...], 1, MAX_LEN)

        q4, k4 = qk_ref[:, 0:64], qk_ref[:, 64:128]
        qlane = lanes((T, 64), FEAT)
        q_scaled = q4.astype(f32) * (FEAT**-0.5)
        k_scaled = k4.astype(f32) * (FEAT**-0.5)
        vlane = lanes((T, 128), HEAD_DIM)
        dnum_f = dou_ref[...] * rden_ref[...]
        term = dnum_f * ou_ref[...]
        high = term.astype(bf16)
        low = (term - high.astype(f32)).astype(bf16)
        pick = jnp.where(
            lax.broadcasted_iota(i32, (8, 256), 0) == lanes((8, 256), HEAD_DIM), 1.0, 0.0
        ).astype(bf16)
        dden = -(dot(pick, high, NT) + dot(pick, low, NT))
        dk_ref[...] = jnp.zeros((T, 64), f32)
        dva_ref[...] = jnp.zeros((T, 256), f32)
        dq = [jnp.zeros((HALF, 64), f32), jnp.zeros((HALF, 64), f32)]
        for pair in range(2):
            cols = slice(pair * 128, pair * 128 + 128)
            v2 = v_ref[:, cols]
            for e in range(2):
                head = pair * 2 + e
                qm = jnp.where(qlane == head, q_scaled, 0.0).astype(bf16)
                km = jnp.where(qlane == head, k_scaled, 0.0).astype(bf16)
                dn = jnp.where(vlane == e, dnum_f[:, cols], 0.0).astype(bf16)
                for tb in range(2):
                    t0, s1 = tb * HALF, (tb + 1) * HALF
                    at = slice(t0, t0 + HALF)
                    a = dot(k4[0:s1], qm[at], NT)
                    m = mask_ref[0:s1, at]
                    p = (1.0 + a * (1.0 + 0.5 * a)) * m
                    dp = dot(v2[0:s1], dn[at], NT) + dden[head : head + 1, at]
                    da = (dp * m * (1.0 + a)).astype(bf16)
                    dk_ref[0:s1, :] += dot(da, qm[at], NN)
                    dva_ref[0:s1, cols] += dot(p.astype(bf16), dn[at], NN)
                    dq[tb] += dot(da, km[0:s1], TN)
        for tb in range(2):
            at = slice(tb * HALF, tb * HALF + HALF)
            dqk_ref[at, 0:64] = dq[tb].astype(bf16)
        dqk_ref[:, 64:128] = dk_ref[...].astype(bf16)
        dv_ref[...] = dva_ref[...].astype(bf16)

    wide = (T, 256)
    col = lambda c: (0, c)
    return call(
        body,
        (4,),
        [(qk, (T, 128), col), (v, wide, col), (dou, wide, col), (ou, wide, col), (rden, wide, col), seg_row, seg_col, live_col],
        [((T, 512), bf16, (T, 128), col), ((T, D), bf16, wide, col)],
        scratch=[pltpu.VMEM((T, T), f32), pltpu.VMEM((T, 64), f32), pltpu.VMEM((T, 256), f32)],
        flops=HEADS * T * T * 2 * 480,
    )


SPAN = ((0, HALF), (HALF - WINDOW, T))


def window_fwd(q, k, v, seg_row, seg_col, live_row):
    def body(q_ref, k_ref, v_ref, sr_ref, sc_ref, lr_ref, o_ref, mask_ref):
        @pl.when(pl.program_id(0) == 0)
        def _():
            fill_mask(mask_ref, sc_ref[...], sr_ref[...], lr_ref[...], 0, WINDOW)

        first = lanes((HALF, 128), HEAD_DIM) == 0
        qlane = lanes((T, 128), HEAD_DIM)
        scaled = q_ref[...].astype(f32) * (HEAD_DIM**-0.5)
        for tb in range(2):
            t0 = tb * HALF
            s0, s1 = SPAN[tb]
            ok = mask_ref[t0 : t0 + HALF, s0:s1] > 0.5
            got = []
            for e in range(2):
                qm = jnp.where(qlane == e, scaled, 0.0).astype(bf16)
                c = dot(qm[t0 : t0 + HALF], k_ref[s0:s1, :], NT)
                c = jnp.where(ok, c, NEG)
                w = jnp.exp(c - jnp.max(c, axis=-1, keepdims=True))
                w = w * (1.0 / jnp.sum(w, axis=-1, keepdims=True))
                got.append(dot(w.astype(bf16), v_ref[s0:s1, :], NN))
            o_ref[t0 : t0 + HALF, :] = jnp.where(first, got[0], got[1]).astype(bf16)

    blk = (T, 128)
    col = lambda c: (0, c)
    return call(
        body,
        (8,),
        [(q, blk, col), (k, blk, col), (v, blk, col), seg_row, seg_col, live_row],
        [((T, D), bf16, blk, col)],
        scratch=[pltpu.VMEM((T, T), f32)],
        flops=HEADS * T * T * 2 * 192,
    )[0]


def window_bwd(q, k, v, dor, seg_row, seg_col, live_col):
    def body(q_ref, k_ref, v_ref, do_ref, sr_ref, sc_ref, lc_ref, dq_ref, dk_ref, dv_ref, mask_ref, dka_ref, dva_ref):
        @pl.when(pl.program_id(0) == 0)
        def _():
            fill_mask(mask_ref, sr_ref[...], sc_ref[...], lc_ref[...], 1, WINDOW)

        lane = lanes((T, 128), HEAD_DIM)
        q_scaled = q_ref[...].astype(f32) * (HEAD_DIM**-0.5)
        k_scaled = k_ref[...].astype(f32) * (HEAD_DIM**-0.5)
        do = do_ref[...]
        dka_ref[...] = jnp.zeros((T, 128), f32)
        dva_ref[...] = jnp.zeros((T, 128), f32)
        for tb in range(2):
            at = slice(tb * HALF, tb * HALF + HALF)
            s0, s1 = SPAN[tb]
            ok = mask_ref[s0:s1, at] > 0.5
            dq = jnp.zeros((HALF, 128), f32)
            for e in range(2):
                qm = jnp.where(lane == e, q_scaled, 0.0).astype(bf16)
                km = jnp.where(lane == e, k_scaled, 0.0).astype(bf16)
                dm = jnp.where(lane == e, do, jnp.zeros_like(do))
                c = dot(k_ref[s0:s1, :], qm[at], NT)
                c = jnp.where(ok, c, NEG)
                w = jnp.exp(c - jnp.max(c, axis=0, keepdims=True))
                w = w * (1.0 / jnp.sum(w, axis=0, keepdims=True))
                dw = dot(v_ref[s0:s1, :], dm[at], NT)
                ds = (w * (dw - jnp.sum(w * dw, axis=0, keepdims=True))).astype(bf16)
                dka_ref[s0:s1, :] += dot(ds, qm[at], NN)
                dva_ref[s0:s1, :] += dot(w.astype(bf16), dm[at], NN)
                dq += dot(ds, km[s0:s1], TN)
            dq_ref[at, :] = dq.astype(bf16)
        dk_ref[...] = dka_ref[...].astype(bf16)
        dv_ref[...] = dva_ref[...].astype(bf16)

    blk = (T, 128)
    col = lambda c: (0, c)
    return call(
        body,
        (8,),
        [(q, blk, col), (k, blk, col), (v, blk, col), (dor, blk, col), seg_row, seg_col, live_col],
        [((T, D), bf16, blk, col)] * 3,
        scratch=[pltpu.VMEM((T, T), f32), pltpu.VMEM((T, 128), f32), pltpu.VMEM((T, 128), f32)],
        flops=HEADS * T * T * 2 * 480,
    )


def attn_out(me, h, o, strip, gain):
    kern = Kernel(3, [strip], 2)

    def body(me_ref, *refs):
        (h_ref, o_ref, gain_ref), hold, (hm_ref, xf_ref), (or_ref,) = kern.split(refs)
        i = pl.program_id(0)

        @pl.when(i == 0)
        def _():
            start_all(hold)
            regroup(or_ref, o_ref, ROWS, me_ref[0])

        x, core = step_place(i)
        s, _, box, sems = hold[0]
        s.wait(box, sems, core, x)
        at = pl.ds(pl.multiple_of(step_col(i, me_ref) * 256, 256), 256)
        hm_ref[:, at] = h_ref[:, at].astype(f32) + dot(or_ref[...], col_block(s, box, x, core), NN)

        @pl.when(i == COLS - 1)
        def _():
            hm = hm_ref[...]
            xf_ref[...] = (hm * norm_factor(hm) * gain_ref[...]).astype(bf16)

    full = whole_map(T, D)
    return call(
        body, (COLS,), [h, o, gain.reshape(1, D)] + kern.ins(),
        [((T, D), f32, (T, D), full), ((T, D), bf16, (T, D), full)],
        scratch=kern.scratch() + [pltpu.VMEM((T, D), bf16)], flops=2 * T * D * D, prefetch=me,
    )


def hidden_block(s, box, x, core):
    return jnp.concatenate([s.piece(box, z, y, x, core)[...] for z, y in BLOCKS], axis=1)


def gate_up(me, xf, w_gate, w_up):
    kern = Kernel(1, [w_gate, w_up], 3)

    def body(me_ref, *refs):
        (xf_ref,), hold, (g_ref, u_ref, hid_ref), (xr_ref,) = kern.split(refs)
        i = pl.program_id(0)

        @pl.when(i == 0)
        def _():
            start_all(hold)
            regroup(xr_ref, xf_ref, ROWS, me_ref[0])

        x, core = step_place(i)
        got = []
        for s, _, box, sems in hold:
            s.wait(box, sems, core, x)
            got.append(dot(hidden_block(s, box, x, core), xr_ref[...], NT))
        g, u = got
        g_ref[...] = g.astype(bf16)
        u_ref[...] = u.astype(bf16)
        hid_ref[...] = (g * (1.0 / (1.0 + jnp.exp(-g))) * u).astype(bf16)

    row = lambda i, me: (step_col(i, me), 0)
    return call(
        body, (COLS,), [xf] + kern.ins(), [((FFP, T), bf16, (FC, T), row)] * 3,
        scratch=kern.scratch() + [pltpu.VMEM((T, D), bf16)], flops=4 * T * D * FFP, prefetch=me,
    )


def down_rows(me_ref, hold, z):
    (s1, _, box1, _), (s2, _, box2, _) = hold
    halves = []
    for y in range(2):
        yr = y ^ me_ref[0]
        parts = []
        for x, core in PLACES:
            parts += [s1.piece(box1, z, yr, x, core)[...], s2.piece(box2, z, yr, x, core)[...]]
        halves.append(jnp.concatenate(parts, axis=1))
    return jnp.concatenate(halves, axis=0)


def down(me, hm, hid, strips):
    kern = Kernel(2, strips, 1)

    def body(me_ref, *refs):
        (hm_ref, hid_ref), hold, (h_ref,), (acc_ref,) = kern.split(refs)
        i = pl.program_id(0)

        @pl.when(i == 0)
        def _():
            start_all(hold)
            regroup(acc_ref, hm_ref, COLS, me_ref[1])
            for s, _, box, sems in hold:
                s.wait_all(box, sems)

        acc_ref[...] += dot(hid_ref[...], down_rows(me_ref, hold, i), TN)

        @pl.when(i == COLS - 1)
        def _():
            regroup(h_ref, acc_ref, COLS, me_ref[1])

    return call(
        body, (COLS,), [hm, (hid, (FC, T), lambda i, me: (i, 0))] + kern.ins(),
        [((T, D), f32, (T, D), whole_map(T, D))],
        scratch=kern.scratch() + [pltpu.VMEM((T, D), f32)], flops=2 * T * D * FFP, prefetch=me,
    )[0]


def down_bwd(me, bd, strips, hid, g, u):
    kern = Kernel(4, strips, 4)

    def body(me_ref, *refs):
        (bd_ref, hid_ref, g_ref, u_ref), hold, (dg_ref, du_ref, p1_ref, p2_ref), (br_ref,) = kern.split(refs)
        i = pl.program_id(0)

        @pl.when(i == 0)
        def _():
            start_all(hold)
            regroup(br_ref, bd_ref, COLS, me_ref[1])

        bdv = br_ref[...].astype(bf16)
        gwd = dot(hid_ref[...], bdv, NN).astype(bf16)
        for x, core in PLACES:
            at = (x * 2 + core) * 256
            for y in range(2):
                yr = y ^ me_ref[0]
                rows = slice(y * FBP, (y + 1) * FBP)
                p1_ref[core, x, yr, 0] = gwd[rows, at : at + 128]
                p2_ref[core, yr, x, 0] = gwd[rows, at + 128 : at + 256]

        @pl.when(i == 0)
        def _():
            for s, _, box, sems in hold:
                s.wait_all(box, sems)

        dhid = dot(down_rows(me_ref, hold, i), bdv, NT)
        gv, uv = g_ref[...].astype(f32), u_ref[...].astype(f32)
        sig = 1.0 / (1.0 + jnp.exp(-gv))
        act = gv * sig
        du_ref[...] = (dhid * act).astype(bf16)
        dg_ref[...] = (dhid * uv * (sig + act * (1.0 - sig))).astype(bf16)

    row = lambda i, me: (i, 0)
    hblk = (FC, T)
    pieces = ((2, 2, 2, 4, FBP, 128), bf16, (2, 2, 2, 1, FBP, 128), lambda i, me: (0, 0, 0, i, 0, 0))
    return call(
        body, (COLS,), [bd, (hid, hblk, row), (g, hblk, row), (u, hblk, row)] + kern.ins(),
        [((FFP, T), bf16, hblk, row), ((FFP, T), bf16, hblk, row), pieces, pieces],
        scratch=kern.scratch() + [pltpu.VMEM((T, D), bd.dtype)], flops=4 * T * D * FFP, prefetch=me,
    )


def piece_specs(n1, n2):
    one = ((2, 2, 2, 4, n1, 128), bf16, (1, 1, 2, 4, n1, 128), lambda i, me: (i // 2, i % 2, 0, 0, 0, 0))
    two = ((2, 2, 2, 4, n2, 128), bf16, (1, 2, 1, 4, n2, 128), lambda i, me: (i // 2, 0, i % 2, 0, 0, 0))
    return [one, two]


def gate_up_bwd(me, xf, dg, du):
    def body(me_ref, xf_ref, dg_ref, du_ref, p1_ref, p2_ref, xr_ref):
        @pl.when(pl.program_id(0) == 0)
        def _():
            regroup(xr_ref, xf_ref, ROWS, me_ref[0])

        gwg = dot(dg_ref[...], xr_ref[...], NN).astype(bf16)
        gwu = dot(du_ref[...], xr_ref[...], NN).astype(bf16)
        for r, (z, y) in enumerate(BLOCKS):
            p1_ref[0, 0, y, z] = gwg[:, r * 128 : (r + 1) * 128]
            p2_ref[0, y, 0, z] = gwu[:, r * 128 : (r + 1) * 128]

    row = lambda i, me: (step_col(i, me), 0)
    return call(
        body, (COLS,), [xf, (dg, (FC, T), row), (du, (FC, T), row)], piece_specs(FC, FC),
        scratch=[pltpu.VMEM((T, D), bf16)], flops=4 * T * D * FFP, prefetch=me,
    )


def norm_bwd(dx, h, gain, g):
    rf = norm_factor(h)
    hr = h * rf
    dgain = jnp.sum(dx * hr, axis=0, keepdims=True)
    gd = gain * dx
    mean = jnp.sum(gd * hr, axis=-1, keepdims=True) * (1.0 / D)
    return dgain, g + rf * (gd - hr * mean)


def add_to(acc_ref, part):
    @pl.when(pl.program_id(0) == 0)
    def _():
        acc_ref[...] = part

    @pl.when(pl.program_id(0) > 0)
    def _():
        acc_ref[...] += part


def mlp_dx(me, dg, du, w_gate, w_up, hm, gain, g, w_out, kind):
    kern = Kernel(5, [w_gate, w_up, w_out], 4)

    def body(me_ref, *refs):
        (dg_ref, du_ref, hm_ref, gain_ref, g_ref), hold, outs, (acc_ref, un_ref, br_ref) = kern.split(refs)
        gm_ref, bo_ref, dou_ref, gg_ref = outs
        i = pl.program_id(0)

        @pl.when(i == 0)
        def _():
            start_all(hold)

        x, core = step_place(i)
        part = None
        for (s, _, box, sems), d_ref in zip(hold[:2], (dg_ref, du_ref)):
            s.wait(box, sems, core, x)
            term = dot(d_ref[...], hidden_block(s, box, x, core), TN)
            part = term if part is None else part + term
        add_to(acc_ref, part)

        @pl.when(i == COLS - 1)
        def _():
            regroup(un_ref, acc_ref, ROWS, me_ref[0])
            gg, gm = norm_bwd(un_ref[...], hm_ref[...], gain_ref[...], g_ref[...].astype(f32))
            gg_ref[...] = gg
            gm_ref[...] = gm
            bo_ref[...] = gm.astype(bf16)
            regroup(br_ref, bo_ref, COLS, me_ref[1])
            s, _, box, sems = hold[2]
            s.wait_all(box, sems)
            w = jnp.concatenate([col_block(s, box, x, core) for x, core in PLACES], axis=1)
            acc_ref[...] = dot(br_ref[...], w, NT)
            regroup(un_ref, acc_ref, ROWS, me_ref[0])
            dou_ref[...] = un_ref[...].astype(kind)

    row = lambda i, me: (step_col(i, me), 0)
    full = whole_map(T, D)
    return call(
        body, (COLS,), [(dg, (FC, T), row), (du, (FC, T), row), hm, gain.reshape(1, D), g] + kern.ins(),
        [((T, D), f32, (T, D), full), ((T, D), bf16, (T, D), full), ((T, D), kind, (T, D), full), ((1, D), f32, (1, D), full)],
        scratch=kern.scratch() + [pltpu.VMEM((T, D), f32), pltpu.VMEM((T, D), f32), pltpu.VMEM((T, D), bf16)],
        flops=4 * T * D * FFP + 2 * T * D * D, prefetch=me,
    )


def attn_bwd(me, xa, grads, strips, o, bo, h, gain, gm, halves):
    n = len(grads)
    kern = Kernel(6 + n, strips, 4)

    def body(me_ref, *refs):
        ins, hold, (p1_ref, p2_ref, g_ref, gg_ref), (xr_ref, or_ref, acc_ref) = kern.split(refs)
        xa_ref, o_ref, h_ref, gain_ref, gm_ref, bo_ref, *d_refs = ins
        i = pl.program_id(0)

        @pl.when(i == 0)
        def _():
            start_all(hold)
            regroup(xr_ref, xa_ref, ROWS, me_ref[0])
            regroup(or_ref, o_ref, ROWS, me_ref[0])

        tiles = [dot(xr_ref[...], d[...], TN).astype(bf16) for d in d_refs]
        tiles.append(dot(or_ref[...], bo_ref[...], TN).astype(bf16))
        for j, (which, at) in enumerate(halves[0]):
            for r, (z, y) in enumerate(BLOCKS):
                p1_ref[0, 0, y, z, j * 128 : (j + 1) * 128] = tiles[which][r * 128 : (r + 1) * 128, at : at + 128]
        for j, (which, at) in enumerate(halves[1]):
            for r, (z, y) in enumerate(BLOCKS):
                p2_ref[0, y, 0, z, j * 128 : (j + 1) * 128] = tiles[which][r * 128 : (r + 1) * 128, at : at + 128]
        x, core = step_place(i)
        part = None
        for (s, _, box, sems), d in zip(hold, d_refs):
            s.wait(box, sems, core, x)
            term = dot(d[...], col_block(s, box, x, core), NT)
            part = term if part is None else part + term
        add_to(acc_ref, part)

        @pl.when(i == COLS - 1)
        def _():
            regroup(g_ref, acc_ref, ROWS, me_ref[0])
            gg, g = norm_bwd(g_ref[...], h_ref[...].astype(f32), gain_ref[...], gm_ref[...])
            gg_ref[...] = gg
            g_ref[...] = g

    col = lambda i, me: (0, step_col(i, me))
    full = whole_map(T, D)
    ins = [xa, o, h, gain.reshape(1, D), gm, (bo, (T, 256), col)]
    ins += [(d, (T, d.shape[1] // COLS), col) for d in grads]
    total = sum(d.shape[1] for d in grads)
    return call(
        body, (COLS,), ins + kern.ins(),
        piece_specs(128 * len(halves[0]), 128 * len(halves[1])) + [((T, D), f32, (T, D), full), ((1, D), f32, (1, D), full)],
        scratch=kern.scratch() + [pltpu.VMEM((T, D), bf16), pltpu.VMEM((T, D), bf16), pltpu.VMEM((T, D), f32)],
        flops=4 * T * D * total + 2 * T * D * D, prefetch=me,
    )


HALVES_ONE = (((1, 0), (1, 128)), ((0, 0), (2, 0), (2, 128)))
HALVES_TWO = (((0, 0), (0, 128), (1, 0), (1, 128)), ((2, 0), (2, 128), (3, 0), (3, 128)))


def weights_of(attn, gu, dn, halves):
    out = []
    for which in range(1 + max(w for half in halves for w, _ in half)):
        for k, half in enumerate(halves):
            at = [j for j, (w, _) in enumerate(half) if w == which]
            if at:
                out.append(Strips(attn[k], k == 1, at[0] * 128, len(at) * 128))
    return out, Strips(gu[0], False, 0, FC), Strips(gu[1], True, 0, FC), [Strips(dn[0], False, 0, FBP), Strips(dn[1], True, 0, FBP)]


def pad_hidden(w):
    k = w.shape[0]
    return jnp.pad(w.reshape(k, -1, FB), ((0, 0), (0, 0), (0, FBP - FB))).reshape(k, -1).T


def pad_rows(w):
    n = w.shape[1]
    return jnp.pad(w.reshape(-1, FB, n), ((0, 0), (0, FBP - FB), (0, 0))).reshape(-1, n)


def strips_of(blocks, halves):
    return tuple(
        jnp.concatenate([blocks[which][..., at : at + 128] for which, at in strips], axis=-2) for strips in halves
    )


def tie(value, *after):
    got = lax.optimization_barrier((value, *after))
    return got[0], got[1:]


class Ring:
    def __init__(self, names):
        self.axes = names
        self.z = lax.axis_index(names[0])

    def swap(self, value, axis, by=1):
        shift = {"z": 3, "y": 2, "x": 1, "core": 0}[axis]
        return lax.ppermute(value, self.axes, [(i, i ^ (by << shift)) for i in range(32)])

    def gather_z(self, both):
        near = [both] + [self.swap(both, "z", by) for by in (1, 2, 3)]
        low, high = self.z % 2 == 1, self.z >= 2
        a, b = jnp.where(low, near[1], near[0]), jnp.where(low, near[0], near[1])
        c, d = jnp.where(low, near[3], near[2]), jnp.where(low, near[2], near[3])
        pick = lambda p, q: jnp.where(high, q, p)
        return jnp.stack([pick(a, c), pick(b, d), pick(c, a), pick(d, b)])

    def gather_z_all(self, both):
        return lax.all_gather(both, self.axes[0], axis=0, tiled=False)

    def gather_lo(self, one, two):
        return [jnp.stack([one, self.swap(one, "x")]), jnp.stack([two, self.swap(two, "y")])]

    def gather_hi(self, pair):
        return [[pair[0], self.swap(pair[0], "y")], [pair[1], self.swap(pair[1], "x")]]

    def gather_core(self, full):
        return [half + [self.swap(b, "core") for b in half] for half in full]

    def reduce_core(self, pair):
        return [g[0] + self.swap(g[1], "core") for g in pair]

    def reduce_lo(self, pair):
        return [pair[0][0] + self.swap(pair[0][1], "x"), pair[1][0] + self.swap(pair[1][1], "y")]

    def reduce_hi(self, pair):
        return [pair[0][0] + self.swap(pair[0][1], "y"), pair[1][0] + self.swap(pair[1][1], "x")]

    def reduce_z(self, pair):
        n1 = pair[0].shape[1]
        both = jnp.concatenate(pair, axis=1)
        here = lambda by: lax.dynamic_index_in_dim(both, self.z ^ by, 0, False)
        total = here(0).astype(f32)
        for by in (1, 2, 3):
            total = total + self.swap(here(by), "z", by).astype(f32)
        return total[:n1], total[n1:]

    def reduce_z_all(self, pair):
        n1 = pair[0].shape[1]
        both = jnp.concatenate(pair, axis=1)
        total = lax.psum_scatter(both, self.axes[0], scatter_dimension=0, tiled=False).astype(f32)
        return total[:n1], total[n1:]


def pack(shards, halves):
    *attn, gate, up, dn = shards
    dp = pad_rows(dn)
    return [strips_of(attn, halves), (pad_hidden(gate), pad_hidden(up)), (dp[:, :128], dp[:, 128:])]


def boxes_any(weights, halves):
    *attn, gate, up, dn = weights

    def cut(w, rows, cols):
        return w.reshape(4, 2, rows, 2, 2, cols).transpose(0, 1, 3, 4, 2, 5)

    def boxes(one, two):
        first = [one[:, y, :, core].transpose(1, 0, 2, 3) for core in range(2) for y in range(2)]
        second = [two[:, :, x, core].transpose(1, 0, 2, 3) for core in range(2) for x in range(2)]
        return first, second

    a = boxes(*strips_of([cut(w, D // ROWS, w.shape[1] // COLS) for w in attn], halves))
    hidden = lambda w: pad_hidden(w).reshape(2, 2, FC, 4, 2, 128).transpose(3, 4, 0, 1, 2, 5)
    d = cut(pad_rows(dn), FBP, 256)
    return [a, boxes(hidden(gate), hidden(up)), boxes(d[..., :128], d[..., 128:])]


def unpad_hidden(g):
    k = g.shape[1]
    return g.reshape(-1, FBP, k)[:, :FB].reshape(-1, k).T


def unpad_rows(g):
    n = g.shape[1]
    return g.reshape(-1, FBP, n)[:, :FB].reshape(-1, n)


def whole_grad(p, swapped):
    if swapped:
        p = jnp.swapaxes(p, 1, 2)
    core, x, y, z, n, w = p.shape
    return p.transpose(3, 2, 1, 0, 4, 5).reshape(z * y, x * core, n, w)


def join_strips(one, two, halves):
    out = []
    for which in range(1 + max(w for half in halves for w, _ in half)):
        got = {}
        for src, strips in ((one, halves[0]), (two, halves[1])):
            for j, (w, at) in enumerate(strips):
                if w == which:
                    got[at] = src[..., j * 128 : j * 128 + 128, :]
        out.append(jnp.concatenate([got[a] for a in sorted(got)], axis=-1))
    return out


def scatter_any(w):
    part = lax.psum_scatter(w, "row", scatter_dimension=0, tiled=True)
    return lax.psum_scatter(part, "col", scatter_dimension=1, tiled=True).astype(f32)


def natural(blocks):
    r, c, n, w = blocks.shape
    return blocks.transpose(0, 2, 1, 3).reshape(r * n, c * w)


def sum_any(pd, pgu, pa, halves):
    whole = jnp.concatenate([whole_grad(pd[0], False), whole_grad(pd[1], True)], axis=-1)
    dn = scatter_any(unpad_rows(natural(whole)))
    gu = []
    for g, swapped in ((pgu[0], False), (pgu[1], True)):
        gu.append(scatter_any(unpad_hidden(whole_grad(g, swapped).transpose(1, 2, 0, 3).reshape(FFP, D))))
    blocks = join_strips(whole_grad(pa[0], False), whole_grad(pa[1], True), halves)
    if len(blocks) == 3:
        blocks = [blocks[0][..., :64], blocks[0][..., 64:]] + blocks[1:]
    return [scatter_any(natural(b)) for b in blocks] + gu + [dn]


def join_qk(q, k, parts):
    n = q.shape[0]
    both = jnp.concatenate([q.reshape(n, parts, -1), k.reshape(n, parts, -1)], axis=2)
    return both.reshape(n, -1)

def route_plan(dest_slot, block_tokens, rows, cols):
    row_count = lax.axis_size(rows)
    col_count = lax.axis_size(cols)
    per_peer = block_tokens // row_count
    row_at = lax.axis_index(rows)
    col_at = lax.axis_index(cols)
    slot_table = dest_slot.reshape(row_count, col_count, block_tokens)
    column = lax.dynamic_index_in_dim(slot_table, col_at, 1, False)
    own_slots = lax.dynamic_index_in_dim(column, row_at, 0, False)
    send_order = jnp.argsort(own_slots)
    arrived = jnp.sort(column, axis=1)
    incoming = lax.dynamic_slice_in_dim(arrived, row_at * per_peer, per_peer, 1)
    local_slots = incoming.reshape(-1) - (row_at * col_count + col_at) * block_tokens
    placing = jnp.argsort(local_slots)
    return (send_order, local_slots, placing)


def exchange(value, axis):
    n, width = value.shape
    row_count = lax.axis_size(axis)
    got = lax.all_to_all(value.reshape(row_count, n // row_count, width), axis, split_axis=0, concat_axis=0, tiled=True)
    return got.reshape(n, width)


def gather_all(shards):
    return [lax.all_gather(lax.all_gather(w, "col", axis=1, tiled=True), "row", axis=0, tiled=True) for w in shards]


def body(names, tokens, cotangent, dest_slot, lengths, pad_mask, *params):
    ring = Ring(names) if len(names) == 4 else None
    rows, cols = (names[:2], names[2:]) if ring else names
    gain_a1, bq, bk, bv, bo_w, gain_m1, wg1, wu1, wd1 = params[:9]
    gain_a2, wq, wk, wv, wo2, gain_m2, wg2, wu2, wd2 = params[9:]
    shards1, shards2 = [bq, bk, bv, bo_w, wg1, wu1, wd1], [wq, wk, wv, wo2, wg2, wu2, wd2]
    send_order, local_slots, placing = route_plan(dest_slot, T, rows, cols)
    start = exchange(tokens[send_order], rows)[placing]
    cot = exchange(cotangent[send_order], rows)[placing]
    restore = jnp.argsort(send_order)
    if ring:
        me = jnp.stack([lax.axis_index(names[1]), lax.axis_index(cols)]).astype(i32)
        packs = pack([join_qk(bq, bk, 1)] + shards1[2:], HALVES_ONE) + pack(shards2, HALVES_TWO)
        flat = [jnp.concatenate(p, axis=0) for p in packs]
        near = [ring.gather_z(f) for f in flat[:2]]
        rest = ring.gather_z_all(jnp.concatenate(flat[2:], axis=0))
        at = 0
        for f in flat[2:]:
            near.append(rest[:, at : at + f.shape[0]])
            at += f.shape[0]
        full = []
        for p, v in zip(packs, near):
            n1 = p[0].shape[0]
            full.append(ring.gather_core(ring.gather_hi(ring.gather_lo(v[:, :n1], v[:, n1:]))))
    else:
        me = jnp.zeros((2,), i32)
        one, two = gather_all(shards1), gather_all(shards2)
        full = boxes_any([join_qk(one[0], one[1], COLS)] + one[2:], HALVES_ONE) + boxes_any(two, HALVES_TWO)
    (w_qk, w_v, w_o), w_g, w_u, w_d = weights_of(*full[:3], HALVES_ONE)
    (v_q, v_k, v_v, v_o), v_g, v_u, v_d = weights_of(*full[3:], HALVES_TWO)
    position = jnp.arange(T, dtype=i32)
    segment, end = jnp.zeros((T,), i32), jnp.zeros((), i32)
    for j in range(lengths.shape[1]):
        end = end + lengths[0, j]
        segment = segment + (position >= end).astype(i32)
    seg_row, seg_col = segment.reshape(1, T), segment.reshape(T, 1)
    live_row, live_col = pad_mask.reshape(1, T), pad_mask.reshape(T, 1)

    xa1, qk1, v1 = norm_proj(me, start, gain_a1, [w_qk, w_v])
    o1, ou1, rden1 = based_fwd(qk1, v1, seg_row, seg_col, live_row)
    hm1, xf1 = attn_out(me, start, o1, w_o, gain_m1)
    g1, u1, hid1 = gate_up(me, xf1, w_g, w_u)
    h1 = down(me, hm1, hid1, w_d)
    xa2, q2, k2, v2 = norm_proj(me, h1, gain_a2, [v_q, v_k, v_v])
    o2 = window_fwd(q2, k2, v2, seg_row, seg_col, live_row)
    hm2, xf2 = attn_out(me, h1, o2, v_o, gain_m2)
    g2, u2, hid2 = gate_up(me, xf2, v_g, v_u)
    h2 = down(me, hm2, hid2, v_d)
    output = exchange(h2.astype(bf16)[local_slots], rows)[restore]

    tied = tie if ring else (lambda value, *after: (value, after))
    step = (lambda f, v: f(v)) if ring else (lambda f, v: v)
    core, low, high = (ring.reduce_core, ring.reduce_lo, ring.reduce_hi) if ring else (None,) * 3
    dg2, du2, *d2 = down_bwd(me, cot, v_d, hid2, g2, u2)
    gu2 = gate_up_bwd(me, xf2, dg2, du2)
    d2 = step(core, d2)
    dg2, d2 = tied(dg2, *d2)
    gm2, bo2, dor2, gg_m2 = mlp_dx(me, dg2, du2, v_g, v_u, hm2, gain_m2, cot, v_o, bf16)
    d2, gu2 = step(low, d2), step(core, gu2)
    dor2, (*d2, gu2a, gu2b) = tied(dor2, *d2, *gu2)
    dq2, dk2, dv2 = window_bwd(q2, k2, v2, dor2, seg_row, seg_col, live_col)
    d2, gu2 = step(high, d2), step(low, [gu2a, gu2b])
    dq2, d2 = tied(dq2, *d2)
    a2a, a2b, gh1, gg_a2 = attn_bwd(me, xa2, [dq2, dk2, dv2], [v_q, v_k, v_v], o2, bo2, h1, gain_a2, gm2, HALVES_TWO)
    gh1, gu2 = tied(gh1, *gu2)
    dg1, du1, *d1 = down_bwd(me, gh1, w_d, hid1, g1, u1)
    gu2, a2 = step(high, gu2), step(core, [a2a, a2b])
    dg1, a2 = tied(dg1, *a2)
    gu1 = gate_up_bwd(me, xf1, dg1, du1)
    d1 = step(core, d1)
    dg1, (*gu2, d1a, d1b) = tied(dg1, *gu2, *d1)
    gm1, bo1, dou1, gg_m1 = mlp_dx(me, dg1, du1, w_g, w_u, hm1, gain_m1, gh1, w_o, f32)
    a2, gu1 = step(low, a2), step(core, gu1)
    dou1, (*a2, gu1a, gu1b) = tied(dou1, *a2, *gu1)
    dqk1, dv1 = based_bwd(qk1, v1, dou1, ou1, rden1, seg_row, seg_col, live_col)
    d1 = step(low, [d1a, d1b])
    dqk1, d1 = tied(dqk1, *d1)
    a1a, a1b, g0, gg_a1 = attn_bwd(me, xa1, [dqk1, dv1], [w_qk, w_v], o1, bo1, start, gain_a1, gm1, HALVES_ONE)
    gains = jnp.concatenate([gg_a1, gg_m1, gg_a2, gg_m2], axis=0)
    if ring:
        a1 = core([a1a, a1b])
        gu1 = low([gu1a, gu1b])
        d1, a2, gu1, a1 = high(d1), high(a2), high(gu1), high(low(a1))
        sums = []
        for a, gu, d, halves in ((a1, gu1, d1, HALVES_ONE), (a2, gu2, d2, HALVES_TWO)):
            last = halves is HALVES_ONE
            sa = (ring.reduce_z if last else ring.reduce_z_all)(a)
            sgu = (ring.reduce_z if last else ring.reduce_z_all)(gu)
            sd = ring.reduce_z_all(d)
            sums.append(join_strips(*sa, halves) + [unpad_hidden(sgu[0]), unpad_hidden(sgu[1]), unpad_rows(jnp.concatenate(sd, axis=1))])
        sums1, sums2 = sums
        sums1 = [sums1[0][:, :64], sums1[0][:, 64:]] + sums1[1:]
        for axis, by in (("core", 1), ("x", 1), ("y", 1), ("z", 1), ("z", 2)):
            gains = gains + ring.swap(gains, axis, by)
    else:
        sums1 = sum_any(d1, [gu1a, gu1b], [a1a, a1b], HALVES_ONE)
        sums2 = sum_any(d2, gu2, a2, HALVES_TWO)
        gains = lax.psum(gains, ("row", "col"))
    tokens_grad = exchange(g0.astype(bf16)[local_slots], rows)[restore]
    return (
        output, tokens_grad,
        gains[0], *sums1[:4], gains[1], *sums1[4:],
        gains[2], *sums2[:4], gains[3], *sums2[4:],
    )


def solution(mesh):
    names, rows, cols = ("row", "col"), "row", "col"
    if (mesh.shape["row"], mesh.shape["col"]) == (ROWS, COLS):
        names = ("z", "y", "x", "core")
        rows, cols = names[:2], names[2:]
        mesh = Mesh(mesh.devices.reshape(4, 2, 2, 2), names)
    block, weight = P(names, None), P(rows, cols)
    layer_in = (P(),) + (weight,) * 4 + (P(),) + (weight,) * 3
    return jax.shard_map(
        functools.partial(body, names),
        mesh=mesh,
        in_specs=(block, block, P(), block, P(names)) + layer_in * 2,
        out_specs=(block, block) + layer_in * 2,
        check_vma=False,
    )
```

```python
import functools

import jax
import jax.numpy as jnp
from jax import lax
from jax.experimental import pallas as pl
from jax.experimental.pallas import tpu as pltpu
from jax.sharding import Mesh, PartitionSpec as P

HEADS = 16
FEAT = 16
HEAD_DIM = 64
WINDOW = 64
MAX_LEN = 256
D = 1024
T = 512
HALF = 256
EPS = 1e-05
NEG = -1e30
ROWS = 8
COLS = 4
FB = 344
FBP = 352
FFP = ROWS * FBP
FC = FFP // COLS

bf16, f32, i32 = jnp.bfloat16, jnp.float32, jnp.int32
NN, NT, TN = ((1,), (0,)), ((1,), (1,)), ((0,), (0,))


def dot(a, b, dims):
    return lax.dot_general(a, b, (dims, ((), ())), preferred_element_type=f32)


def call(body, grid, ins, outs, scratch=(), flops=0, prefetch=None):
    extra = 0 if prefetch is None else 1

    def spec(block, index):
        if block is None:
            return pl.BlockSpec(memory_space=pl.ANY)
        return pl.BlockSpec(block, index)

    in_specs, args = [], []
    for item in ins:
        if not isinstance(item, tuple):
            nd = item.ndim
            item = (item, item.shape, functools.partial(lambda n, *_: (0,) * n, nd))
        args.append(item[0])
        in_specs.append(spec(item[1], item[2]))
    out_specs = [spec(o[2], o[3]) for o in outs]
    out_shape = [jax.ShapeDtypeStruct(o[0], o[1]) for o in outs]
    moved = sum(a.size * a.dtype.itemsize for a in args)
    moved += sum(s.size * s.dtype.itemsize for s in out_shape)
    cost = pl.CostEstimate(flops=int(flops), bytes_accessed=int(moved), transcendentals=0)
    got = pl.pallas_call(
        body,
        out_shape=out_shape,
        grid_spec=pltpu.PrefetchScalarGridSpec(
            num_scalar_prefetch=extra,
            grid=grid,
            in_specs=in_specs,
            out_specs=out_specs,
            scratch_shapes=list(scratch),
        ),
        compiler_params=pltpu.CompilerParams(vmem_limit_bytes=56 * 2**20),
        cost_estimate=cost,
    )(*(([prefetch] if extra else []) + args))
    return got


def whole_map(*shape):
    zeros = (0,) * len(shape)
    return lambda *_: zeros


def norm_factor(h):
    return lax.rsqrt(jnp.mean(h * h, axis=-1, keepdims=True) + EPS)


class Strips:
    def __init__(self, half, swapped, at, n):
        self.bufs, self.swapped, self.at, self.n = half, swapped, at, n

    def ins(self):
        return [(b, None, None) for b in self.bufs]

    def scratch(self):
        return [pltpu.VMEM((2, 2, 2, 4, self.n, 128), bf16), pltpu.SemaphoreType.DMA((2, 2, 2))]

    def start(self, refs, box, sems):
        order = [(core, x, y) for core in range(2) for x in range(2) for y in range(2)]
        for core, x, y in order:
            hi, lo = (x, y) if self.swapped else (y, x)
            src = refs[core * 2 + hi].at[lo]
            if self.n != self.bufs[0].shape[2]:
                src = src.at[:, pl.ds(self.at, self.n)]
            pltpu.make_async_copy(src, box.at[core, hi, lo], sems.at[core, hi, lo]).start()

    def wait(self, box, sems, core, x):
        for y in range(2):
            hi, lo = (x, y) if self.swapped else (y, x)
            there = box.at[core, hi, lo]
            pltpu.make_async_copy(there, there, sems.at[core, hi, lo]).wait()

    def wait_all(self, box, sems):
        for core in range(2):
            for x in range(2):
                self.wait(box, sems, core, x)

    def piece(self, box, z, y, x, core):
        return box.at[core, x, y, z] if self.swapped else box.at[core, y, x, z]


BLOCKS = [(z, y) for z in range(4) for y in range(2)]
PLACES = [(x, core) for x in range(2) for core in range(2)]


def step_place(i):
    return i % 2, i // 2


def step_col(i, me):
    return ((i % 2) * 2 + i // 2) ^ me[1]


def regroup(dst_ref, src_ref, count, me):
    width = D // count
    for j in range(count):
        at = pl.multiple_of((j ^ me) * width, 128)
        dst_ref[:, j * width : (j + 1) * width] = src_ref[:, pl.ds(at, width)]


class Kernel:
    def __init__(self, n_in, strips, n_out):
        self.n_in, self.strips, self.n_out = n_in, strips, n_out

    def split(self, refs):
        n, m = self.n_in, len(self.strips)
        ins, refs = refs[:n], refs[n:]
        srcs, refs = refs[: 4 * m], refs[4 * m :]
        outs, refs = refs[: self.n_out], refs[self.n_out :]
        boxes, rest = refs[: 2 * m], refs[2 * m :]
        hold = [(s, srcs[4 * j : 4 * j + 4], boxes[2 * j], boxes[2 * j + 1]) for j, s in enumerate(self.strips)]
        return ins, hold, outs, rest

    def ins(self):
        return [i for s in self.strips for i in s.ins()]

    def scratch(self):
        return [i for s in self.strips for i in s.scratch()]


def start_all(hold):
    for s, srcs, box, sems in hold:
        s.start(srcs, box, sems)


def col_block(s, box, x, core):
    strips = []
    for j in range(s.n // 128):
        strips.append(jnp.concatenate([s.piece(box, z, y, x, core)[j * 128 : (j + 1) * 128, :] for z, y in BLOCKS], axis=0))
    return strips[0] if len(strips) == 1 else jnp.concatenate(strips, axis=1)


def norm_proj(me, h, gain, strips):
    n = len(strips)
    kern = Kernel(2, strips, n + 1)

    def body(me_ref, *refs):
        (h_ref, gain_ref), hold, (xa_ref, *outs), (xr_ref,) = kern.split(refs)
        i = pl.program_id(0)

        @pl.when(i == 0)
        def _():
            start_all(hold)
            hv = h_ref[...].astype(f32)
            xa_ref[...] = (hv * norm_factor(hv) * gain_ref[...]).astype(bf16)
            regroup(xr_ref, xa_ref, ROWS, me_ref[0])

        x, core = step_place(i)
        for (s, _, box, sems), o_ref in zip(hold, outs):
            s.wait(box, sems, core, x)
            o_ref[...] = dot(xr_ref[...], col_block(s, box, x, core), NN).astype(bf16)

    outs = [((T, D), bf16, (T, D), whole_map(T, D))]
    for s in strips:
        outs.append(((T, s.n * COLS), bf16, (T, s.n), lambda i, me: (0, step_col(i, me))))
    total = sum(s.n * COLS for s in strips)
    return call(
        body, (COLS,), [h, gain.reshape(1, D)] + kern.ins(), outs,
        scratch=kern.scratch() + [pltpu.VMEM((T, D), bf16)], flops=2 * T * D * total, prefetch=me,
    )


def lanes(shape, width):
    return lax.broadcasted_iota(i32, shape, len(shape) - 1) // width


def fill_mask(mask_ref, seg_q, seg_k, live_k, q_axis, window):
    q = lax.broadcasted_iota(i32, (T, T), q_axis)
    k = lax.broadcasted_iota(i32, (T, T), 1 - q_axis)
    ok = (k <= q) & (k > q - window) & (seg_q == seg_k) & ((live_k > 0) | (k == q))
    mask_ref[...] = jnp.where(ok, 1.0, 0.0)


def based_fwd(qk, v, seg_row, seg_col, live_row):
    def body(qk_ref, v_ref, sr_ref, sc_ref, lr_ref, o_ref, ou_ref, rden_ref, mask_ref):
        @pl.when(pl.program_id(0) == 0)
        def _():
            fill_mask(mask_ref, sc_ref[...], sr_ref[...], lr_ref[...], 0, MAX_LEN)

        q4, k4 = qk_ref[:, 0:64], qk_ref[:, 64:128]
        qlane = lanes((T, 64), FEAT)
        first = lanes((HALF, 128), HEAD_DIM) == 0
        scaled = q4.astype(f32) * (FEAT**-0.5)
        for pair in range(2):
            v2 = v_ref[:, pair * 128 : pair * 128 + 128]
            for tb in range(2):
                t0, s1 = tb * HALF, (tb + 1) * HALF
                got = []
                for e in range(2):
                    qm = jnp.where(qlane == pair * 2 + e, scaled, 0.0).astype(bf16)
                    a = dot(qm[t0 : t0 + HALF], k4[0:s1], NT)
                    p = (1.0 + a * (1.0 + 0.5 * a)) * mask_ref[t0 : t0 + HALF, 0:s1]
                    den = jnp.sum(p, axis=-1, keepdims=True)
                    got.append((dot(p.astype(bf16), v2[0:s1], NN), den))
                rden = 1.0 / jnp.where(first, got[0][1], got[1][1])
                ou = jnp.where(first, got[0][0], got[1][0]) * rden
                at = (slice(t0, t0 + HALF), slice(pair * 128, pair * 128 + 128))
                ou_ref[at] = ou
                rden_ref[at] = rden
                o_ref[at] = ou.astype(bf16)

    wide = (T, 256)
    col = lambda c: (0, c)
    return call(
        body,
        (4,),
        [(qk, (T, 128), col), (v, wide, col), seg_row, seg_col, live_row],
        [((T, D), bf16, wide, col), ((T, D), f32, wide, col), ((T, D), f32, wide, col)],
        scratch=[pltpu.VMEM((T, T), f32)],
        flops=HEADS * T * T * 2 * 192,
    )


def based_bwd(qk, v, dou, ou, rden, seg_row, seg_col, live_col):
    def body(qk_ref, v_ref, dou_ref, ou_ref, rden_ref, sr_ref, sc_ref, lc_ref, dqk_ref, dv_ref, mask_ref, dk_ref, dva_ref):
        @pl.when(pl.program_id(0) == 0)
        def _():
            fill_mask(mask_ref, sr_ref[...], sc_ref[...], lc_ref[...], 1, MAX_LEN)

        q4, k4 = qk_ref[:, 0:64], qk_ref[:, 64:128]
        qlane = lanes((T, 64), FEAT)
        q_scaled = q4.astype(f32) * (FEAT**-0.5)
        k_scaled = k4.astype(f32) * (FEAT**-0.5)
        vlane = lanes((T, 128), HEAD_DIM)
        dnum_f = dou_ref[...] * rden_ref[...]
        term = dnum_f * ou_ref[...]
        high = term.astype(bf16)
        low = (term - high.astype(f32)).astype(bf16)
        pick = jnp.where(
            lax.broadcasted_iota(i32, (8, 256), 0) == lanes((8, 256), HEAD_DIM), 1.0, 0.0
        ).astype(bf16)
        dden = -(dot(pick, high, NT) + dot(pick, low, NT))
        dk_ref[...] = jnp.zeros((T, 64), f32)
        dva_ref[...] = jnp.zeros((T, 256), f32)
        dq = [jnp.zeros((HALF, 64), f32), jnp.zeros((HALF, 64), f32)]
        for pair in range(2):
            cols = slice(pair * 128, pair * 128 + 128)
            v2 = v_ref[:, cols]
            for e in range(2):
                head = pair * 2 + e
                qm = jnp.where(qlane == head, q_scaled, 0.0).astype(bf16)
                km = jnp.where(qlane == head, k_scaled, 0.0).astype(bf16)
                dn = jnp.where(vlane == e, dnum_f[:, cols], 0.0).astype(bf16)
                for tb in range(2):
                    t0, s1 = tb * HALF, (tb + 1) * HALF
                    at = slice(t0, t0 + HALF)
                    a = dot(k4[0:s1], qm[at], NT)
                    m = mask_ref[0:s1, at]
                    p = (1.0 + a * (1.0 + 0.5 * a)) * m
                    dp = dot(v2[0:s1], dn[at], NT) + dden[head : head + 1, at]
                    da = (dp * m * (1.0 + a)).astype(bf16)
                    dk_ref[0:s1, :] += dot(da, qm[at], NN)
                    dva_ref[0:s1, cols] += dot(p.astype(bf16), dn[at], NN)
                    dq[tb] += dot(da, km[0:s1], TN)
        for tb in range(2):
            at = slice(tb * HALF, tb * HALF + HALF)
            dqk_ref[at, 0:64] = dq[tb].astype(bf16)
        dqk_ref[:, 64:128] = dk_ref[...].astype(bf16)
        dv_ref[...] = dva_ref[...].astype(bf16)

    wide = (T, 256)
    col = lambda c: (0, c)
    return call(
        body,
        (4,),
        [(qk, (T, 128), col), (v, wide, col), (dou, wide, col), (ou, wide, col), (rden, wide, col), seg_row, seg_col, live_col],
        [((T, 512), bf16, (T, 128), col), ((T, D), bf16, wide, col)],
        scratch=[pltpu.VMEM((T, T), f32), pltpu.VMEM((T, 64), f32), pltpu.VMEM((T, 256), f32)],
        flops=HEADS * T * T * 2 * 480,
    )


SPAN = ((0, HALF), (HALF - WINDOW, T))


def window_fwd(q, k, v, seg_row, seg_col, live_row):
    def body(q_ref, k_ref, v_ref, sr_ref, sc_ref, lr_ref, o_ref, mask_ref):
        @pl.when(pl.program_id(0) == 0)
        def _():
            fill_mask(mask_ref, sc_ref[...], sr_ref[...], lr_ref[...], 0, WINDOW)

        first = lanes((HALF, 128), HEAD_DIM) == 0
        qlane = lanes((T, 128), HEAD_DIM)
        scaled = q_ref[...].astype(f32) * (HEAD_DIM**-0.5)
        for tb in range(2):
            t0 = tb * HALF
            s0, s1 = SPAN[tb]
            ok = mask_ref[t0 : t0 + HALF, s0:s1] > 0.5
            got = []
            for e in range(2):
                qm = jnp.where(qlane == e, scaled, 0.0).astype(bf16)
                c = dot(qm[t0 : t0 + HALF], k_ref[s0:s1, :], NT)
                c = jnp.where(ok, c, NEG)
                w = jnp.exp(c - jnp.max(c, axis=-1, keepdims=True))
                w = w * (1.0 / jnp.sum(w, axis=-1, keepdims=True))
                got.append(dot(w.astype(bf16), v_ref[s0:s1, :], NN))
            o_ref[t0 : t0 + HALF, :] = jnp.where(first, got[0], got[1]).astype(bf16)

    blk = (T, 128)
    col = lambda c: (0, c)
    return call(
        body,
        (8,),
        [(q, blk, col), (k, blk, col), (v, blk, col), seg_row, seg_col, live_row],
        [((T, D), bf16, blk, col)],
        scratch=[pltpu.VMEM((T, T), f32)],
        flops=HEADS * T * T * 2 * 192,
    )[0]


def window_bwd(q, k, v, dor, seg_row, seg_col, live_col):
    def body(q_ref, k_ref, v_ref, do_ref, sr_ref, sc_ref, lc_ref, dq_ref, dk_ref, dv_ref, mask_ref, dka_ref, dva_ref):
        @pl.when(pl.program_id(0) == 0)
        def _():
            fill_mask(mask_ref, sr_ref[...], sc_ref[...], lc_ref[...], 1, WINDOW)

        lane = lanes((T, 128), HEAD_DIM)
        q_scaled = q_ref[...].astype(f32) * (HEAD_DIM**-0.5)
        k_scaled = k_ref[...].astype(f32) * (HEAD_DIM**-0.5)
        do = do_ref[...]
        dka_ref[...] = jnp.zeros((T, 128), f32)
        dva_ref[...] = jnp.zeros((T, 128), f32)
        for tb in range(2):
            at = slice(tb * HALF, tb * HALF + HALF)
            s0, s1 = SPAN[tb]
            ok = mask_ref[s0:s1, at] > 0.5
            dq = jnp.zeros((HALF, 128), f32)
            for e in range(2):
                qm = jnp.where(lane == e, q_scaled, 0.0).astype(bf16)
                km = jnp.where(lane == e, k_scaled, 0.0).astype(bf16)
                dm = jnp.where(lane == e, do, jnp.zeros_like(do))
                c = dot(k_ref[s0:s1, :], qm[at], NT)
                c = jnp.where(ok, c, NEG)
                w = jnp.exp(c - jnp.max(c, axis=0, keepdims=True))
                w = w * (1.0 / jnp.sum(w, axis=0, keepdims=True))
                dw = dot(v_ref[s0:s1, :], dm[at], NT)
                ds = (w * (dw - jnp.sum(w * dw, axis=0, keepdims=True))).astype(bf16)
                dka_ref[s0:s1, :] += dot(ds, qm[at], NN)
                dva_ref[s0:s1, :] += dot(w.astype(bf16), dm[at], NN)
                dq += dot(ds, km[s0:s1], TN)
            dq_ref[at, :] = dq.astype(bf16)
        dk_ref[...] = dka_ref[...].astype(bf16)
        dv_ref[...] = dva_ref[...].astype(bf16)

    blk = (T, 128)
    col = lambda c: (0, c)
    return call(
        body,
        (8,),
        [(q, blk, col), (k, blk, col), (v, blk, col), (dor, blk, col), seg_row, seg_col, live_col],
        [((T, D), bf16, blk, col)] * 3,
        scratch=[pltpu.VMEM((T, T), f32), pltpu.VMEM((T, 128), f32), pltpu.VMEM((T, 128), f32)],
        flops=HEADS * T * T * 2 * 480,
    )


def attn_out(me, h, o, strip, gain):
    kern = Kernel(3, [strip], 2)

    def body(me_ref, *refs):
        (h_ref, o_ref, gain_ref), hold, (hm_ref, xf_ref), (or_ref,) = kern.split(refs)
        i = pl.program_id(0)

        @pl.when(i == 0)
        def _():
            start_all(hold)
            regroup(or_ref, o_ref, ROWS, me_ref[0])

        x, core = step_place(i)
        s, _, box, sems = hold[0]
        s.wait(box, sems, core, x)
        at = pl.ds(pl.multiple_of(step_col(i, me_ref) * 256, 256), 256)
        hm_ref[:, at] = h_ref[:, at].astype(f32) + dot(or_ref[...], col_block(s, box, x, core), NN)

        @pl.when(i == COLS - 1)
        def _():
            hm = hm_ref[...]
            xf_ref[...] = (hm * norm_factor(hm) * gain_ref[...]).astype(bf16)

    full = whole_map(T, D)
    return call(
        body, (COLS,), [h, o, gain.reshape(1, D)] + kern.ins(),
        [((T, D), f32, (T, D), full), ((T, D), bf16, (T, D), full)],
        scratch=kern.scratch() + [pltpu.VMEM((T, D), bf16)], flops=2 * T * D * D, prefetch=me,
    )


def hidden_block(s, box, x, core):
    return jnp.concatenate([s.piece(box, z, y, x, core)[...] for z, y in BLOCKS], axis=1)


def gate_up(me, xf, w_gate, w_up):
    kern = Kernel(1, [w_gate, w_up], 3)

    def body(me_ref, *refs):
        (xf_ref,), hold, (g_ref, u_ref, hid_ref), (xr_ref,) = kern.split(refs)
        i = pl.program_id(0)

        @pl.when(i == 0)
        def _():
            start_all(hold)
            regroup(xr_ref, xf_ref, ROWS, me_ref[0])

        x, core = step_place(i)
        got = []
        for s, _, box, sems in hold:
            s.wait(box, sems, core, x)
            got.append(dot(hidden_block(s, box, x, core), xr_ref[...], NT))
        g, u = got
        g_ref[...] = g.astype(bf16)
        u_ref[...] = u.astype(bf16)
        hid_ref[...] = (g * (1.0 / (1.0 + jnp.exp(-g))) * u).astype(bf16)

    row = lambda i, me: (step_col(i, me), 0)
    return call(
        body, (COLS,), [xf] + kern.ins(), [((FFP, T), bf16, (FC, T), row)] * 3,
        scratch=kern.scratch() + [pltpu.VMEM((T, D), bf16)], flops=4 * T * D * FFP, prefetch=me,
    )


def down_rows(me_ref, hold, z):
    (s1, _, box1, _), (s2, _, box2, _) = hold
    halves = []
    for y in range(2):
        yr = y ^ me_ref[0]
        parts = []
        for x, core in PLACES:
            parts += [s1.piece(box1, z, yr, x, core)[...], s2.piece(box2, z, yr, x, core)[...]]
        halves.append(jnp.concatenate(parts, axis=1))
    return jnp.concatenate(halves, axis=0)


def down(me, hm, hid, strips):
    kern = Kernel(2, strips, 1)

    def body(me_ref, *refs):
        (hm_ref, hid_ref), hold, (h_ref,), (acc_ref,) = kern.split(refs)
        i = pl.program_id(0)

        @pl.when(i == 0)
        def _():
            start_all(hold)
            regroup(acc_ref, hm_ref, COLS, me_ref[1])
            for s, _, box, sems in hold:
                s.wait_all(box, sems)

        acc_ref[...] += dot(hid_ref[...], down_rows(me_ref, hold, i), TN)

        @pl.when(i == COLS - 1)
        def _():
            regroup(h_ref, acc_ref, COLS, me_ref[1])

    return call(
        body, (COLS,), [hm, (hid, (FC, T), lambda i, me: (i, 0))] + kern.ins(),
        [((T, D), f32, (T, D), whole_map(T, D))],
        scratch=kern.scratch() + [pltpu.VMEM((T, D), f32)], flops=2 * T * D * FFP, prefetch=me,
    )[0]


def down_bwd(me, bd, strips, hid, g, u):
    kern = Kernel(4, strips, 6)

    def body(me_ref, *refs):
        (bd_ref, hid_ref, g_ref, u_ref), hold, (dg_ref, du_ref, *p_refs), (br_ref,) = kern.split(refs)
        i = pl.program_id(0)

        @pl.when(i == 0)
        def _():
            start_all(hold)
            regroup(br_ref, bd_ref, COLS, me_ref[1])

        bdv = br_ref[...].astype(bf16)
        gwd = dot(hid_ref[...], bdv, NN).astype(bf16)
        for x, core in PLACES:
            at = (x * 2 + core) * 256
            for y in range(2):
                yr = y ^ me_ref[0]
                rows = slice(y * FBP, (y + 1) * FBP)
                p_refs[core][x, yr, 0] = gwd[rows, at : at + 128]
                p_refs[2 + core][yr, x, 0] = gwd[rows, at + 128 : at + 256]

        @pl.when(i == 0)
        def _():
            for s, _, box, sems in hold:
                s.wait_all(box, sems)

        dhid = dot(down_rows(me_ref, hold, i), bdv, NT)
        gv, uv = g_ref[...].astype(f32), u_ref[...].astype(f32)
        sig = 1.0 / (1.0 + jnp.exp(-gv))
        act = gv * sig
        du_ref[...] = (dhid * act).astype(bf16)
        dg_ref[...] = (dhid * uv * (sig + act * (1.0 - sig))).astype(bf16)

    row = lambda i, me: (i, 0)
    hblk = (FC, T)
    pieces = ((2, 2, 4, FBP, 128), bf16, (2, 2, 1, FBP, 128), lambda i, me: (0, 0, i, 0, 0))
    return call(
        body, (COLS,), [bd, (hid, hblk, row), (g, hblk, row), (u, hblk, row)] + kern.ins(),
        [((FFP, T), bf16, hblk, row), ((FFP, T), bf16, hblk, row)] + [pieces] * 4,
        scratch=kern.scratch() + [pltpu.VMEM((T, D), bd.dtype)], flops=4 * T * D * FFP, prefetch=me,
    )


def piece_specs(n1, n2):
    out = []
    for n, block, place in ((n1, (1, 2, 4), lambda j: (j, 0)), (n2, (2, 1, 4), lambda j: (0, j))):
        for step in (lambda i: jnp.minimum(i, 1), lambda i: jnp.maximum(i - 2, 0)):
            index = functools.partial(lambda place, step, i, me: (*place(step(i)), 0, 0, 0), place, step)
            out.append(((2, 2, 4, n, 128), bf16, (*block, n, 128), index))
    return out


def for_core(refs, write):
    for core in range(2):

        @pl.when(pl.program_id(0) // 2 == core)
        def _():
            write(refs[core], refs[2 + core])


def gate_up_bwd(me, xf, dg, du):
    def body(me_ref, xf_ref, dg_ref, du_ref, *refs):
        *p_refs, xr_ref = refs

        @pl.when(pl.program_id(0) == 0)
        def _():
            regroup(xr_ref, xf_ref, ROWS, me_ref[0])

        gwg = dot(dg_ref[...], xr_ref[...], NN).astype(bf16)
        gwu = dot(du_ref[...], xr_ref[...], NN).astype(bf16)

        def write(one, two):
            for r, (z, y) in enumerate(BLOCKS):
                one[0, y, z] = gwg[:, r * 128 : (r + 1) * 128]
                two[y, 0, z] = gwu[:, r * 128 : (r + 1) * 128]

        for_core(p_refs, write)

    row = lambda i, me: (step_col(i, me), 0)
    return call(
        body, (COLS,), [xf, (dg, (FC, T), row), (du, (FC, T), row)], piece_specs(FC, FC),
        scratch=[pltpu.VMEM((T, D), bf16)], flops=4 * T * D * FFP, prefetch=me,
    )


def norm_bwd(dx, h, gain, g):
    rf = norm_factor(h)
    hr = h * rf
    dgain = jnp.sum(dx * hr, axis=0, keepdims=True)
    gd = gain * dx
    mean = jnp.sum(gd * hr, axis=-1, keepdims=True) * (1.0 / D)
    return dgain, g + rf * (gd - hr * mean)


def add_to(acc_ref, part):
    @pl.when(pl.program_id(0) == 0)
    def _():
        acc_ref[...] = part

    @pl.when(pl.program_id(0) > 0)
    def _():
        acc_ref[...] += part


def mlp_dx(me, dg, du, w_gate, w_up, hm, gain, g, w_out, kind):
    kern = Kernel(5, [w_gate, w_up, w_out], 4)

    def body(me_ref, *refs):
        (dg_ref, du_ref, hm_ref, gain_ref, g_ref), hold, outs, (acc_ref, un_ref, br_ref) = kern.split(refs)
        gm_ref, bo_ref, dou_ref, gg_ref = outs
        i = pl.program_id(0)

        @pl.when(i == 0)
        def _():
            start_all(hold)

        x, core = step_place(i)
        part = None
        for (s, _, box, sems), d_ref in zip(hold[:2], (dg_ref, du_ref)):
            s.wait(box, sems, core, x)
            term = dot(d_ref[...], hidden_block(s, box, x, core), TN)
            part = term if part is None else part + term
        add_to(acc_ref, part)

        @pl.when(i == COLS - 1)
        def _():
            regroup(un_ref, acc_ref, ROWS, me_ref[0])
            gg, gm = norm_bwd(un_ref[...], hm_ref[...], gain_ref[...], g_ref[...].astype(f32))
            gg_ref[...] = gg
            gm_ref[...] = gm
            bo_ref[...] = gm.astype(bf16)
            regroup(br_ref, bo_ref, COLS, me_ref[1])
            s, _, box, sems = hold[2]
            s.wait_all(box, sems)
            w = jnp.concatenate([col_block(s, box, x, core) for x, core in PLACES], axis=1)
            acc_ref[...] = dot(br_ref[...], w, NT)
            regroup(un_ref, acc_ref, ROWS, me_ref[0])
            dou_ref[...] = un_ref[...].astype(kind)

    row = lambda i, me: (step_col(i, me), 0)
    full = whole_map(T, D)
    return call(
        body, (COLS,), [(dg, (FC, T), row), (du, (FC, T), row), hm, gain.reshape(1, D), g] + kern.ins(),
        [((T, D), f32, (T, D), full), ((T, D), bf16, (T, D), full), ((T, D), kind, (T, D), full), ((1, D), f32, (1, D), full)],
        scratch=kern.scratch() + [pltpu.VMEM((T, D), f32), pltpu.VMEM((T, D), f32), pltpu.VMEM((T, D), bf16)],
        flops=4 * T * D * FFP + 2 * T * D * D, prefetch=me,
    )


def attn_bwd(me, xa, grads, strips, o, bo, h, gain, gm, halves):
    n = len(grads)
    kern = Kernel(6 + n, strips, 6)

    def body(me_ref, *refs):
        ins, hold, (*p_refs, g_ref, gg_ref), (xr_ref, or_ref, acc_ref) = kern.split(refs)
        xa_ref, o_ref, h_ref, gain_ref, gm_ref, bo_ref, *d_refs = ins
        i = pl.program_id(0)

        @pl.when(i == 0)
        def _():
            start_all(hold)
            regroup(xr_ref, xa_ref, ROWS, me_ref[0])
            regroup(or_ref, o_ref, ROWS, me_ref[0])

        tiles = [dot(xr_ref[...], d[...], TN).astype(bf16) for d in d_refs]
        tiles.append(dot(or_ref[...], bo_ref[...], TN).astype(bf16))

        def write(one, two):
            for j, (which, at) in enumerate(halves[0]):
                for r, (z, y) in enumerate(BLOCKS):
                    one[0, y, z, j * 128 : (j + 1) * 128] = tiles[which][r * 128 : (r + 1) * 128, at : at + 128]
            for j, (which, at) in enumerate(halves[1]):
                for r, (z, y) in enumerate(BLOCKS):
                    two[y, 0, z, j * 128 : (j + 1) * 128] = tiles[which][r * 128 : (r + 1) * 128, at : at + 128]

        for_core(p_refs, write)
        x, core = step_place(i)
        part = None
        for (s, _, box, sems), d in zip(hold, d_refs):
            s.wait(box, sems, core, x)
            term = dot(d[...], col_block(s, box, x, core), NT)
            part = term if part is None else part + term
        add_to(acc_ref, part)

        @pl.when(i == COLS - 1)
        def _():
            regroup(g_ref, acc_ref, ROWS, me_ref[0])
            gg, g = norm_bwd(g_ref[...], h_ref[...].astype(f32), gain_ref[...], gm_ref[...])
            gg_ref[...] = gg
            g_ref[...] = g

    col = lambda i, me: (0, step_col(i, me))
    full = whole_map(T, D)
    ins = [xa, o, h, gain.reshape(1, D), gm, (bo, (T, 256), col)]
    ins += [(d, (T, d.shape[1] // COLS), col) for d in grads]
    total = sum(d.shape[1] for d in grads)
    return call(
        body, (COLS,), ins + kern.ins(),
        piece_specs(128 * len(halves[0]), 128 * len(halves[1])) + [((T, D), f32, (T, D), full), ((1, D), f32, (1, D), full)],
        scratch=kern.scratch() + [pltpu.VMEM((T, D), bf16), pltpu.VMEM((T, D), bf16), pltpu.VMEM((T, D), f32)],
        flops=4 * T * D * total + 2 * T * D * D, prefetch=me,
    )


HALVES_ONE = (((1, 0), (1, 128)), ((0, 0), (2, 0), (2, 128)))
HALVES_TWO = (((0, 0), (0, 128), (1, 0), (1, 128)), ((2, 0), (2, 128), (3, 0), (3, 128)))


def attn_weights(bufs, halves):
    out = []
    for which in range(1 + max(w for half in halves for w, _ in half)):
        for k, half in enumerate(halves):
            at = [j for j, (w, _) in enumerate(half) if w == which]
            if at:
                out.append(Strips(bufs[k], k == 1, at[0] * 128, len(at) * 128))
    return out


def gate_weights(bufs):
    return Strips(bufs[0], False, 0, FC), Strips(bufs[1], True, 0, FC)


def down_weights(bufs):
    return [Strips(bufs[0], False, 0, FBP), Strips(bufs[1], True, 0, FBP)]


def pad_hidden(w):
    k = w.shape[0]
    return jnp.pad(w.reshape(k, -1, FB), ((0, 0), (0, 0), (0, FBP - FB))).reshape(k, -1).T


def pad_rows(w):
    n = w.shape[1]
    return jnp.pad(w.reshape(-1, FB, n), ((0, 0), (0, FBP - FB), (0, 0))).reshape(-1, n)


def strips_of(blocks, halves):
    return tuple(
        jnp.concatenate([blocks[which][..., at : at + 128] for which, at in strips], axis=-2) for strips in halves
    )


def after(value, *arrays):
    return lax.optimization_barrier((value, *arrays))[0] if arrays else value


class Ring:
    def __init__(self, names):
        self.axes = names
        self.z = lax.axis_index(names[0])

    def swap(self, value, axis, by=1):
        shift = {"z": 3, "y": 2, "x": 1, "core": 0}[axis]
        return lax.ppermute(value, self.axes, [(i, i ^ (by << shift)) for i in range(32)])

    def gather_z(self, both):
        near = [both] + [self.swap(both, "z", by) for by in (1, 2, 3)]
        low, high = self.z % 2 == 1, self.z >= 2
        a, b = jnp.where(low, near[1], near[0]), jnp.where(low, near[0], near[1])
        c, d = jnp.where(low, near[3], near[2]), jnp.where(low, near[2], near[3])
        pick = lambda p, q: jnp.where(high, q, p)
        return jnp.stack([pick(a, c), pick(b, d), pick(c, a), pick(d, b)])

    def gather_z_all(self, both):
        return lax.all_gather(both, self.axes[0], axis=0, tiled=False)

    def gather_lo(self, pair, *behind):
        got = [after(self.swap(v, axis), *behind) for v, axis in zip(pair, ("x", "y"))]
        return [jnp.stack([v, g]) for v, g in zip(pair, got)]

    def gather_hi(self, pair, *behind):
        return [[v, after(self.swap(v, axis), *behind)] for v, axis in zip(pair, ("y", "x"))]

    def gather_core(self, full, *behind):
        return [half + [after(self.swap(b, "core"), *behind) for b in half] for half in full]

    def reduce_core(self, four, *behind):
        out = []
        for own, send in (four[:2], four[2:]):
            got = after(self.swap(send, "core"), *behind)
            out += [own[0] + got[0], own[1] + got[1]]
        return out

    def reduce_lo(self, four, *behind):
        out = []
        for (keep, go), axis in ((four[:2], "x"), (four[2:], "y")):
            got = after(self.swap(go, axis), *behind)
            out += [keep[0] + got[0], keep[1] + got[1]]
        return out

    def reduce_hi(self, four, *behind):
        pairs = ((four[:2], "y"), (four[2:], "x"))
        return [keep + after(self.swap(go, axis), *behind) for (keep, go), axis in pairs]

    def reduce_z(self, pair):
        n1 = pair[0].shape[1]
        both = jnp.concatenate(pair, axis=1)
        here = lambda by: lax.dynamic_index_in_dim(both, self.z ^ by, 0, False)
        total = here(0).astype(f32)
        for by in (1, 2, 3):
            total = total + self.swap(here(by), "z", by).astype(f32)
        return total[:n1], total[n1:]

    def reduce_z_all(self, pair):
        n1 = pair[0].shape[1]
        both = jnp.concatenate(pair, axis=1)
        total = lax.psum_scatter(both, self.axes[0], scatter_dimension=0, tiled=False).astype(f32)
        return total[:n1], total[n1:]


def pack(shards, halves):
    *attn, gate, up, dn = shards
    dp = pad_rows(dn)
    return [strips_of(attn, halves), (pad_hidden(gate), pad_hidden(up)), (dp[:, :128], dp[:, 128:])]


def boxes_any(weights, halves):
    *attn, gate, up, dn = weights

    def cut(w, rows, cols):
        return w.reshape(4, 2, rows, 2, 2, cols).transpose(0, 1, 3, 4, 2, 5)

    def boxes(one, two):
        first = [one[:, y, :, core].transpose(1, 0, 2, 3) for core in range(2) for y in range(2)]
        second = [two[:, :, x, core].transpose(1, 0, 2, 3) for core in range(2) for x in range(2)]
        return first, second

    a = boxes(*strips_of([cut(w, D // ROWS, w.shape[1] // COLS) for w in attn], halves))
    hidden = lambda w: pad_hidden(w).reshape(2, 2, FC, 4, 2, 128).transpose(3, 4, 0, 1, 2, 5)
    d = cut(pad_rows(dn), FBP, 256)
    return [a, boxes(hidden(gate), hidden(up)), boxes(d[..., :128], d[..., 128:])]


def unpad_hidden(g):
    k = g.shape[1]
    return g.reshape(-1, FBP, k)[:, :FB].reshape(-1, k).T


def unpad_rows(g):
    n = g.shape[1]
    return g.reshape(-1, FBP, n)[:, :FB].reshape(-1, n)


def whole_grad(own, send, swapped):
    p = jnp.stack([own, send])
    if swapped:
        p = jnp.swapaxes(p, 1, 2)
    core, x, y, z, n, w = p.shape
    return p.transpose(3, 2, 1, 0, 4, 5).reshape(z * y, x * core, n, w)


def join_strips(one, two, halves):
    out = []
    for which in range(1 + max(w for half in halves for w, _ in half)):
        got = {}
        for src, strips in ((one, halves[0]), (two, halves[1])):
            for j, (w, at) in enumerate(strips):
                if w == which:
                    got[at] = src[..., j * 128 : j * 128 + 128, :]
        out.append(jnp.concatenate([got[a] for a in sorted(got)], axis=-1))
    return out


def scatter_any(w):
    part = lax.psum_scatter(w, "row", scatter_dimension=0, tiled=True)
    return lax.psum_scatter(part, "col", scatter_dimension=1, tiled=True).astype(f32)


def natural(blocks):
    r, c, n, w = blocks.shape
    return blocks.transpose(0, 2, 1, 3).reshape(r * n, c * w)


def sum_any(pd, pgu, pa, halves):
    pairs = lambda p: (whole_grad(*p[:2], False), whole_grad(*p[2:], True))
    dn = scatter_any(unpad_rows(natural(jnp.concatenate(pairs(pd), axis=-1))))
    gu = [scatter_any(unpad_hidden(g.transpose(1, 2, 0, 3).reshape(FFP, D))) for g in pairs(pgu)]
    blocks = join_strips(*pairs(pa), halves)
    if len(blocks) == 3:
        blocks = [blocks[0][..., :64], blocks[0][..., 64:]] + blocks[1:]
    return [scatter_any(natural(b)) for b in blocks] + gu + [dn]


def join_qk(q, k, parts):
    n = q.shape[0]
    both = jnp.concatenate([q.reshape(n, parts, -1), k.reshape(n, parts, -1)], axis=2)
    return both.reshape(n, -1)

def route_plan(dest_slot, block_tokens, rows, cols):
    row_count = lax.axis_size(rows)
    col_count = lax.axis_size(cols)
    per_peer = block_tokens // row_count
    row_at = lax.axis_index(rows)
    col_at = lax.axis_index(cols)
    slot_table = dest_slot.reshape(row_count, col_count, block_tokens)
    column = lax.dynamic_index_in_dim(slot_table, col_at, 1, False)
    own_slots = lax.dynamic_index_in_dim(column, row_at, 0, False)
    send_order = jnp.argsort(own_slots)
    arrived = jnp.sort(column, axis=1)
    incoming = lax.dynamic_slice_in_dim(arrived, row_at * per_peer, per_peer, 1)
    local_slots = incoming.reshape(-1) - (row_at * col_count + col_at) * block_tokens
    placing = jnp.argsort(local_slots)
    return (send_order, local_slots, placing)


def exchange(value, axis):
    n, width = value.shape
    row_count = lax.axis_size(axis)
    got = lax.all_to_all(value.reshape(row_count, n // row_count, width), axis, split_axis=0, concat_axis=0, tiled=True)
    return got.reshape(n, width)


def gather_all(shards):
    return [lax.all_gather(lax.all_gather(w, "col", axis=1, tiled=True), "row", axis=0, tiled=True) for w in shards]


def body(names, tokens, cotangent, dest_slot, lengths, pad_mask, *params):
    ring = Ring(names) if len(names) == 4 else None
    rows, cols = (names[:2], names[2:]) if ring else names
    gain_a1, bq, bk, bv, bo_w, gain_m1, wg1, wu1, wd1 = params[:9]
    gain_a2, wq, wk, wv, wo2, gain_m2, wg2, wu2, wd2 = params[9:]
    shards1, shards2 = [bq, bk, bv, bo_w, wg1, wu1, wd1], [wq, wk, wv, wo2, wg2, wu2, wd2]
    send_order, local_slots, placing = route_plan(dest_slot, T, rows, cols)
    restore = jnp.argsort(send_order)
    outgoing = tokens[send_order]
    cot_going = cotangent[send_order]
    if ring:
        me = jnp.stack([lax.axis_index(names[1]), lax.axis_index(cols)]).astype(i32)
        packs = pack([join_qk(bq, bk, 1)] + shards1[2:], HALVES_ONE) + pack(shards2, HALVES_TWO)
        flat = [jnp.concatenate(p, axis=0) for p in packs]
        near = [ring.gather_z(flat[0])]
        for f in flat[1:4]:
            near.append(ring.gather_z(after(f, near[-1], outgoing)))
        rest = ring.gather_z_all(after(jnp.concatenate(flat[4:], axis=0), near[1]))
        near += [rest[:, : flat[4].shape[0]], rest[:, flat[4].shape[0] :]]
        near = [[v[:, : p[0].shape[0]], v[:, p[0].shape[0] :]] for p, v in zip(packs, near)]
        start = exchange(outgoing, rows)[placing]
    else:
        me = jnp.zeros((2,), i32)
        one, two = gather_all(shards1), gather_all(shards2)
        full = boxes_any([join_qk(one[0], one[1], COLS)] + one[2:], HALVES_ONE) + boxes_any(two, HALVES_TWO)
        start = exchange(outgoing, rows)[placing]
    position = jnp.arange(T, dtype=i32)
    segment, end = jnp.zeros((T,), i32), jnp.zeros((), i32)
    for j in range(lengths.shape[1]):
        end = end + lengths[0, j]
        segment = segment + (position >= end).astype(i32)
    seg_row, seg_col = segment.reshape(1, T), segment.reshape(T, 1)
    live_row, live_col = pad_mask.reshape(1, T), pad_mask.reshape(T, 1)

    tied = after if ring else (lambda value, *arrays: value)
    if ring:
        near_a1, near_gu1, near_d1, near_a2, near_gu2, near_d2 = near
        each = lambda pair, *arrays: [after(v, *arrays) for v in pair]
        far = lambda halves: [half[1] for half in halves]
        hi_a1 = ring.gather_hi(ring.gather_lo(near_a1))
        lo_gu1 = ring.gather_lo(each(near_gu1, *far(hi_a1)))
        full_a1 = ring.gather_core(hi_a1)
        start = after(start, *lo_gu1)
    else:
        full_a1 = full[0]
    w_qk, w_v, w_o = attn_weights(full_a1, HALVES_ONE)
    xa1, qk1, v1 = norm_proj(me, start, gain_a1, [w_qk, w_v])
    o1, ou1, rden1 = based_fwd(qk1, v1, seg_row, seg_col, live_row)
    if ring:
        hi_gu1 = ring.gather_hi(lo_gu1, o1)
        lo_d1 = ring.gather_lo(each(near_d1, *lo_gu1), o1)
    hm1, xf1 = attn_out(me, start, tied(o1, *(far(hi_gu1) + lo_d1 if ring else [])), w_o, gain_m1)
    if ring:
        full_gu1 = ring.gather_core(hi_gu1, xf1)
        hi_d1 = ring.gather_hi(lo_d1, xf1)
        lo_a2 = ring.gather_lo(each(near_a2, *far(hi_gu1)), xf1)
        cot_going = after(cot_going, xf1)
        xf1_late = after(xf1, *far(hi_d1), *lo_a2)
    else:
        full_gu1, xf1_late = full[1], xf1
    cot = exchange(cot_going, rows)[placing]
    w_g, w_u = gate_weights(full_gu1)
    g1, u1, hid1 = gate_up(me, xf1_late, w_g, w_u)
    if ring:
        full_d1 = ring.gather_core(hi_d1, hid1)
        hi_a2 = ring.gather_hi(lo_a2, hid1)
        lo_gu2 = each(near_gu2, *far(hi_d1))
        hid1_late = after(hid1, *far(hi_a2))
    else:
        full_d1, hid1_late = full[2], hid1
    w_d = down_weights(full_d1)
    h1 = down(me, hm1, hid1_late, w_d)
    if ring:
        full_a2 = ring.gather_core(hi_a2, h1)
        lo_gu2 = ring.gather_lo(lo_gu2, h1)
        h1_late = after(h1, *lo_gu2)
    else:
        full_a2, h1_late = full[3], h1
    v_q, v_k, v_v, v_o = attn_weights(full_a2, HALVES_TWO)
    xa2, q2, k2, v2 = norm_proj(me, h1_late, gain_a2, [v_q, v_k, v_v])
    o2 = window_fwd(q2, k2, v2, seg_row, seg_col, live_row)
    if ring:
        hi_gu2 = ring.gather_hi(lo_gu2, o2)
        lo_d2 = ring.gather_lo(each(near_d2, *lo_gu2), o2)
    hm2, xf2 = attn_out(me, h1, tied(o2, *(far(hi_gu2) + lo_d2 if ring else [])), v_o, gain_m2)
    if ring:
        full_gu2 = ring.gather_core(hi_gu2, xf2)
        hi_d2 = ring.gather_hi(lo_d2, xf2)
        xf2_late = after(xf2, *far(hi_d2))
    else:
        full_gu2, xf2_late = full[4], xf2
    v_g, v_u = gate_weights(full_gu2)
    g2, u2, hid2 = gate_up(me, xf2_late, v_g, v_u)
    v_d = down_weights(ring.gather_core(hi_d2, hid2) if ring else full[5])

    step = (lambda f, v, *behind: f(v, *behind)) if ring else (lambda f, v, *behind: v)
    core, low, high = (ring.reduce_core, ring.reduce_lo, ring.reduce_hi) if ring else (None,) * 3
    dg2, du2, *d2 = down_bwd(me, cot, v_d, hid2, g2, u2)
    gu2 = gate_up_bwd(me, xf2, dg2, du2)
    d2 = step(core, d2, gu2[0])
    gm2, bo2, dor2, gg_m2 = mlp_dx(me, tied(dg2, *d2, *gu2), du2, v_g, v_u, hm2, gain_m2, cot, v_o, bf16)
    d2, gu2 = step(low, d2, gm2), step(core, gu2, gm2)
    dq2, dk2, dv2 = window_bwd(q2, k2, v2, tied(dor2, *d2, *gu2), seg_row, seg_col, live_col)
    d2 = step(high, d2, dq2)
    *a2, gh1, gg_a2 = attn_bwd(me, xa2, [tied(dq2, *d2), dk2, dv2], [v_q, v_k, v_v], o2, bo2, h1, gain_a2, gm2, HALVES_TWO)
    gu2 = step(low, gu2, gh1)
    dg1, du1, *d1 = down_bwd(me, tied(gh1, *gu2), w_d, hid1, g1, u1)
    gu2, a2 = step(high, gu2, dg1), step(core, a2, dg1)
    gu1 = gate_up_bwd(me, xf1, tied(dg1, *gu2, *a2), du1)
    a2, d1 = step(low, a2, gu1[0]), step(core, d1, gu1[0])
    gm1, bo1, dou1, gg_m1 = mlp_dx(me, tied(dg1, *a2, *d1, *gu1), du1, w_g, w_u, hm1, gain_m1, gh1, w_o, f32)
    a2, d1, gu1 = step(high, a2, gm1), step(low, d1, gm1), step(core, gu1, gm1)
    dqk1, dv1 = based_bwd(qk1, v1, tied(dou1, *a2, *d1, *gu1), ou1, rden1, seg_row, seg_col, live_col)
    d1 = step(high, d1, dqk1)
    *a1, g0, gg_a1 = attn_bwd(me, xa1, [tied(dqk1, *d1), dv1], [w_qk, w_v], o1, bo1, start, gain_a1, gm1, HALVES_ONE)
    gu1 = step(low, gu1, g0)
    h2 = down(me, tied(hm2, g0), hid2, v_d)
    output = exchange(h2.astype(bf16)[local_slots], rows)[restore]
    gains = jnp.concatenate([gg_a1, gg_m1, gg_a2, gg_m2], axis=0)
    if ring:
        gu1, a1 = high(gu1), high(low(core(a1)))
        sums = []
        for a, gu, d, halves in ((a1, gu1, d1, HALVES_ONE), (a2, gu2, d2, HALVES_TWO)):
            last = halves is HALVES_ONE
            sa = (ring.reduce_z if last else ring.reduce_z_all)(a)
            sgu = (ring.reduce_z if last else ring.reduce_z_all)(gu)
            sd = ring.reduce_z_all(d)
            sums.append(join_strips(*sa, halves) + [unpad_hidden(sgu[0]), unpad_hidden(sgu[1]), unpad_rows(jnp.concatenate(sd, axis=1))])
        sums1, sums2 = sums
        sums1 = [sums1[0][:, :64], sums1[0][:, 64:]] + sums1[1:]
        for axis, by in (("core", 1), ("x", 1), ("y", 1), ("z", 1), ("z", 2)):
            gains = gains + ring.swap(gains, axis, by)
    else:
        sums1 = sum_any(d1, gu1, a1, HALVES_ONE)
        sums2 = sum_any(d2, gu2, a2, HALVES_TWO)
        gains = lax.psum(gains, ("row", "col"))
    tokens_grad = exchange(g0.astype(bf16)[local_slots], rows)[restore]
    return (
        output, tokens_grad,
        gains[0], *sums1[:4], gains[1], *sums1[4:],
        gains[2], *sums2[:4], gains[3], *sums2[4:],
    )


def solution(mesh):
    names, rows, cols = ("row", "col"), "row", "col"
    if (mesh.shape["row"], mesh.shape["col"]) == (ROWS, COLS):
        names = ("z", "y", "x", "core")
        rows, cols = names[:2], names[2:]
        mesh = Mesh(mesh.devices.reshape(4, 2, 2, 2), names)
    block, weight = P(names, None), P(rows, cols)
    layer_in = (P(),) + (weight,) * 4 + (P(),) + (weight,) * 3
    return jax.shard_map(
        functools.partial(body, names),
        mesh=mesh,
        in_specs=(block, block, P(), block, P(names)) + layer_in * 2,
        out_specs=(block, block) + layer_in * 2,
        check_vma=False,
    )
```

```python
import functools

import jax
import jax.numpy as jnp
from jax import lax
from jax.experimental import pallas as pl
from jax.experimental.pallas import tpu as pltpu
from jax.sharding import Mesh, PartitionSpec as P

HEADS = 16
FEAT = 16
HEAD_DIM = 64
WINDOW = 64
MAX_LEN = 256
D = 1024
T = 512
HALF = 256
EPS = 1e-05
NEG = -1e30
ROWS = 8
COLS = 4
FB = 344
FBP = 352
FFP = ROWS * FBP
FC = FFP // COLS

bf16, f32, i32 = jnp.bfloat16, jnp.float32, jnp.int32
NN, NT, TN = ((1,), (0,)), ((1,), (1,)), ((0,), (0,))


def dot(a, b, dims):
    return lax.dot_general(a, b, (dims, ((), ())), preferred_element_type=f32)


def call(body, grid, ins, outs, scratch=(), flops=0, prefetch=None):
    extra = 0 if prefetch is None else 1

    def spec(block, index):
        if block is None:
            return pl.BlockSpec(memory_space=pl.ANY)
        return pl.BlockSpec(block, index)

    in_specs, args = [], []
    for item in ins:
        if not isinstance(item, tuple):
            nd = item.ndim
            item = (item, item.shape, functools.partial(lambda n, *_: (0,) * n, nd))
        args.append(item[0])
        in_specs.append(spec(item[1], item[2]))
    out_specs = [spec(o[2], o[3]) for o in outs]
    out_shape = [jax.ShapeDtypeStruct(o[0], o[1]) for o in outs]
    moved = sum(a.size * a.dtype.itemsize for a in args)
    moved += sum(s.size * s.dtype.itemsize for s in out_shape)
    cost = pl.CostEstimate(flops=int(flops), bytes_accessed=int(moved), transcendentals=0)
    got = pl.pallas_call(
        body,
        out_shape=out_shape,
        grid_spec=pltpu.PrefetchScalarGridSpec(
            num_scalar_prefetch=extra,
            grid=grid,
            in_specs=in_specs,
            out_specs=out_specs,
            scratch_shapes=list(scratch),
        ),
        compiler_params=pltpu.CompilerParams(vmem_limit_bytes=56 * 2**20),
        cost_estimate=cost,
    )(*(([prefetch] if extra else []) + args))
    return got


def whole_map(*shape):
    zeros = (0,) * len(shape)
    return lambda *_: zeros


def norm_factor(h):
    return lax.rsqrt(jnp.mean(h * h, axis=-1, keepdims=True) + EPS)


class Strips:
    def __init__(self, half, swapped, at, n):
        self.bufs, self.swapped, self.at, self.n = half, swapped, at, n

    def scratch(self):
        return [pltpu.VMEM((2, 2, 2, 4, self.n, 128), bf16), pltpu.SemaphoreType.DMA((2, 2, 2))]

    def start(self, refs, box, sems):
        order = [(core, x, y) for core in range(2) for x in range(2) for y in range(2)]
        for core, x, y in order:
            hi, lo = (x, y) if self.swapped else (y, x)
            src = refs[core * 2 + hi].at[lo]
            if self.n != self.bufs[0].shape[2]:
                src = src.at[:, pl.ds(self.at, self.n)]
            pltpu.make_async_copy(src, box.at[core, hi, lo], sems.at[core, hi, lo]).start()

    def wait(self, box, sems, core, x):
        for y in range(2):
            hi, lo = (x, y) if self.swapped else (y, x)
            there = box.at[core, hi, lo]
            pltpu.make_async_copy(there, there, sems.at[core, hi, lo]).wait()

    def wait_all(self, box, sems):
        for core in range(2):
            for x in range(2):
                self.wait(box, sems, core, x)

    def piece(self, box, z, y, x, core):
        return box.at[core, x, y, z] if self.swapped else box.at[core, y, x, z]


class DownRows:
    def __init__(self, bufs):
        self.bufs = bufs

    def scratch(self):
        return [pltpu.VMEM((2, 4, FFP, 128), bf16), pltpu.SemaphoreType.DMA((2, 4))]

    def start(self, refs, box, sems):
        for z in range(4):
            for core in range(2):
                pltpu.make_async_copy(refs[core].at[z], box.at[core, z], sems.at[core, z]).start()

    def rows(self, box, sems, z, my):
        for core in range(2):
            there = box.at[core, z]
            pltpu.make_async_copy(there, there, sems.at[core, z]).wait()
        halves = []
        for y in range(2):
            parts = []
            for x, core in PLACES:
                for at in down_places(x, y ^ my):
                    parts.append(box[core, z, pl.ds(at, FBP), :])
            halves.append(jnp.concatenate(parts, axis=1))
        return jnp.concatenate(halves, axis=0)


def down_places(x, y):
    return [pl.multiple_of(p * FBP, 16) for p in (y * 2 + x, 4 + x * 2 + y)]


BLOCKS = [(z, y) for z in range(4) for y in range(2)]
PLACES = [(x, core) for x in range(2) for core in range(2)]


def step_place(i):
    return i % 2, i // 2


def step_col(i, me):
    return ((i % 2) * 2 + i // 2) ^ me[1]


def regroup(dst_ref, src_ref, count, me):
    width = D // count
    for j in range(count):
        at = pl.multiple_of((j ^ me) * width, 128)
        dst_ref[:, j * width : (j + 1) * width] = src_ref[:, pl.ds(at, width)]


class Kernel:
    def __init__(self, n_in, strips, n_out):
        self.n_in, self.strips, self.n_out = n_in, strips, n_out

    def split(self, refs):
        ins, refs = refs[: self.n_in], refs[self.n_in :]
        srcs = []
        for s in self.strips:
            srcs.append(refs[: len(s.bufs)])
            refs = refs[len(s.bufs) :]
        outs, refs = refs[: self.n_out], refs[self.n_out :]
        hold = [(s, srcs[j], refs[2 * j], refs[2 * j + 1]) for j, s in enumerate(self.strips)]
        return ins, hold, outs, refs[2 * len(self.strips) :]

    def ins(self):
        return [(b, None, None) for s in self.strips for b in s.bufs]

    def scratch(self):
        return [i for s in self.strips for i in s.scratch()]


def start_all(hold):
    for s, srcs, box, sems in hold:
        s.start(srcs, box, sems)


def col_block(s, box, x, core):
    strips = []
    for j in range(s.n // 128):
        strips.append(jnp.concatenate([s.piece(box, z, y, x, core)[j * 128 : (j + 1) * 128, :] for z, y in BLOCKS], axis=0))
    return strips[0] if len(strips) == 1 else jnp.concatenate(strips, axis=1)


def norm_proj(me, h, gain, strips):
    n = len(strips)
    kern = Kernel(2, strips, n + 1)

    def body(me_ref, *refs):
        (h_ref, gain_ref), hold, (xa_ref, *outs), (xr_ref,) = kern.split(refs)
        i = pl.program_id(0)

        @pl.when(i == 0)
        def _():
            start_all(hold)
            hv = h_ref[...].astype(f32)
            xa_ref[...] = (hv * norm_factor(hv) * gain_ref[...]).astype(bf16)
            regroup(xr_ref, xa_ref, ROWS, me_ref[0])

        x, core = step_place(i)
        for (s, _, box, sems), o_ref in zip(hold, outs):
            s.wait(box, sems, core, x)
            o_ref[...] = dot(xr_ref[...], col_block(s, box, x, core), NN).astype(bf16)

    outs = [((T, D), bf16, (T, D), whole_map(T, D))]
    for s in strips:
        outs.append(((T, s.n * COLS), bf16, (T, s.n), lambda i, me: (0, step_col(i, me))))
    total = sum(s.n * COLS for s in strips)
    return call(
        body, (COLS,), [h, gain.reshape(1, D)] + kern.ins(), outs,
        scratch=kern.scratch() + [pltpu.VMEM((T, D), bf16)], flops=2 * T * D * total, prefetch=me,
    )


def lanes(shape, width):
    return lax.broadcasted_iota(i32, shape, len(shape) - 1) // width


def fill_mask(mask_ref, seg_q, seg_k, live_k, q_axis, window):
    q = lax.broadcasted_iota(i32, (T, T), q_axis)
    k = lax.broadcasted_iota(i32, (T, T), 1 - q_axis)
    ok = (k <= q) & (k > q - window) & (seg_q == seg_k) & ((live_k > 0) | (k == q))
    mask_ref[...] = jnp.where(ok, 1.0, 0.0)


def based_fwd(qk, v, seg_row, seg_col, live_row):
    def body(qk_ref, v_ref, sr_ref, sc_ref, lr_ref, o_ref, ou_ref, rden_ref, mask_ref):
        @pl.when(pl.program_id(0) == 0)
        def _():
            fill_mask(mask_ref, sc_ref[...], sr_ref[...], lr_ref[...], 0, MAX_LEN)

        q4, k4 = qk_ref[:, 0:64], qk_ref[:, 64:128]
        qlane = lanes((T, 64), FEAT)
        first = lanes((HALF, 128), HEAD_DIM) == 0
        scaled = q4.astype(f32) * (FEAT**-0.5)
        for pair in range(2):
            v2 = v_ref[:, pair * 128 : pair * 128 + 128]
            for tb in range(2):
                t0, s1 = tb * HALF, (tb + 1) * HALF
                got = []
                for e in range(2):
                    qm = jnp.where(qlane == pair * 2 + e, scaled, 0.0).astype(bf16)
                    a = dot(qm[t0 : t0 + HALF], k4[0:s1], NT)
                    p = (1.0 + a * (1.0 + 0.5 * a)) * mask_ref[t0 : t0 + HALF, 0:s1]
                    den = jnp.sum(p, axis=-1, keepdims=True)
                    got.append((dot(p.astype(bf16), v2[0:s1], NN), den))
                rden = 1.0 / jnp.where(first, got[0][1], got[1][1])
                ou = jnp.where(first, got[0][0], got[1][0]) * rden
                at = (slice(t0, t0 + HALF), slice(pair * 128, pair * 128 + 128))
                ou_ref[at] = ou
                rden_ref[at] = rden
                o_ref[at] = ou.astype(bf16)

    wide = (T, 256)
    col = lambda c: (0, c)
    return call(
        body,
        (4,),
        [(qk, (T, 128), col), (v, wide, col), seg_row, seg_col, live_row],
        [((T, D), bf16, wide, col), ((T, D), f32, wide, col), ((T, D), f32, wide, col)],
        scratch=[pltpu.VMEM((T, T), f32)],
        flops=HEADS * T * T * 2 * 192,
    )


def based_bwd(qk, v, dou, ou, rden, seg_row, seg_col, live_col):
    def body(qk_ref, v_ref, dou_ref, ou_ref, rden_ref, sr_ref, sc_ref, lc_ref, dqk_ref, dv_ref, mask_ref, dk_ref, dva_ref):
        @pl.when(pl.program_id(0) == 0)
        def _():
            fill_mask(mask_ref, sr_ref[...], sc_ref[...], lc_ref[...], 1, MAX_LEN)

        q4, k4 = qk_ref[:, 0:64], qk_ref[:, 64:128]
        qlane = lanes((T, 64), FEAT)
        q_scaled = q4.astype(f32) * (FEAT**-0.5)
        k_scaled = k4.astype(f32) * (FEAT**-0.5)
        vlane = lanes((T, 128), HEAD_DIM)
        dnum_f = dou_ref[...] * rden_ref[...]
        term = dnum_f * ou_ref[...]
        high = term.astype(bf16)
        low = (term - high.astype(f32)).astype(bf16)
        pick = jnp.where(
            lax.broadcasted_iota(i32, (8, 256), 0) == lanes((8, 256), HEAD_DIM), 1.0, 0.0
        ).astype(bf16)
        dden = -(dot(pick, high, NT) + dot(pick, low, NT))
        dk_ref[...] = jnp.zeros((T, 64), f32)
        dva_ref[...] = jnp.zeros((T, 256), f32)
        dq = [jnp.zeros((HALF, 64), f32), jnp.zeros((HALF, 64), f32)]
        for pair in range(2):
            cols = slice(pair * 128, pair * 128 + 128)
            v2 = v_ref[:, cols]
            for e in range(2):
                head = pair * 2 + e
                qm = jnp.where(qlane == head, q_scaled, 0.0).astype(bf16)
                km = jnp.where(qlane == head, k_scaled, 0.0).astype(bf16)
                dn = jnp.where(vlane == e, dnum_f[:, cols], 0.0).astype(bf16)
                for tb in range(2):
                    t0, s1 = tb * HALF, (tb + 1) * HALF
                    at = slice(t0, t0 + HALF)
                    a = dot(k4[0:s1], qm[at], NT)
                    m = mask_ref[0:s1, at]
                    p = (1.0 + a * (1.0 + 0.5 * a)) * m
                    dp = dot(v2[0:s1], dn[at], NT) + dden[head : head + 1, at]
                    da = (dp * m * (1.0 + a)).astype(bf16)
                    dk_ref[0:s1, :] += dot(da, qm[at], NN)
                    dva_ref[0:s1, cols] += dot(p.astype(bf16), dn[at], NN)
                    dq[tb] += dot(da, km[0:s1], TN)
        for tb in range(2):
            at = slice(tb * HALF, tb * HALF + HALF)
            dqk_ref[at, 0:64] = dq[tb].astype(bf16)
        dqk_ref[:, 64:128] = dk_ref[...].astype(bf16)
        dv_ref[...] = dva_ref[...].astype(bf16)

    wide = (T, 256)
    col = lambda c: (0, c)
    return call(
        body,
        (4,),
        [(qk, (T, 128), col), (v, wide, col), (dou, wide, col), (ou, wide, col), (rden, wide, col), seg_row, seg_col, live_col],
        [((T, 512), bf16, (T, 128), col), ((T, D), bf16, wide, col)],
        scratch=[pltpu.VMEM((T, T), f32), pltpu.VMEM((T, 64), f32), pltpu.VMEM((T, 256), f32)],
        flops=HEADS * T * T * 2 * 480,
    )


SPAN = ((0, HALF), (HALF - WINDOW, T))


def window_fwd(q, k, v, seg_row, seg_col, live_col):
    def body(q_ref, k_ref, v_ref, sr_ref, sc_ref, lc_ref, o_ref, mask_ref):
        @pl.when(pl.program_id(0) == 0)
        def _():
            fill_mask(mask_ref, sr_ref[...], sc_ref[...], lc_ref[...], 1, WINDOW)

        first = lanes((HALF, 128), HEAD_DIM) == 0
        qlane = lanes((T, 128), HEAD_DIM)
        scaled = q_ref[...].astype(f32) * (HEAD_DIM**-0.5)
        for tb in range(2):
            at = slice(tb * HALF, tb * HALF + HALF)
            s0, s1 = SPAN[tb]
            ok = mask_ref[s0:s1, at] > 0.5
            got = []
            for e in range(2):
                qm = jnp.where(qlane == e, scaled, 0.0).astype(bf16)
                c = dot(k_ref[s0:s1, :], qm[at], NT)
                c = jnp.where(ok, c, NEG)
                w = jnp.exp(c - jnp.max(c, axis=0, keepdims=True))
                w = w * (1.0 / jnp.sum(w, axis=0, keepdims=True))
                got.append(dot(w.astype(bf16), v_ref[s0:s1, :], TN))
            o_ref[at, :] = jnp.where(first, got[0], got[1]).astype(bf16)

    blk = (T, 128)
    col = lambda c: (0, c)
    return call(
        body,
        (8,),
        [(q, blk, col), (k, blk, col), (v, blk, col), seg_row, seg_col, live_col],
        [((T, D), bf16, blk, col)],
        scratch=[pltpu.VMEM((T, T), f32)],
        flops=HEADS * T * T * 2 * 192,
    )[0]


def window_bwd(q, k, v, dor, seg_row, seg_col, live_col):
    def body(q_ref, k_ref, v_ref, do_ref, sr_ref, sc_ref, lc_ref, dq_ref, dk_ref, dv_ref, mask_ref, dka_ref, dva_ref):
        @pl.when(pl.program_id(0) == 0)
        def _():
            fill_mask(mask_ref, sr_ref[...], sc_ref[...], lc_ref[...], 1, WINDOW)

        lane = lanes((T, 128), HEAD_DIM)
        q_scaled = q_ref[...].astype(f32) * (HEAD_DIM**-0.5)
        k_scaled = k_ref[...].astype(f32) * (HEAD_DIM**-0.5)
        do = do_ref[...]
        dka_ref[...] = jnp.zeros((T, 128), f32)
        dva_ref[...] = jnp.zeros((T, 128), f32)
        for tb in range(2):
            at = slice(tb * HALF, tb * HALF + HALF)
            s0, s1 = SPAN[tb]
            ok = mask_ref[s0:s1, at] > 0.5
            dq = jnp.zeros((HALF, 128), f32)
            for e in range(2):
                qm = jnp.where(lane == e, q_scaled, 0.0).astype(bf16)
                km = jnp.where(lane == e, k_scaled, 0.0).astype(bf16)
                dm = jnp.where(lane == e, do, jnp.zeros_like(do))
                c = dot(k_ref[s0:s1, :], qm[at], NT)
                c = jnp.where(ok, c, NEG)
                w = jnp.exp(c - jnp.max(c, axis=0, keepdims=True))
                w = w * (1.0 / jnp.sum(w, axis=0, keepdims=True))
                dw = dot(v_ref[s0:s1, :], dm[at], NT)
                ds = (w * (dw - jnp.sum(w * dw, axis=0, keepdims=True))).astype(bf16)
                dka_ref[s0:s1, :] += dot(ds, qm[at], NN)
                dva_ref[s0:s1, :] += dot(w.astype(bf16), dm[at], NN)
                dq += dot(ds, km[s0:s1], TN)
            dq_ref[at, :] = dq.astype(bf16)
        dk_ref[...] = dka_ref[...].astype(bf16)
        dv_ref[...] = dva_ref[...].astype(bf16)

    blk = (T, 128)
    col = lambda c: (0, c)
    return call(
        body,
        (8,),
        [(q, blk, col), (k, blk, col), (v, blk, col), (dor, blk, col), seg_row, seg_col, live_col],
        [((T, D), bf16, blk, col)] * 3,
        scratch=[pltpu.VMEM((T, T), f32), pltpu.VMEM((T, 128), f32), pltpu.VMEM((T, 128), f32)],
        flops=HEADS * T * T * 2 * 480,
    )


def attn_out(me, h, o, strip, gain):
    kern = Kernel(3, [strip], 2)

    def body(me_ref, *refs):
        (h_ref, o_ref, gain_ref), hold, (hm_ref, xf_ref), (or_ref,) = kern.split(refs)
        i = pl.program_id(0)

        @pl.when(i == 0)
        def _():
            start_all(hold)
            regroup(or_ref, o_ref, ROWS, me_ref[0])

        x, core = step_place(i)
        s, _, box, sems = hold[0]
        s.wait(box, sems, core, x)
        at = pl.ds(pl.multiple_of(step_col(i, me_ref) * 256, 256), 256)
        hm_ref[:, at] = h_ref[:, at].astype(f32) + dot(or_ref[...], col_block(s, box, x, core), NN)

        @pl.when(i == COLS - 1)
        def _():
            hm = hm_ref[...]
            xf_ref[...] = (hm * norm_factor(hm) * gain_ref[...]).astype(bf16)

    full = whole_map(T, D)
    return call(
        body, (COLS,), [h, o, gain.reshape(1, D)] + kern.ins(),
        [((T, D), f32, (T, D), full), ((T, D), bf16, (T, D), full)],
        scratch=kern.scratch() + [pltpu.VMEM((T, D), bf16)], flops=2 * T * D * D, prefetch=me,
    )


def hidden_block(s, box, x, core):
    return jnp.concatenate([s.piece(box, z, y, x, core)[...] for z, y in BLOCKS], axis=1)


def gate_up(me, xf, w_gate, w_up):
    kern = Kernel(1, [w_gate, w_up], 3)

    def body(me_ref, *refs):
        (xf_ref,), hold, (g_ref, u_ref, hid_ref), (xr_ref,) = kern.split(refs)
        i = pl.program_id(0)

        @pl.when(i == 0)
        def _():
            start_all(hold)
            regroup(xr_ref, xf_ref, ROWS, me_ref[0])

        x, core = step_place(i)
        got = []
        for s, _, box, sems in hold:
            s.wait(box, sems, core, x)
            got.append(dot(hidden_block(s, box, x, core), xr_ref[...], NT))
        g, u = got
        g_ref[...] = g.astype(bf16)
        u_ref[...] = u.astype(bf16)
        hid_ref[...] = (g * (1.0 / (1.0 + jnp.exp(-g))) * u).astype(bf16)

    row = lambda i, me: (step_col(i, me), 0)
    return call(
        body, (COLS,), [xf] + kern.ins(), [((FFP, T), bf16, (FC, T), row)] * 3,
        scratch=kern.scratch() + [pltpu.VMEM((T, D), bf16)], flops=4 * T * D * FFP, prefetch=me,
    )


def down(me, hm, hid, w_down):
    kern = Kernel(2, [w_down], 1)

    def body(me_ref, *refs):
        (hm_ref, hid_ref), hold, (h_ref,), (acc_ref,) = kern.split(refs)
        i = pl.program_id(0)

        @pl.when(i == 0)
        def _():
            start_all(hold)
            regroup(acc_ref, hm_ref, COLS, me_ref[1])

        s, _, box, sems = hold[0]
        acc_ref[...] += dot(hid_ref[...], s.rows(box, sems, i, me_ref[0]), TN)

        @pl.when(i == COLS - 1)
        def _():
            regroup(h_ref, acc_ref, COLS, me_ref[1])

    return call(
        body, (COLS,), [hm, (hid, (FC, T), lambda i, me: (i, 0))] + kern.ins(),
        [((T, D), f32, (T, D), whole_map(T, D))],
        scratch=kern.scratch() + [pltpu.VMEM((T, D), f32)], flops=2 * T * D * FFP, prefetch=me,
    )[0]


def down_bwd(me, bd, w_down, hid, g, u):
    kern = Kernel(4, [w_down], 4)

    def body(me_ref, *refs):
        (bd_ref, hid_ref, g_ref, u_ref), hold, (dg_ref, du_ref, *p_refs), (br_ref,) = kern.split(refs)
        i = pl.program_id(0)

        @pl.when(i == 0)
        def _():
            start_all(hold)
            regroup(br_ref, bd_ref, COLS, me_ref[1])

        bdv = br_ref[...].astype(bf16)
        gwd = dot(hid_ref[...], bdv, NN).astype(bf16)
        for x, core in PLACES:
            at = (x * 2 + core) * 256
            for y in range(2):
                rows = slice(y * FBP, (y + 1) * FBP)
                for half, to in enumerate(down_places(x, y ^ me_ref[0])):
                    p_refs[core][0, pl.ds(to, FBP), :] = gwd[rows, at + half * 128 : at + half * 128 + 128]
        s, _, box, sems = hold[0]
        dhid = dot(s.rows(box, sems, i, me_ref[0]), bdv, NT)
        gv, uv = g_ref[...].astype(f32), u_ref[...].astype(f32)
        sig = 1.0 / (1.0 + jnp.exp(-gv))
        act = gv * sig
        du_ref[...] = (dhid * act).astype(bf16)
        dg_ref[...] = (dhid * uv * (sig + act * (1.0 - sig))).astype(bf16)

    row = lambda i, me: (i, 0)
    hblk = (FC, T)
    pieces = ((4, FFP, 128), bf16, (1, FFP, 128), lambda i, me: (i, 0, 0))
    return call(
        body, (COLS,), [bd, (hid, hblk, row), (g, hblk, row), (u, hblk, row)] + kern.ins(),
        [((FFP, T), bf16, hblk, row), ((FFP, T), bf16, hblk, row)] + [pieces] * 2,
        scratch=kern.scratch() + [pltpu.VMEM((T, D), bd.dtype)], flops=4 * T * D * FFP, prefetch=me,
    )


def piece_specs(n1, n2):
    out = []
    for n, block, place in ((n1, (1, 2, 4), lambda j: (j, 0)), (n2, (2, 1, 4), lambda j: (0, j))):
        for step in (lambda i: jnp.minimum(i, 1), lambda i: jnp.maximum(i - 2, 0)):
            index = functools.partial(lambda place, step, i, me: (*place(step(i)), 0, 0, 0), place, step)
            out.append(((2, 2, 4, n, 128), bf16, (*block, n, 128), index))
    return out


def for_core(refs, write):
    for core in range(2):

        @pl.when(pl.program_id(0) // 2 == core)
        def _():
            write(refs[core], refs[2 + core])


def gate_up_bwd(me, xf, dg, du):
    def body(me_ref, xf_ref, dg_ref, du_ref, *refs):
        *p_refs, xr_ref = refs

        @pl.when(pl.program_id(0) == 0)
        def _():
            regroup(xr_ref, xf_ref, ROWS, me_ref[0])

        gwg = dot(dg_ref[...], xr_ref[...], NN).astype(bf16)
        gwu = dot(du_ref[...], xr_ref[...], NN).astype(bf16)

        def write(one, two):
            for r, (z, y) in enumerate(BLOCKS):
                one[0, y, z] = gwg[:, r * 128 : (r + 1) * 128]
                two[y, 0, z] = gwu[:, r * 128 : (r + 1) * 128]

        for_core(p_refs, write)

    row = lambda i, me: (step_col(i, me), 0)
    return call(
        body, (COLS,), [xf, (dg, (FC, T), row), (du, (FC, T), row)], piece_specs(FC, FC),
        scratch=[pltpu.VMEM((T, D), bf16)], flops=4 * T * D * FFP, prefetch=me,
    )


def norm_bwd(dx, h, gain, g):
    rf = norm_factor(h)
    hr = h * rf
    dgain = jnp.sum(dx * hr, axis=0, keepdims=True)
    gd = gain * dx
    mean = jnp.sum(gd * hr, axis=-1, keepdims=True) * (1.0 / D)
    return dgain, g + rf * (gd - hr * mean)


def add_to(acc_ref, part):
    @pl.when(pl.program_id(0) == 0)
    def _():
        acc_ref[...] = part

    @pl.when(pl.program_id(0) > 0)
    def _():
        acc_ref[...] += part


def mlp_dx(me, dg, du, w_gate, w_up, hm, gain, g, w_out, kind):
    kern = Kernel(5, [w_gate, w_up, w_out], 4)

    def body(me_ref, *refs):
        (dg_ref, du_ref, hm_ref, gain_ref, g_ref), hold, outs, (acc_ref, un_ref, br_ref) = kern.split(refs)
        gm_ref, bo_ref, dou_ref, gg_ref = outs
        i = pl.program_id(0)

        @pl.when(i == 0)
        def _():
            start_all(hold)

        x, core = step_place(i)
        part = None
        for (s, _, box, sems), d_ref in zip(hold[:2], (dg_ref, du_ref)):
            s.wait(box, sems, core, x)
            term = dot(d_ref[...], hidden_block(s, box, x, core), TN)
            part = term if part is None else part + term
        add_to(acc_ref, part)

        @pl.when(i == COLS - 1)
        def _():
            regroup(un_ref, acc_ref, ROWS, me_ref[0])
            gg, gm = norm_bwd(un_ref[...], hm_ref[...], gain_ref[...], g_ref[...].astype(f32))
            gg_ref[...] = gg
            gm_ref[...] = gm
            bo_ref[...] = gm.astype(bf16)
            regroup(br_ref, bo_ref, COLS, me_ref[1])
            s, _, box, sems = hold[2]
            s.wait_all(box, sems)
            w = jnp.concatenate([col_block(s, box, x, core) for x, core in PLACES], axis=1)
            acc_ref[...] = dot(br_ref[...], w, NT)
            regroup(un_ref, acc_ref, ROWS, me_ref[0])
            dou_ref[...] = un_ref[...].astype(kind)

    row = lambda i, me: (step_col(i, me), 0)
    full = whole_map(T, D)
    return call(
        body, (COLS,), [(dg, (FC, T), row), (du, (FC, T), row), hm, gain.reshape(1, D), g] + kern.ins(),
        [((T, D), f32, (T, D), full), ((T, D), bf16, (T, D), full), ((T, D), kind, (T, D), full), ((1, D), f32, (1, D), full)],
        scratch=kern.scratch() + [pltpu.VMEM((T, D), f32), pltpu.VMEM((T, D), f32), pltpu.VMEM((T, D), bf16)],
        flops=4 * T * D * FFP + 2 * T * D * D, prefetch=me,
    )


def attn_bwd(me, xa, grads, strips, o, bo, h, gain, gm, halves):
    n = len(grads)
    kern = Kernel(6 + n, strips, 6)

    def body(me_ref, *refs):
        ins, hold, (*p_refs, g_ref, gg_ref), (xr_ref, or_ref, acc_ref) = kern.split(refs)
        xa_ref, o_ref, h_ref, gain_ref, gm_ref, bo_ref, *d_refs = ins
        i = pl.program_id(0)

        @pl.when(i == 0)
        def _():
            start_all(hold)
            regroup(xr_ref, xa_ref, ROWS, me_ref[0])
            regroup(or_ref, o_ref, ROWS, me_ref[0])

        tiles = [dot(xr_ref[...], d[...], TN).astype(bf16) for d in d_refs]
        tiles.append(dot(or_ref[...], bo_ref[...], TN).astype(bf16))

        def write(one, two):
            for j, (which, at) in enumerate(halves[0]):
                for r, (z, y) in enumerate(BLOCKS):
                    one[0, y, z, j * 128 : (j + 1) * 128] = tiles[which][r * 128 : (r + 1) * 128, at : at + 128]
            for j, (which, at) in enumerate(halves[1]):
                for r, (z, y) in enumerate(BLOCKS):
                    two[y, 0, z, j * 128 : (j + 1) * 128] = tiles[which][r * 128 : (r + 1) * 128, at : at + 128]

        for_core(p_refs, write)
        x, core = step_place(i)
        part = None
        for (s, _, box, sems), d in zip(hold, d_refs):
            s.wait(box, sems, core, x)
            term = dot(d[...], col_block(s, box, x, core), NT)
            part = term if part is None else part + term
        add_to(acc_ref, part)

        @pl.when(i == COLS - 1)
        def _():
            regroup(g_ref, acc_ref, ROWS, me_ref[0])
            gg, g = norm_bwd(g_ref[...], h_ref[...].astype(f32), gain_ref[...], gm_ref[...])
            gg_ref[...] = gg
            g_ref[...] = g

    col = lambda i, me: (0, step_col(i, me))
    full = whole_map(T, D)
    ins = [xa, o, h, gain.reshape(1, D), gm, (bo, (T, 256), col)]
    ins += [(d, (T, d.shape[1] // COLS), col) for d in grads]
    total = sum(d.shape[1] for d in grads)
    return call(
        body, (COLS,), ins + kern.ins(),
        piece_specs(128 * len(halves[0]), 128 * len(halves[1])) + [((T, D), f32, (T, D), full), ((1, D), f32, (1, D), full)],
        scratch=kern.scratch() + [pltpu.VMEM((T, D), bf16), pltpu.VMEM((T, D), bf16), pltpu.VMEM((T, D), f32)],
        flops=4 * T * D * total + 2 * T * D * D, prefetch=me,
    )


HALVES_ONE = (((1, 0), (1, 128)), ((0, 0), (2, 0), (2, 128)))
HALVES_TWO = (((0, 0), (0, 128), (1, 0), (1, 128)), ((2, 0), (2, 128), (3, 0), (3, 128)))


def attn_weights(bufs, halves):
    out = []
    for which in range(1 + max(w for half in halves for w, _ in half)):
        for k, half in enumerate(halves):
            at = [j for j, (w, _) in enumerate(half) if w == which]
            if at:
                out.append(Strips(bufs[k], k == 1, at[0] * 128, len(at) * 128))
    return out


def gate_weights(bufs):
    return Strips(bufs[0], False, 0, FC), Strips(bufs[1], True, 0, FC)


def pad_hidden(w):
    k = w.shape[0]
    return jnp.pad(w.reshape(k, -1, FB), ((0, 0), (0, 0), (0, FBP - FB))).reshape(k, -1).T


def pad_rows(w):
    n = w.shape[1]
    return jnp.pad(w.reshape(-1, FB, n), ((0, 0), (0, FBP - FB), (0, 0))).reshape(-1, n)


def strips_of(blocks, halves):
    return tuple(
        jnp.concatenate([blocks[which][..., at : at + 128] for which, at in strips], axis=-2) for strips in halves
    )


def after(value, *arrays):
    return lax.optimization_barrier((value, *arrays))[0] if arrays else value


def sync(*groups):
    flat, tree = jax.tree.flatten(groups)
    return jax.tree.unflatten(tree, lax.optimization_barrier(flat))


def add_core(four, got):
    keep = [four[0][0] + got[0][0], four[2][0] + got[1][0]]
    return keep, [four[0][1] + got[0][1], four[2][1] + got[1][1]]


def add_two(keep, got):
    return [k[0] + g[0] for k, g in zip(keep, got)], [k[1] + g[1] for k, g in zip(keep, got)]


def add_one(keep, got):
    return [k + g for k, g in zip(keep, got)]


def far_rows(total):
    parts = jnp.split(total, 4, axis=0)
    return parts[0::2], parts[1::2]


def near_rows(halves):
    parts = [jnp.split(h, 2, axis=0) for h in halves]
    return [p[0] for p in parts], [p[1] for p in parts]


class Ring:
    def __init__(self, names):
        self.axes = names
        self.z = lax.axis_index(names[0])

    def swap(self, value, axis, by=1):
        shift = {"z": 3, "y": 2, "x": 1, "core": 0}[axis]
        return lax.ppermute(value, self.axes, [(i, i ^ (by << shift)) for i in range(32)])

    def gather_z(self, both, *behind):
        near = [both] + [after(self.swap(both, "z", by), *behind) for by in (1, 2, 3)]
        low, high = self.z % 2 == 1, self.z >= 2
        a, b = jnp.where(low, near[1], near[0]), jnp.where(low, near[0], near[1])
        c, d = jnp.where(low, near[3], near[2]), jnp.where(low, near[2], near[3])
        pick = lambda p, q: jnp.where(high, q, p)
        return jnp.stack([pick(a, c), pick(b, d), pick(c, a), pick(d, b)])

    def gather_z_all(self, both):
        return lax.all_gather(both, self.axes[0], axis=0, tiled=False)

    def gather_lo(self, pair, *behind):
        got = [after(self.swap(v, axis), *behind) for v, axis in zip(pair, ("x", "y"))]
        return [jnp.stack([v, g]) for v, g in zip(pair, got)]

    def gather_hi(self, pair, *behind):
        return [[v, after(self.swap(v, axis), *behind)] for v, axis in zip(pair, ("y", "x"))]

    def gather_core(self, full, *behind):
        return [half + [after(self.swap(b, "core"), *behind) for b in half] for half in full]

    def gather_down(self, pair):
        return jnp.stack([jnp.stack(half) for half in self.gather_hi(self.gather_lo(pair))]).reshape(-1, 128)

    def scatter_z(self, value):
        return lax.psum_scatter(value, self.axes[0], scatter_dimension=0, tiled=False)

    def send(self, values, axes):
        return [self.swap(v, axis) for v, axis in zip(values, axes)]

    def reduce_z(self, pair, *behind):
        n1 = pair[0].shape[1]
        both = jnp.concatenate(pair, axis=1)
        here = lambda by: lax.dynamic_index_in_dim(both, self.z ^ by, 0, False)
        total = here(0).astype(f32)
        for by in (1, 2, 3):
            total = total + after(self.swap(here(by), "z", by), *behind).astype(f32)
        return total[:n1], total[n1:]

    def reduce_z_all(self, pair):
        n1 = pair[0].shape[1]
        both = jnp.concatenate(pair, axis=1)
        total = lax.psum_scatter(both, self.axes[0], scatter_dimension=0, tiled=False).astype(f32)
        return total[:n1], total[n1:]


def pack(shards, halves):
    *attn, gate, up, dn = shards
    dp = pad_rows(dn)
    return [strips_of(attn, halves), (pad_hidden(gate), pad_hidden(up)), (dp[:, :128], dp[:, 128:])]


def boxes_any(weights, halves):
    *attn, gate, up, dn = weights

    def cut(w, rows, cols):
        return w.reshape(4, 2, rows, 2, 2, cols).transpose(0, 1, 3, 4, 2, 5)

    def boxes(one, two):
        first = [one[:, y, :, core].transpose(1, 0, 2, 3) for core in range(2) for y in range(2)]
        second = [two[:, :, x, core].transpose(1, 0, 2, 3) for core in range(2) for x in range(2)]
        return first, second

    a = boxes(*strips_of([cut(w, D // ROWS, w.shape[1] // COLS) for w in attn], halves))
    hidden = lambda w: pad_hidden(w).reshape(2, 2, FC, 4, 2, 128).transpose(3, 4, 0, 1, 2, 5)
    d = cut(pad_rows(dn), FBP, 256)
    one = d[..., :128].transpose(3, 0, 1, 2, 4, 5)
    two = d[..., 128:].transpose(3, 0, 2, 1, 4, 5)
    d = jnp.stack([one, two], axis=2).reshape(2, 4, FFP, 128)
    return [a, boxes(hidden(gate), hidden(up)), [d[0], d[1]]]


def unpad_hidden(g):
    k = g.shape[1]
    return g.reshape(-1, FBP, k)[:, :FB].reshape(-1, k).T


def unpad_rows(g):
    n = g.shape[1]
    return g.reshape(-1, FBP, n)[:, :FB].reshape(-1, n)


def whole_grad(own, send, swapped):
    p = jnp.stack([own, send])
    if swapped:
        p = jnp.swapaxes(p, 1, 2)
    core, x, y, z, n, w = p.shape
    return p.transpose(3, 2, 1, 0, 4, 5).reshape(z * y, x * core, n, w)


def join_strips(one, two, halves):
    out = []
    for which in range(1 + max(w for half in halves for w, _ in half)):
        got = {}
        for src, strips in ((one, halves[0]), (two, halves[1])):
            for j, (w, at) in enumerate(strips):
                if w == which:
                    got[at] = src[..., j * 128 : j * 128 + 128, :]
        out.append(jnp.concatenate([got[a] for a in sorted(got)], axis=-1))
    return out


def sum_parts(a, gu, d, halves):
    return join_strips(*a, halves) + [unpad_hidden(gu[0]), unpad_hidden(gu[1]), unpad_rows(jnp.concatenate(d, axis=1))]


def scatter_any(w):
    part = lax.psum_scatter(w, "row", scatter_dimension=0, tiled=True)
    return lax.psum_scatter(part, "col", scatter_dimension=1, tiled=True).astype(f32)


def natural(blocks):
    r, c, n, w = blocks.shape
    return blocks.transpose(0, 2, 1, 3).reshape(r * n, c * w)


def sum_any(pd, pgu, pa, halves):
    pairs = lambda p: (whole_grad(*p[:2], False), whole_grad(*p[2:], True))
    one, two = jnp.split(jnp.stack(pd).reshape(2, 4, 2, 2, 2, FBP, 128), 2, axis=2)
    dn = jnp.concatenate([one[:, :, 0], jnp.swapaxes(two[:, :, 0], 2, 3)], axis=-1)
    dn = dn.transpose(1, 2, 3, 0, 4, 5).reshape(ROWS, COLS, FBP, 256)
    dn = scatter_any(unpad_rows(natural(dn)))
    gu = [scatter_any(unpad_hidden(g.transpose(1, 2, 0, 3).reshape(FFP, D))) for g in pairs(pgu)]
    blocks = join_strips(*pairs(pa), halves)
    if len(blocks) == 3:
        blocks = [blocks[0][..., :64], blocks[0][..., 64:]] + blocks[1:]
    return [scatter_any(natural(b)) for b in blocks] + gu + [dn]


def join_qk(q, k, parts):
    n = q.shape[0]
    both = jnp.concatenate([q.reshape(n, parts, -1), k.reshape(n, parts, -1)], axis=2)
    return both.reshape(n, -1)

def route_plan(dest_slot, block_tokens, rows, cols):
    row_count = lax.axis_size(rows)
    col_count = lax.axis_size(cols)
    per_peer = block_tokens // row_count
    row_at = lax.axis_index(rows)
    col_at = lax.axis_index(cols)
    slot_table = dest_slot.reshape(row_count, col_count, block_tokens)
    column = lax.dynamic_index_in_dim(slot_table, col_at, 1, False)
    own_slots = lax.dynamic_index_in_dim(column, row_at, 0, False)
    send_order = jnp.argsort(own_slots)
    arrived = jnp.sort(column, axis=1)
    incoming = lax.dynamic_slice_in_dim(arrived, row_at * per_peer, per_peer, 1)
    local_slots = incoming.reshape(-1) - (row_at * col_count + col_at) * block_tokens
    placing = jnp.argsort(local_slots)
    return (send_order, local_slots, placing)


def exchange(value, axis):
    n, width = value.shape
    row_count = lax.axis_size(axis)
    got = lax.all_to_all(value.reshape(row_count, n // row_count, width), axis, split_axis=0, concat_axis=0, tiled=True)
    return got.reshape(n, width)


def gather_all(shards):
    return [lax.all_gather(lax.all_gather(w, "col", axis=1, tiled=True), "row", axis=0, tiled=True) for w in shards]


def body(names, tokens, cotangent, dest_slot, lengths, pad_mask, *params):
    ring = Ring(names) if len(names) == 4 else None
    rows, cols = (names[:2], names[2:]) if ring else names
    gain_a1, bq, bk, bv, bo_w, gain_m1, wg1, wu1, wd1 = params[:9]
    gain_a2, wq, wk, wv, wo2, gain_m2, wg2, wu2, wd2 = params[9:]
    shards1, shards2 = [bq, bk, bv, bo_w, wg1, wu1, wd1], [wq, wk, wv, wo2, wg2, wu2, wd2]
    send_order, local_slots, placing = route_plan(dest_slot, T, rows, cols)
    restore = jnp.argsort(send_order)
    outgoing = after(tokens[send_order], restore) if ring else tokens[send_order]
    cot_going = cotangent[send_order]
    if ring:
        me = jnp.stack([lax.axis_index(names[1]), lax.axis_index(cols)]).astype(i32)
        packs = pack([join_qk(bq, bk, 1)] + shards1[2:], HALVES_ONE) + pack(shards2, HALVES_TWO)
        flat = [jnp.concatenate(p, axis=0) for p in packs]
        mid_d2 = ring.gather_down(packs[5])
        split = lambda k, v: [v[:, : packs[k][0].shape[0]], v[:, packs[k][0].shape[0] :]]
        each = lambda pair, *arrays: [after(v, *arrays) for v in pair]
        far = lambda halves: [half[1] for half in halves]
        near_a1 = ring.gather_z(flat[0])
        hi_a1 = ring.gather_hi(ring.gather_lo(each(split(0, near_a1), mid_d2)))
        near_gu1 = ring.gather_z(after(flat[1], near_a1))
        lo_gu1 = ring.gather_lo(each(split(1, near_gu1), *far(hi_a1)))
        outgoing = after(outgoing, near_gu1, *far(hi_a1))
        arrived = exchange(outgoing, rows)
        near_d1 = ring.gather_z(after(flat[2], arrived))
        start = arrived[placing]
    else:
        me = jnp.zeros((2,), i32)
        one, two = gather_all(shards1), gather_all(shards2)
        full = boxes_any([join_qk(one[0], one[1], COLS)] + one[2:], HALVES_ONE) + boxes_any(two, HALVES_TWO)
        start = exchange(outgoing, rows)[placing]
    position = jnp.arange(T, dtype=i32)
    segment, end = jnp.zeros((T,), i32), jnp.zeros((), i32)
    for j in range(lengths.shape[1]):
        end = end + lengths[0, j]
        segment = segment + (position >= end).astype(i32)
    seg_row, seg_col = segment.reshape(1, T), segment.reshape(T, 1)
    live_row, live_col = pad_mask.reshape(1, T), pad_mask.reshape(T, 1)

    tied = after if ring else (lambda value, *arrays: value)
    if ring:
        full_a1 = ring.gather_core(hi_a1)
        start = after(start, *lo_gu1)
    else:
        full_a1 = full[0]
    w_qk, w_v, w_o = attn_weights(full_a1, HALVES_ONE)
    xa1, qk1, v1 = norm_proj(me, start, gain_a1, [w_qk, w_v])
    o1, ou1, rden1 = based_fwd(qk1, v1, seg_row, seg_col, live_row)
    if ring:
        hi_gu1 = ring.gather_hi(lo_gu1, o1)
        near_a2 = ring.gather_z(after(flat[3], near_d1), o1)
    hm1, xf1 = attn_out(me, start, tied(o1, *(far(hi_gu1) + [near_a2] if ring else [])), w_o, gain_m1)
    if ring:
        full_gu1 = ring.gather_core(hi_gu1, xf1)
        lo_d1 = ring.gather_lo(each(split(2, near_d1), *far(hi_gu1)), xf1)
        xf1_late = after(xf1, *lo_d1)
    else:
        full_gu1, xf1_late = full[1], xf1
    w_g, w_u = gate_weights(full_gu1)
    g1, u1, hid1 = gate_up(me, xf1_late, w_g, w_u)
    if ring:
        hi_d1 = ring.gather_hi(lo_d1, hid1)
        lo_a2 = ring.gather_lo(each(split(3, near_a2), *lo_d1), hid1)
        near_gu2 = ring.gather_z(after(flat[4], near_a2), hid1)
        own_d1 = jnp.stack([jnp.stack(half) for half in hi_d1]).transpose(3, 0, 1, 2, 4, 5).reshape(4, FFP, 128)
        full_d1 = [own_d1, ring.swap(own_d1, "core")]
        hid1_late = after(hid1, *lo_a2)
        all_d2 = ring.gather_z_all(after(mid_d2, near_gu2))
        cot_going = after(cot_going, near_gu2)
    else:
        full_d1, hid1_late = full[2], hid1
    cot = exchange(cot_going, rows)[placing]
    w_d = DownRows(full_d1)
    h1 = down(me, hm1, hid1_late, w_d)
    if ring:
        hi_a2 = ring.gather_hi(lo_a2, h1)
        full_a2 = ring.gather_core(hi_a2)
        lo_gu2 = each(split(4, near_gu2), *far(hi_a2))
    else:
        full_a2 = full[3]
    v_q, v_k, v_v, v_o = attn_weights(full_a2, HALVES_TWO)
    xa2, q2, k2, v2 = norm_proj(me, h1, gain_a2, [v_q, v_k, v_v])
    if ring:
        lo_gu2 = ring.gather_lo(lo_gu2, q2)
    o2 = window_fwd(tied(q2, *(lo_gu2 if ring else [])), k2, v2, seg_row, seg_col, live_col)
    hm2, xf2 = attn_out(me, h1, o2, v_o, gain_m2)
    if ring:
        full_gu2 = ring.gather_core(ring.gather_hi(lo_gu2, xf2))
    else:
        full_gu2 = full[4]
    v_g, v_u = gate_weights(full_gu2)
    v_d = DownRows([all_d2, after(ring.swap(all_d2, "core"), xf2)] if ring else full[5])
    g2, u2, hid2 = gate_up(me, xf2, v_g, v_u)

    dg2, du2, *d2 = down_bwd(me, cot, v_d, hid2, g2, u2)
    if ring:
        r_d2 = ring.send(d2[1:], ("core",))
    gu2 = gate_up_bwd(me, xf2, dg2, du2)
    if ring:
        dg2, du2, gu2, r_d2 = sync(dg2, du2, gu2, r_d2)
        z_d2 = ring.scatter_z(d2[0] + r_d2[0])
        r_gu2 = ring.send(gu2[1::2], ("core", "core"))
    gm2, bo2, dor2, gg_m2 = mlp_dx(me, dg2, du2, v_g, v_u, hm2, gain_m2, cot, v_o, bf16)
    if ring:
        gm2, bo2, dor2, gg_m2, r_gu2 = sync(gm2, bo2, dor2, gg_m2, r_gu2)
        keep_gu2, go = add_core(gu2, r_gu2)
        r_gu2 = ring.send(go, ("x", "y"))
    dq2, dk2, dv2 = window_bwd(q2, k2, v2, dor2, seg_row, seg_col, live_col)
    *a2, gh1, gg_a2 = attn_bwd(me, xa2, [dq2, dk2, dv2], [v_q, v_k, v_v], o2, bo2, h1, gain_a2, gm2, HALVES_TWO)
    if ring:
        a2, gh1, gg_a2, r_gu2, z_d2 = sync(a2, gh1, gg_a2, r_gu2, z_d2)
        keep_gu2, go = add_two(keep_gu2, r_gu2)
        r_gu2 = ring.send(go, ("y", "x"))
        r_a2 = ring.send(a2[1::2], ("core", "core"))
        keep_d2, go = far_rows(z_d2)
        r_d2 = ring.send(go, ("y", "x"))
    dg1, du1, *d1 = down_bwd(me, gh1, w_d, hid1, g1, u1)
    if ring:
        dg1, du1, d1, r_gu2, r_a2, r_d2 = sync(dg1, du1, d1, r_gu2, r_a2, r_d2)
        z_gu2 = ring.scatter_z(jnp.concatenate(add_one(keep_gu2, r_gu2), axis=1))
        keep_a2, go = add_core(a2, r_a2)
        r_a2 = ring.send(go, ("x", "y"))
        r_d1 = ring.send(d1[1:], ("core",))
        keep_d2, go = near_rows(add_one(keep_d2, r_d2))
        r_d2 = ring.send(go, ("x", "y"))
    gu1 = gate_up_bwd(me, xf1, dg1, du1)
    h2 = down(me, tied(hm2, gu1[0]), hid2, v_d)
    if ring:
        gu1, h2, r_a2, r_d1, r_d2 = sync(gu1, h2, r_a2, r_d1, r_d2)
        sum_d2 = add_one(keep_d2, r_d2)
        keep_a2, go = add_two(keep_a2, r_a2)
        r_a2 = ring.send(go, ("y", "x"))
        r_gu1 = ring.send(gu1[1::2], ("core", "core"))
        z_d1 = ring.scatter_z(d1[0] + r_d1[0])
    output = exchange(h2.astype(bf16)[local_slots], rows)
    gm1, bo1, dou1, gg_m1 = mlp_dx(me, dg1, du1, w_g, w_u, hm1, gain_m1, gh1, w_o, f32)
    if ring:
        gm1, bo1, dou1, gg_m1, r_a2, r_gu1 = sync(gm1, bo1, dou1, gg_m1, r_a2, r_gu1)
        done_a2 = add_one(keep_a2, r_a2)
        keep_gu1, go = add_core(gu1, r_gu1)
        r_gu1 = ring.send(go, ("x", "y"))
    dqk1, dv1 = based_bwd(qk1, v1, dou1, ou1, rden1, seg_row, seg_col, live_col)
    if ring:
        dqk1, dv1, output, r_gu1 = sync(dqk1, dv1, output, r_gu1)
        keep_gu1, go = add_two(keep_gu1, r_gu1)
        r_gu1 = ring.send(go, ("y", "x"))
    *a1, g0, gg_a1 = attn_bwd(me, xa1, [dqk1, dv1], [w_qk, w_v], o1, bo1, start, gain_a1, gm1, HALVES_ONE)
    output = output[restore]
    gains = jnp.concatenate([gg_a1, gg_m1, gg_a2, gg_m2], axis=0)
    if ring:
        a1, g0, gains, r_gu1, z_gu2, z_d1 = sync(a1, g0, gains, r_gu1, z_gu2, z_d1)
        gu1 = add_one(keep_gu1, r_gu1)
        arrived = exchange(g0.astype(bf16)[local_slots], rows)
        r_a1 = ring.send(a1[1::2], ("core", "core"))
        r_gains = ring.send([gains], ("core",))
        keep_d1, go = far_rows(z_d1)
        r_d1 = ring.send(go, ("y", "x"))
        r_a1, r_gains, r_d1 = sync(r_a1, r_gains, r_d1)
        keep_a1, go = add_core(a1, r_a1)
        r_a1 = ring.send(go, ("x", "y"))
        gains = gains + r_gains[0]
        r_gains = ring.send([gains], ("x",))
        keep_d1, go = near_rows(add_one(keep_d1, r_d1))
        r_d1 = ring.send(go, ("x", "y"))
        r_a1, r_gains, r_d1 = sync(r_a1, r_gains, r_d1)
        keep_a1, go = add_two(keep_a1, r_a1)
        r_a1 = ring.send(go, ("y", "x"))
        gains = gains + r_gains[0]
        r_gains = ring.send([gains], ("y",))
        sum_d1 = add_one(keep_d1, r_d1)
        gu1, r_a1, r_gains, arrived = sync(gu1, r_a1, r_gains, arrived)
        a1 = add_one(keep_a1, r_a1)
        gains = gains + r_gains[0]
        last = ring.reduce_z([jnp.concatenate(gu1, axis=1), jnp.concatenate(a1, axis=1)])
        far_z = [ring.swap(gains, "z", by) for by in (1, 2, 3)]
        gains = (gains + far_z[0]) + (far_z[1] + far_z[2])
        z_a2 = ring.scatter_z(jnp.concatenate([after(v, z_d1) for v in done_a2], axis=1))
        cut = lambda v, n: [v[:n].astype(f32), v[n:].astype(f32)]
        sum_gu1, sum_a1 = cut(last[0], FC), cut(last[1], a1[0].shape[1])
        sum_gu2, sum_a2 = cut(z_gu2, FC), cut(z_a2, done_a2[0].shape[1])
        tokens_grad = arrived
        wide = lambda halves: [h.astype(f32) for h in halves]
        sum_d1, sum_d2 = wide(sum_d1), wide(sum_d2)
        rest = sum_parts(sum_a2, sum_gu2, sum_d2, HALVES_TWO)
        sums1, sums2 = sum_parts(sum_a1, sum_gu1, sum_d1, HALVES_ONE), rest
        sums1 = [sums1[0][:, :64], sums1[0][:, 64:]] + sums1[1:]
        tokens_grad = tokens_grad[restore]
    else:
        sums1 = sum_any(d1, gu1, a1, HALVES_ONE)
        sums2 = sum_any(d2, gu2, a2, HALVES_TWO)
        gains = lax.psum(gains, ("row", "col"))
        tokens_grad = exchange(g0.astype(bf16)[local_slots], rows)[restore]
    return (
        output, tokens_grad,
        gains[0], *sums1[:4], gains[1], *sums1[4:],
        gains[2], *sums2[:4], gains[3], *sums2[4:],
    )


def solution(mesh):
    names, rows, cols = ("row", "col"), "row", "col"
    if (mesh.shape["row"], mesh.shape["col"]) == (ROWS, COLS):
        names = ("z", "y", "x", "core")
        rows, cols = names[:2], names[2:]
        mesh = Mesh(mesh.devices.reshape(4, 2, 2, 2), names)
    block, weight = P(names, None), P(rows, cols)
    layer_in = (P(),) + (weight,) * 4 + (P(),) + (weight,) * 3
    return jax.shard_map(
        functools.partial(body, names),
        mesh=mesh,
        in_specs=(block, block, P(), block, P(names)) + layer_in * 2,
        out_specs=(block, block) + layer_in * 2,
        check_vma=False,
    )
```

```python
import functools

import jax
import jax.numpy as jnp
from jax import lax
from jax.experimental import pallas as pl
from jax.experimental.pallas import tpu as pltpu
from jax.sharding import Mesh, PartitionSpec as P

HEADS = 16
FEAT = 16
HEAD_DIM = 64
WINDOW = 64
MAX_LEN = 256
D = 1024
T = 512
HALF = 256
EPS = 1e-05
NEG = -1e30
ROWS = 8
COLS = 4
FB = 344
FBP = 352
FFP = ROWS * FBP
FC = FFP // COLS

bf16, f32, i32 = jnp.bfloat16, jnp.float32, jnp.int32
NN, NT, TN = ((1,), (0,)), ((1,), (1,)), ((0,), (0,))


def dot(a, b, dims):
    return lax.dot_general(a, b, (dims, ((), ())), preferred_element_type=f32)


def call(body, grid, ins, outs, scratch=(), flops=0, prefetch=None):
    extra = 0 if prefetch is None else 1

    def spec(block, index):
        if block is None:
            return pl.BlockSpec(memory_space=pl.ANY)
        return pl.BlockSpec(block, index)

    in_specs, args = [], []
    for item in ins:
        if not isinstance(item, tuple):
            nd = item.ndim
            item = (item, item.shape, functools.partial(lambda n, *_: (0,) * n, nd))
        args.append(item[0])
        in_specs.append(spec(item[1], item[2]))
    out_specs = [spec(o[2], o[3]) for o in outs]
    out_shape = [jax.ShapeDtypeStruct(o[0], o[1]) for o in outs]
    moved = sum(a.size * a.dtype.itemsize for a in args)
    moved += sum(s.size * s.dtype.itemsize for s in out_shape)
    cost = pl.CostEstimate(flops=int(flops), bytes_accessed=int(moved), transcendentals=0)
    got = pl.pallas_call(
        body,
        out_shape=out_shape,
        grid_spec=pltpu.PrefetchScalarGridSpec(
            num_scalar_prefetch=extra,
            grid=grid,
            in_specs=in_specs,
            out_specs=out_specs,
            scratch_shapes=list(scratch),
        ),
        compiler_params=pltpu.CompilerParams(vmem_limit_bytes=56 * 2**20),
        cost_estimate=cost,
    )(*(([prefetch] if extra else []) + args))
    return got


def whole_map(*shape):
    zeros = (0,) * len(shape)
    return lambda *_: zeros


def norm_factor(h):
    return lax.rsqrt(jnp.mean(h * h, axis=-1, keepdims=True) + EPS)


class Strips:
    def __init__(self, half, swapped, at, n):
        self.bufs, self.swapped, self.at, self.n = half, swapped, at, n

    def scratch(self):
        return [pltpu.VMEM((2, 2, 2, 4, self.n, 128), bf16), pltpu.SemaphoreType.DMA((2, 2, 2))]

    def start(self, refs, box, sems):
        order = [(core, x, y) for core in range(2) for x in range(2) for y in range(2)]
        for core, x, y in order:
            hi, lo = (x, y) if self.swapped else (y, x)
            src = refs[core * 2 + hi].at[lo]
            if self.n != self.bufs[0].shape[2]:
                src = src.at[:, pl.ds(self.at, self.n)]
            pltpu.make_async_copy(src, box.at[core, hi, lo], sems.at[core, hi, lo]).start()

    def wait(self, box, sems, core, x):
        for y in range(2):
            hi, lo = (x, y) if self.swapped else (y, x)
            there = box.at[core, hi, lo]
            pltpu.make_async_copy(there, there, sems.at[core, hi, lo]).wait()

    def wait_all(self, box, sems):
        for core in range(2):
            for x in range(2):
                self.wait(box, sems, core, x)

    def piece(self, box, z, y, x, core):
        return box.at[core, x, y, z] if self.swapped else box.at[core, y, x, z]


class DownRows:
    def __init__(self, bufs):
        self.bufs = bufs

    def scratch(self):
        return [pltpu.VMEM((2, 4, FFP, 128), bf16), pltpu.SemaphoreType.DMA((2, 4))]

    def start(self, refs, box, sems):
        for z in range(4):
            for core in range(2):
                pltpu.make_async_copy(refs[core].at[z], box.at[core, z], sems.at[core, z]).start()

    def rows(self, box, sems, z, my):
        for core in range(2):
            there = box.at[core, z]
            pltpu.make_async_copy(there, there, sems.at[core, z]).wait()
        halves = []
        for y in range(2):
            parts = []
            for x, core in PLACES:
                for at in down_places(x, y ^ my):
                    parts.append(box[core, z, pl.ds(at, FBP), :])
            halves.append(jnp.concatenate(parts, axis=1))
        return jnp.concatenate(halves, axis=0)


def down_places(x, y):
    return [pl.multiple_of(p * FBP, 16) for p in (y * 2 + x, 4 + x * 2 + y)]


BLOCKS = [(z, y) for z in range(4) for y in range(2)]
PLACES = [(x, core) for x in range(2) for core in range(2)]


def step_place(i):
    return i % 2, i // 2


def step_col(i, me):
    return ((i % 2) * 2 + i // 2) ^ me[1]


def regroup(dst_ref, src_ref, count, me):
    width = D // count
    for j in range(count):
        at = pl.multiple_of((j ^ me) * width, 128)
        dst_ref[:, j * width : (j + 1) * width] = src_ref[:, pl.ds(at, width)]


class Kernel:
    def __init__(self, n_in, strips, n_out):
        self.n_in, self.strips, self.n_out = n_in, strips, n_out

    def split(self, refs):
        ins, refs = refs[: self.n_in], refs[self.n_in :]
        srcs = []
        for s in self.strips:
            srcs.append(refs[: len(s.bufs)])
            refs = refs[len(s.bufs) :]
        outs, refs = refs[: self.n_out], refs[self.n_out :]
        hold = [(s, srcs[j], refs[2 * j], refs[2 * j + 1]) for j, s in enumerate(self.strips)]
        return ins, hold, outs, refs[2 * len(self.strips) :]

    def ins(self):
        return [(b, None, None) for s in self.strips for b in s.bufs]

    def scratch(self):
        return [i for s in self.strips for i in s.scratch()]


def start_all(hold):
    for s, srcs, box, sems in hold:
        s.start(srcs, box, sems)


def col_block(s, box, x, core):
    strips = []
    for j in range(s.n // 128):
        strips.append(jnp.concatenate([s.piece(box, z, y, x, core)[j * 128 : (j + 1) * 128, :] for z, y in BLOCKS], axis=0))
    return strips[0] if len(strips) == 1 else jnp.concatenate(strips, axis=1)


def norm_proj(me, h, gain, strips):
    n = len(strips)
    kern = Kernel(2, strips, n + 1)

    def body(me_ref, *refs):
        (h_ref, gain_ref), hold, (xa_ref, *outs), (xr_ref,) = kern.split(refs)
        i = pl.program_id(0)

        @pl.when(i == 0)
        def _():
            start_all(hold)
            hv = h_ref[...].astype(f32)
            xa_ref[...] = (hv * norm_factor(hv) * gain_ref[...]).astype(bf16)
            regroup(xr_ref, xa_ref, ROWS, me_ref[0])

        x, core = step_place(i)
        for (s, _, box, sems), o_ref in zip(hold, outs):
            s.wait(box, sems, core, x)
            o_ref[...] = dot(xr_ref[...], col_block(s, box, x, core), NN).astype(bf16)

    outs = [((T, D), bf16, (T, D), whole_map(T, D))]
    for s in strips:
        outs.append(((T, s.n * COLS), bf16, (T, s.n), lambda i, me: (0, step_col(i, me))))
    total = sum(s.n * COLS for s in strips)
    return call(
        body, (COLS,), [h, gain.reshape(1, D)] + kern.ins(), outs,
        scratch=kern.scratch() + [pltpu.VMEM((T, D), bf16)], flops=2 * T * D * total, prefetch=me,
    )


def lanes(shape, width):
    return lax.broadcasted_iota(i32, shape, len(shape) - 1) // width


def fill_mask(mask_ref, seg_q, seg_k, live_k, q_axis, window):
    q = lax.broadcasted_iota(i32, (T, T), q_axis)
    k = lax.broadcasted_iota(i32, (T, T), 1 - q_axis)
    ok = (k <= q) & (k > q - window) & (seg_q == seg_k) & ((live_k > 0) | (k == q))
    mask_ref[...] = jnp.where(ok, 1.0, 0.0)


def based_fwd(qk, v, seg_row, seg_col, live_row):
    def body(qk_ref, v_ref, sr_ref, sc_ref, lr_ref, o_ref, ou_ref, rden_ref, mask_ref):
        @pl.when(pl.program_id(0) == 0)
        def _():
            fill_mask(mask_ref, sc_ref[...], sr_ref[...], lr_ref[...], 0, MAX_LEN)

        q4, k4 = qk_ref[:, 0:64], qk_ref[:, 64:128]
        qlane = lanes((T, 64), FEAT)
        first = lanes((HALF, 128), HEAD_DIM) == 0
        scaled = q4.astype(f32) * (FEAT**-0.5)
        for pair in range(2):
            v2 = v_ref[:, pair * 128 : pair * 128 + 128]
            for tb in range(2):
                t0, s1 = tb * HALF, (tb + 1) * HALF
                got = []
                for e in range(2):
                    qm = jnp.where(qlane == pair * 2 + e, scaled, 0.0).astype(bf16)
                    a = dot(qm[t0 : t0 + HALF], k4[0:s1], NT)
                    p = (1.0 + a * (1.0 + 0.5 * a)) * mask_ref[t0 : t0 + HALF, 0:s1]
                    den = jnp.sum(p, axis=-1, keepdims=True)
                    got.append((dot(p.astype(bf16), v2[0:s1], NN), den))
                rden = 1.0 / jnp.where(first, got[0][1], got[1][1])
                ou = jnp.where(first, got[0][0], got[1][0]) * rden
                at = (slice(t0, t0 + HALF), slice(pair * 128, pair * 128 + 128))
                ou_ref[at] = ou
                rden_ref[at] = rden
                o_ref[at] = ou.astype(bf16)

    wide = (T, 256)
    col = lambda c: (0, c)
    return call(
        body,
        (4,),
        [(qk, (T, 128), col), (v, wide, col), seg_row, seg_col, live_row],
        [((T, D), bf16, wide, col), ((T, D), f32, wide, col), ((T, D), f32, wide, col)],
        scratch=[pltpu.VMEM((T, T), f32)],
        flops=HEADS * T * T * 2 * 192,
    )


def based_bwd(qk, v, dou, ou, rden, seg_row, seg_col, live_col):
    def body(qk_ref, v_ref, dou_ref, ou_ref, rden_ref, sr_ref, sc_ref, lc_ref, dqk_ref, dv_ref, mask_ref, dk_ref, dva_ref):
        @pl.when(pl.program_id(0) == 0)
        def _():
            fill_mask(mask_ref, sr_ref[...], sc_ref[...], lc_ref[...], 1, MAX_LEN)

        q4, k4 = qk_ref[:, 0:64], qk_ref[:, 64:128]
        qlane = lanes((T, 64), FEAT)
        q_scaled = q4.astype(f32) * (FEAT**-0.5)
        k_scaled = k4.astype(f32) * (FEAT**-0.5)
        vlane = lanes((T, 128), HEAD_DIM)
        dnum_f = dou_ref[...] * rden_ref[...]
        term = dnum_f * ou_ref[...]
        high = term.astype(bf16)
        low = (term - high.astype(f32)).astype(bf16)
        pick = jnp.where(
            lax.broadcasted_iota(i32, (8, 256), 0) == lanes((8, 256), HEAD_DIM), 1.0, 0.0
        ).astype(bf16)
        dden = -(dot(pick, high, NT) + dot(pick, low, NT))
        dk_ref[...] = jnp.zeros((T, 64), f32)
        dva_ref[...] = jnp.zeros((T, 256), f32)
        dq = [jnp.zeros((HALF, 64), f32), jnp.zeros((HALF, 64), f32)]
        for pair in range(2):
            cols = slice(pair * 128, pair * 128 + 128)
            v2 = v_ref[:, cols]
            for e in range(2):
                head = pair * 2 + e
                qm = jnp.where(qlane == head, q_scaled, 0.0).astype(bf16)
                km = jnp.where(qlane == head, k_scaled, 0.0).astype(bf16)
                dn = jnp.where(vlane == e, dnum_f[:, cols], 0.0).astype(bf16)
                for tb in range(2):
                    t0, s1 = tb * HALF, (tb + 1) * HALF
                    at = slice(t0, t0 + HALF)
                    a = dot(k4[0:s1], qm[at], NT)
                    m = mask_ref[0:s1, at]
                    p = (1.0 + a * (1.0 + 0.5 * a)) * m
                    dp = dot(v2[0:s1], dn[at], NT) + dden[head : head + 1, at]
                    da = (dp * m * (1.0 + a)).astype(bf16)
                    dk_ref[0:s1, :] += dot(da, qm[at], NN)
                    dva_ref[0:s1, cols] += dot(p.astype(bf16), dn[at], NN)
                    dq[tb] += dot(da, km[0:s1], TN)
        for tb in range(2):
            at = slice(tb * HALF, tb * HALF + HALF)
            dqk_ref[at, 0:64] = dq[tb].astype(bf16)
        dqk_ref[:, 64:128] = dk_ref[...].astype(bf16)
        dv_ref[...] = dva_ref[...].astype(bf16)

    wide = (T, 256)
    col = lambda c: (0, c)
    return call(
        body,
        (4,),
        [(qk, (T, 128), col), (v, wide, col), (dou, wide, col), (ou, wide, col), (rden, wide, col), seg_row, seg_col, live_col],
        [((T, 512), bf16, (T, 128), col), ((T, D), bf16, wide, col)],
        scratch=[pltpu.VMEM((T, T), f32), pltpu.VMEM((T, 64), f32), pltpu.VMEM((T, 256), f32)],
        flops=HEADS * T * T * 2 * 480,
    )


SPAN = ((0, HALF), (HALF - WINDOW, T))


def window_fwd(q, k, v, seg_row, seg_col, live_col):
    def body(q_ref, k_ref, v_ref, sr_ref, sc_ref, lc_ref, o_ref, mask_ref):
        @pl.when(pl.program_id(0) == 0)
        def _():
            fill_mask(mask_ref, sr_ref[...], sc_ref[...], lc_ref[...], 1, WINDOW)

        first = lanes((HALF, 128), HEAD_DIM) == 0
        qlane = lanes((T, 128), HEAD_DIM)
        scaled = q_ref[...].astype(f32) * (HEAD_DIM**-0.5)
        for tb in range(2):
            at = slice(tb * HALF, tb * HALF + HALF)
            s0, s1 = SPAN[tb]
            ok = mask_ref[s0:s1, at] > 0.5
            got = []
            for e in range(2):
                qm = jnp.where(qlane == e, scaled, 0.0).astype(bf16)
                c = dot(k_ref[s0:s1, :], qm[at], NT)
                c = jnp.where(ok, c, NEG)
                w = jnp.exp(c - jnp.max(c, axis=0, keepdims=True))
                w = w * (1.0 / jnp.sum(w, axis=0, keepdims=True))
                got.append(dot(w.astype(bf16), v_ref[s0:s1, :], TN))
            o_ref[at, :] = jnp.where(first, got[0], got[1]).astype(bf16)

    blk = (T, 128)
    col = lambda c: (0, c)
    return call(
        body,
        (8,),
        [(q, blk, col), (k, blk, col), (v, blk, col), seg_row, seg_col, live_col],
        [((T, D), bf16, blk, col)],
        scratch=[pltpu.VMEM((T, T), f32)],
        flops=HEADS * T * T * 2 * 192,
    )[0]


def window_bwd(q, k, v, dor, seg_row, seg_col, live_col):
    def body(q_ref, k_ref, v_ref, do_ref, sr_ref, sc_ref, lc_ref, dq_ref, dk_ref, dv_ref, mask_ref, dka_ref, dva_ref):
        @pl.when(pl.program_id(0) == 0)
        def _():
            fill_mask(mask_ref, sr_ref[...], sc_ref[...], lc_ref[...], 1, WINDOW)

        lane = lanes((T, 128), HEAD_DIM)
        q_scaled = q_ref[...].astype(f32) * (HEAD_DIM**-0.5)
        k_scaled = k_ref[...].astype(f32) * (HEAD_DIM**-0.5)
        do = do_ref[...]
        dka_ref[...] = jnp.zeros((T, 128), f32)
        dva_ref[...] = jnp.zeros((T, 128), f32)
        for tb in range(2):
            at = slice(tb * HALF, tb * HALF + HALF)
            s0, s1 = SPAN[tb]
            ok = mask_ref[s0:s1, at] > 0.5
            dq = jnp.zeros((HALF, 128), f32)
            for e in range(2):
                qm = jnp.where(lane == e, q_scaled, 0.0).astype(bf16)
                km = jnp.where(lane == e, k_scaled, 0.0).astype(bf16)
                dm = jnp.where(lane == e, do, jnp.zeros_like(do))
                c = dot(k_ref[s0:s1, :], qm[at], NT)
                c = jnp.where(ok, c, NEG)
                w = jnp.exp(c - jnp.max(c, axis=0, keepdims=True))
                w = w * (1.0 / jnp.sum(w, axis=0, keepdims=True))
                dw = dot(v_ref[s0:s1, :], dm[at], NT)
                ds = (w * (dw - jnp.sum(w * dw, axis=0, keepdims=True))).astype(bf16)
                dka_ref[s0:s1, :] += dot(ds, qm[at], NN)
                dva_ref[s0:s1, :] += dot(w.astype(bf16), dm[at], NN)
                dq += dot(ds, km[s0:s1], TN)
            dq_ref[at, :] = dq.astype(bf16)
        dk_ref[...] = dka_ref[...].astype(bf16)
        dv_ref[...] = dva_ref[...].astype(bf16)

    blk = (T, 128)
    col = lambda c: (0, c)
    return call(
        body,
        (8,),
        [(q, blk, col), (k, blk, col), (v, blk, col), (dor, blk, col), seg_row, seg_col, live_col],
        [((T, D), bf16, blk, col)] * 3,
        scratch=[pltpu.VMEM((T, T), f32), pltpu.VMEM((T, 128), f32), pltpu.VMEM((T, 128), f32)],
        flops=HEADS * T * T * 2 * 480,
    )


def attn_out(me, h, o, strip, gain):
    kern = Kernel(3, [strip], 2)

    def body(me_ref, *refs):
        (h_ref, o_ref, gain_ref), hold, (hm_ref, xf_ref), (or_ref,) = kern.split(refs)
        i = pl.program_id(0)

        @pl.when(i == 0)
        def _():
            start_all(hold)
            regroup(or_ref, o_ref, ROWS, me_ref[0])

        x, core = step_place(i)
        s, _, box, sems = hold[0]
        s.wait(box, sems, core, x)
        at = pl.ds(pl.multiple_of(step_col(i, me_ref) * 256, 256), 256)
        hm_ref[:, at] = h_ref[:, at].astype(f32) + dot(or_ref[...], col_block(s, box, x, core), NN)

        @pl.when(i == COLS - 1)
        def _():
            hm = hm_ref[...]
            xf_ref[...] = (hm * norm_factor(hm) * gain_ref[...]).astype(bf16)

    full = whole_map(T, D)
    return call(
        body, (COLS,), [h, o, gain.reshape(1, D)] + kern.ins(),
        [((T, D), f32, (T, D), full), ((T, D), bf16, (T, D), full)],
        scratch=kern.scratch() + [pltpu.VMEM((T, D), bf16)], flops=2 * T * D * D, prefetch=me,
    )


def hidden_block(s, box, x, core):
    return jnp.concatenate([s.piece(box, z, y, x, core)[...] for z, y in BLOCKS], axis=1)


def gate_up(me, xf, w_gate, w_up):
    kern = Kernel(1, [w_gate, w_up], 3)

    def body(me_ref, *refs):
        (xf_ref,), hold, (g_ref, u_ref, hid_ref), (xr_ref,) = kern.split(refs)
        i = pl.program_id(0)

        @pl.when(i == 0)
        def _():
            start_all(hold)
            regroup(xr_ref, xf_ref, ROWS, me_ref[0])

        x, core = step_place(i)
        got = []
        for s, _, box, sems in hold:
            s.wait(box, sems, core, x)
            got.append(dot(hidden_block(s, box, x, core), xr_ref[...], NT))
        g, u = got
        g_ref[...] = g.astype(bf16)
        u_ref[...] = u.astype(bf16)
        hid_ref[...] = (g * (1.0 / (1.0 + jnp.exp(-g))) * u).astype(bf16)

    row = lambda i, me: (step_col(i, me), 0)
    return call(
        body, (COLS,), [xf] + kern.ins(), [((FFP, T), bf16, (FC, T), row)] * 3,
        scratch=kern.scratch() + [pltpu.VMEM((T, D), bf16)], flops=4 * T * D * FFP, prefetch=me,
    )


def down(me, hm, hid, w_down):
    kern = Kernel(2, [w_down], 1)

    def body(me_ref, *refs):
        (hm_ref, hid_ref), hold, (h_ref,), (acc_ref,) = kern.split(refs)
        i = pl.program_id(0)

        @pl.when(i == 0)
        def _():
            start_all(hold)
            regroup(acc_ref, hm_ref, COLS, me_ref[1])

        s, _, box, sems = hold[0]
        acc_ref[...] += dot(hid_ref[...], s.rows(box, sems, i, me_ref[0]), TN)

        @pl.when(i == COLS - 1)
        def _():
            regroup(h_ref, acc_ref, COLS, me_ref[1])

    return call(
        body, (COLS,), [hm, (hid, (FC, T), lambda i, me: (i, 0))] + kern.ins(),
        [((T, D), f32, (T, D), whole_map(T, D))],
        scratch=kern.scratch() + [pltpu.VMEM((T, D), f32)], flops=2 * T * D * FFP, prefetch=me,
    )[0]


def down_bwd(me, bd, w_down, hid, g, u):
    kern = Kernel(4, [w_down], 4)

    def body(me_ref, *refs):
        (bd_ref, hid_ref, g_ref, u_ref), hold, (dg_ref, du_ref, *p_refs), (br_ref,) = kern.split(refs)
        i = pl.program_id(0)

        @pl.when(i == 0)
        def _():
            start_all(hold)
            regroup(br_ref, bd_ref, COLS, me_ref[1])

        bdv = br_ref[...].astype(bf16)
        gwd = dot(hid_ref[...], bdv, NN).astype(bf16)
        for x, core in PLACES:
            at = (x * 2 + core) * 256
            for y in range(2):
                rows = slice(y * FBP, (y + 1) * FBP)
                for half, to in enumerate(down_places(x, y ^ me_ref[0])):
                    p_refs[core][0, pl.ds(to, FBP), :] = gwd[rows, at + half * 128 : at + half * 128 + 128]
        s, _, box, sems = hold[0]
        dhid = dot(s.rows(box, sems, i, me_ref[0]), bdv, NT)
        gv, uv = g_ref[...].astype(f32), u_ref[...].astype(f32)
        sig = 1.0 / (1.0 + jnp.exp(-gv))
        act = gv * sig
        du_ref[...] = (dhid * act).astype(bf16)
        dg_ref[...] = (dhid * uv * (sig + act * (1.0 - sig))).astype(bf16)

    row = lambda i, me: (i, 0)
    hblk = (FC, T)
    pieces = ((4, FFP, 128), bf16, (1, FFP, 128), lambda i, me: (i, 0, 0))
    return call(
        body, (COLS,), [bd, (hid, hblk, row), (g, hblk, row), (u, hblk, row)] + kern.ins(),
        [((FFP, T), bf16, hblk, row), ((FFP, T), bf16, hblk, row)] + [pieces] * 2,
        scratch=kern.scratch() + [pltpu.VMEM((T, D), bd.dtype)], flops=4 * T * D * FFP, prefetch=me,
    )


def piece_specs(n1, n2):
    out = []
    for n, block, place in ((n1, (1, 2, 4), lambda j: (j, 0)), (n2, (2, 1, 4), lambda j: (0, j))):
        for step in (lambda i: jnp.minimum(i, 1), lambda i: jnp.maximum(i - 2, 0)):
            index = functools.partial(lambda place, step, i, me: (*place(step(i)), 0, 0, 0), place, step)
            out.append(((2, 2, 4, n, 128), bf16, (*block, n, 128), index))
    return out


def for_core(refs, write):
    for core in range(2):

        @pl.when(pl.program_id(0) // 2 == core)
        def _():
            write(refs[core], refs[2 + core])


def gate_up_bwd(me, xf, dg, du):
    def body(me_ref, xf_ref, dg_ref, du_ref, *refs):
        *p_refs, xr_ref = refs

        @pl.when(pl.program_id(0) == 0)
        def _():
            regroup(xr_ref, xf_ref, ROWS, me_ref[0])

        gwg = dot(dg_ref[...], xr_ref[...], NN).astype(bf16)
        gwu = dot(du_ref[...], xr_ref[...], NN).astype(bf16)

        def write(one, two):
            for r, (z, y) in enumerate(BLOCKS):
                one[0, y, z] = gwg[:, r * 128 : (r + 1) * 128]
                two[y, 0, z] = gwu[:, r * 128 : (r + 1) * 128]

        for_core(p_refs, write)

    row = lambda i, me: (step_col(i, me), 0)
    return call(
        body, (COLS,), [xf, (dg, (FC, T), row), (du, (FC, T), row)], piece_specs(FC, FC),
        scratch=[pltpu.VMEM((T, D), bf16)], flops=4 * T * D * FFP, prefetch=me,
    )


def norm_bwd(dx, h, gain, g):
    rf = norm_factor(h)
    hr = h * rf
    dgain = jnp.sum(dx * hr, axis=0, keepdims=True)
    gd = gain * dx
    mean = jnp.sum(gd * hr, axis=-1, keepdims=True) * (1.0 / D)
    return dgain, g + rf * (gd - hr * mean)


def add_to(acc_ref, part):
    @pl.when(pl.program_id(0) == 0)
    def _():
        acc_ref[...] = part

    @pl.when(pl.program_id(0) > 0)
    def _():
        acc_ref[...] += part


def mlp_dx(me, dg, du, w_gate, w_up, hm, gain, g, w_out, kind):
    kern = Kernel(5, [w_gate, w_up, w_out], 4)

    def body(me_ref, *refs):
        (dg_ref, du_ref, hm_ref, gain_ref, g_ref), hold, outs, (acc_ref, un_ref, br_ref) = kern.split(refs)
        gm_ref, bo_ref, dou_ref, gg_ref = outs
        i = pl.program_id(0)

        @pl.when(i == 0)
        def _():
            start_all(hold)

        x, core = step_place(i)
        part = None
        for (s, _, box, sems), d_ref in zip(hold[:2], (dg_ref, du_ref)):
            s.wait(box, sems, core, x)
            term = dot(d_ref[...], hidden_block(s, box, x, core), TN)
            part = term if part is None else part + term
        add_to(acc_ref, part)

        @pl.when(i == COLS - 1)
        def _():
            regroup(un_ref, acc_ref, ROWS, me_ref[0])
            gg, gm = norm_bwd(un_ref[...], hm_ref[...], gain_ref[...], g_ref[...].astype(f32))
            gg_ref[...] = gg
            gm_ref[...] = gm
            bo_ref[...] = gm.astype(bf16)
            regroup(br_ref, bo_ref, COLS, me_ref[1])
            s, _, box, sems = hold[2]
            s.wait_all(box, sems)
            w = jnp.concatenate([col_block(s, box, x, core) for x, core in PLACES], axis=1)
            acc_ref[...] = dot(br_ref[...], w, NT)
            regroup(un_ref, acc_ref, ROWS, me_ref[0])
            dou_ref[...] = un_ref[...].astype(kind)

    row = lambda i, me: (step_col(i, me), 0)
    full = whole_map(T, D)
    return call(
        body, (COLS,), [(dg, (FC, T), row), (du, (FC, T), row), hm, gain.reshape(1, D), g] + kern.ins(),
        [((T, D), f32, (T, D), full), ((T, D), bf16, (T, D), full), ((T, D), kind, (T, D), full), ((1, D), f32, (1, D), full)],
        scratch=kern.scratch() + [pltpu.VMEM((T, D), f32), pltpu.VMEM((T, D), f32), pltpu.VMEM((T, D), bf16)],
        flops=4 * T * D * FFP + 2 * T * D * D, prefetch=me,
    )


def attn_bwd(me, xa, grads, strips, o, bo, h, gain, gm, halves):
    n = len(grads)
    kern = Kernel(6 + n, strips, 6)

    def body(me_ref, *refs):
        ins, hold, (*p_refs, g_ref, gg_ref), (xr_ref, or_ref, xt_ref, ot_ref, acc_ref) = kern.split(refs)
        xa_ref, o_ref, h_ref, gain_ref, gm_ref, bo_ref, *d_refs = ins
        i = pl.program_id(0)

        @pl.when(i == 0)
        def _():
            start_all(hold)
            regroup(xr_ref, xa_ref, ROWS, me_ref[0])
            regroup(or_ref, o_ref, ROWS, me_ref[0])
            xt_ref[...] = xr_ref[...].T
            ot_ref[...] = or_ref[...].T

        tiles = [dot(xt_ref[...], d[...], NN).astype(bf16) for d in d_refs]
        tiles.append(dot(ot_ref[...], bo_ref[...], NN).astype(bf16))

        def write(one, two):
            for j, (which, at) in enumerate(halves[0]):
                for r, (z, y) in enumerate(BLOCKS):
                    one[0, y, z, j * 128 : (j + 1) * 128] = tiles[which][r * 128 : (r + 1) * 128, at : at + 128]
            for j, (which, at) in enumerate(halves[1]):
                for r, (z, y) in enumerate(BLOCKS):
                    two[y, 0, z, j * 128 : (j + 1) * 128] = tiles[which][r * 128 : (r + 1) * 128, at : at + 128]

        for_core(p_refs, write)
        x, core = step_place(i)
        part = None
        for (s, _, box, sems), d in zip(hold, d_refs):
            s.wait(box, sems, core, x)
            term = dot(d[...], col_block(s, box, x, core), NT)
            part = term if part is None else part + term
        add_to(acc_ref, part)

        @pl.when(i == COLS - 1)
        def _():
            regroup(g_ref, acc_ref, ROWS, me_ref[0])
            gg, g = norm_bwd(g_ref[...], h_ref[...].astype(f32), gain_ref[...], gm_ref[...])
            gg_ref[...] = gg
            g_ref[...] = g

    col = lambda i, me: (0, step_col(i, me))
    full = whole_map(T, D)
    ins = [xa, o, h, gain.reshape(1, D), gm, (bo, (T, 256), col)]
    ins += [(d, (T, d.shape[1] // COLS), col) for d in grads]
    total = sum(d.shape[1] for d in grads)
    return call(
        body, (COLS,), ins + kern.ins(),
        piece_specs(128 * len(halves[0]), 128 * len(halves[1])) + [((T, D), f32, (T, D), full), ((1, D), f32, (1, D), full)],
        scratch=kern.scratch()
        + [pltpu.VMEM((T, D), bf16)] * 2
        + [pltpu.VMEM((D, T), bf16)] * 2
        + [pltpu.VMEM((T, D), f32)],
        flops=4 * T * D * total + 2 * T * D * D, prefetch=me,
    )


HALVES_ONE = (((1, 0), (1, 128)), ((0, 0), (2, 0), (2, 128)))
HALVES_TWO = (((0, 0), (0, 128), (1, 0), (1, 128)), ((2, 0), (2, 128), (3, 0), (3, 128)))


def attn_weights(bufs, halves):
    out = []
    for which in range(1 + max(w for half in halves for w, _ in half)):
        for k, half in enumerate(halves):
            at = [j for j, (w, _) in enumerate(half) if w == which]
            if at:
                out.append(Strips(bufs[k], k == 1, at[0] * 128, len(at) * 128))
    return out


def gate_weights(bufs):
    return Strips(bufs[0], False, 0, FC), Strips(bufs[1], True, 0, FC)


def pad_hidden(w):
    k = w.shape[0]
    return jnp.pad(w.reshape(k, -1, FB), ((0, 0), (0, 0), (0, FBP - FB))).reshape(k, -1).T


def pad_rows(w):
    n = w.shape[1]
    return jnp.pad(w.reshape(-1, FB, n), ((0, 0), (0, FBP - FB), (0, 0))).reshape(-1, n)


def strips_of(blocks, halves):
    return tuple(
        jnp.concatenate([blocks[which][..., at : at + 128] for which, at in strips], axis=-2) for strips in halves
    )


def after(value, *arrays):
    return lax.optimization_barrier((value, *arrays))[0] if arrays else value


def sync(*groups):
    flat, tree = jax.tree.flatten(groups)
    return jax.tree.unflatten(tree, lax.optimization_barrier(flat))


def add_core(four, got):
    keep = [four[0][0] + got[0][0], four[2][0] + got[1][0]]
    return keep, [four[0][1] + got[0][1], four[2][1] + got[1][1]]


def add_two(keep, got):
    return [k[0] + g[0] for k, g in zip(keep, got)], [k[1] + g[1] for k, g in zip(keep, got)]


def add_one(keep, got):
    return [k + g for k, g in zip(keep, got)]


def far_rows(total):
    parts = jnp.split(total, 4, axis=0)
    return parts[0::2], parts[1::2]


def near_rows(halves):
    parts = [jnp.split(h, 2, axis=0) for h in halves]
    return [p[0] for p in parts], [p[1] for p in parts]


class Ring:
    def __init__(self, names):
        self.axes = names
        self.z = lax.axis_index(names[0])

    def swap(self, value, axis, by=1):
        shift = {"z": 3, "y": 2, "x": 1, "core": 0}[axis]
        return lax.ppermute(value, self.axes, [(i, i ^ (by << shift)) for i in range(32)])

    def gather_z(self, both, *behind):
        near = [both] + [after(self.swap(both, "z", by), *behind) for by in (1, 2, 3)]
        low, high = self.z % 2 == 1, self.z >= 2
        a, b = jnp.where(low, near[1], near[0]), jnp.where(low, near[0], near[1])
        c, d = jnp.where(low, near[3], near[2]), jnp.where(low, near[2], near[3])
        pick = lambda p, q: jnp.where(high, q, p)
        return jnp.stack([pick(a, c), pick(b, d), pick(c, a), pick(d, b)])

    def gather_z_all(self, both):
        return lax.all_gather(both, self.axes[0], axis=0, tiled=False)

    def gather_lo(self, pair, *behind):
        got = [after(self.swap(v, axis), *behind) for v, axis in zip(pair, ("x", "y"))]
        return [jnp.stack([v, g]) for v, g in zip(pair, got)]

    def gather_hi(self, pair, *behind):
        return [[v, after(self.swap(v, axis), *behind)] for v, axis in zip(pair, ("y", "x"))]

    def gather_core(self, full, *behind):
        return [half + [after(self.swap(b, "core"), *behind) for b in half] for half in full]

    def gather_down(self, pair):
        return jnp.stack([jnp.stack(half) for half in self.gather_hi(self.gather_lo(pair))]).reshape(-1, 128)

    def scatter_z(self, value):
        return lax.psum_scatter(value, self.axes[0], scatter_dimension=0, tiled=False)

    def send(self, values, axes):
        return [self.swap(v, axis) for v, axis in zip(values, axes)]

    def send_back(self, value):
        part = lambda by: lax.dynamic_index_in_dim(value, self.z ^ by, 0, False)
        return [self.swap(part(by), "z", by) for by in (1, 2, 3)]

    def add_back(self, value, got):
        total = lax.dynamic_index_in_dim(value, self.z, 0, False).astype(f32)
        for g in got:
            total = total + g.astype(f32)
        return total

    def reduce_z_all(self, pair):
        n1 = pair[0].shape[1]
        both = jnp.concatenate(pair, axis=1)
        total = lax.psum_scatter(both, self.axes[0], scatter_dimension=0, tiled=False).astype(f32)
        return total[:n1], total[n1:]


def pack(shards, halves):
    *attn, gate, up, dn = shards
    dp = pad_rows(dn)
    return [strips_of(attn, halves), (pad_hidden(gate), pad_hidden(up)), (dp[:, :128], dp[:, 128:])]


def boxes_any(weights, halves):
    *attn, gate, up, dn = weights

    def cut(w, rows, cols):
        return w.reshape(4, 2, rows, 2, 2, cols).transpose(0, 1, 3, 4, 2, 5)

    def boxes(one, two):
        first = [one[:, y, :, core].transpose(1, 0, 2, 3) for core in range(2) for y in range(2)]
        second = [two[:, :, x, core].transpose(1, 0, 2, 3) for core in range(2) for x in range(2)]
        return first, second

    a = boxes(*strips_of([cut(w, D // ROWS, w.shape[1] // COLS) for w in attn], halves))
    hidden = lambda w: pad_hidden(w).reshape(2, 2, FC, 4, 2, 128).transpose(3, 4, 0, 1, 2, 5)
    d = cut(pad_rows(dn), FBP, 256)
    one = d[..., :128].transpose(3, 0, 1, 2, 4, 5)
    two = d[..., 128:].transpose(3, 0, 2, 1, 4, 5)
    d = jnp.stack([one, two], axis=2).reshape(2, 4, FFP, 128)
    return [a, boxes(hidden(gate), hidden(up)), [d[0], d[1]]]


def unpad_hidden(g):
    k = g.shape[1]
    return g.reshape(-1, FBP, k)[:, :FB].reshape(-1, k).T


def unpad_rows(g):
    n = g.shape[1]
    return g.reshape(-1, FBP, n)[:, :FB].reshape(-1, n)


def whole_grad(own, send, swapped):
    p = jnp.stack([own, send])
    if swapped:
        p = jnp.swapaxes(p, 1, 2)
    core, x, y, z, n, w = p.shape
    return p.transpose(3, 2, 1, 0, 4, 5).reshape(z * y, x * core, n, w)


def join_strips(one, two, halves):
    out = []
    for which in range(1 + max(w for half in halves for w, _ in half)):
        got = {}
        for src, strips in ((one, halves[0]), (two, halves[1])):
            for j, (w, at) in enumerate(strips):
                if w == which:
                    got[at] = src[..., j * 128 : j * 128 + 128, :]
        out.append(jnp.concatenate([got[a] for a in sorted(got)], axis=-1))
    return out


def sum_parts(a, gu, d, halves):
    return join_strips(*a, halves) + [unpad_hidden(gu[0]), unpad_hidden(gu[1]), unpad_rows(jnp.concatenate(d, axis=1))]


def scatter_any(w):
    part = lax.psum_scatter(w, "row", scatter_dimension=0, tiled=True)
    return lax.psum_scatter(part, "col", scatter_dimension=1, tiled=True).astype(f32)


def natural(blocks):
    r, c, n, w = blocks.shape
    return blocks.transpose(0, 2, 1, 3).reshape(r * n, c * w)


def sum_any(pd, pgu, pa, halves):
    pairs = lambda p: (whole_grad(*p[:2], False), whole_grad(*p[2:], True))
    one, two = jnp.split(jnp.stack(pd).reshape(2, 4, 2, 2, 2, FBP, 128), 2, axis=2)
    dn = jnp.concatenate([one[:, :, 0], jnp.swapaxes(two[:, :, 0], 2, 3)], axis=-1)
    dn = dn.transpose(1, 2, 3, 0, 4, 5).reshape(ROWS, COLS, FBP, 256)
    dn = scatter_any(unpad_rows(natural(dn)))
    gu = [scatter_any(unpad_hidden(g.transpose(1, 2, 0, 3).reshape(FFP, D))) for g in pairs(pgu)]
    blocks = join_strips(*pairs(pa), halves)
    if len(blocks) == 3:
        blocks = [blocks[0][..., :64], blocks[0][..., 64:]] + blocks[1:]
    return [scatter_any(natural(b)) for b in blocks] + gu + [dn]


def join_qk(q, k, parts):
    n = q.shape[0]
    both = jnp.concatenate([q.reshape(n, parts, -1), k.reshape(n, parts, -1)], axis=2)
    return both.reshape(n, -1)

def route_plan(dest_slot, block_tokens, rows, cols):
    row_count = lax.axis_size(rows)
    col_count = lax.axis_size(cols)
    per_peer = block_tokens // row_count
    row_at = lax.axis_index(rows)
    col_at = lax.axis_index(cols)
    slot_table = dest_slot.reshape(row_count, col_count, block_tokens)
    column = lax.dynamic_index_in_dim(slot_table, col_at, 1, False)
    own_slots = lax.dynamic_index_in_dim(column, row_at, 0, False)
    send_order = jnp.argsort(own_slots)
    arrived = jnp.sort(column, axis=1)
    incoming = lax.dynamic_slice_in_dim(arrived, row_at * per_peer, per_peer, 1)
    local_slots = incoming.reshape(-1) - (row_at * col_count + col_at) * block_tokens
    placing = jnp.argsort(local_slots)
    return (send_order, local_slots, placing)


def exchange(value, axis):
    n, width = value.shape
    row_count = lax.axis_size(axis)
    got = lax.all_to_all(value.reshape(row_count, n // row_count, width), axis, split_axis=0, concat_axis=0, tiled=True)
    return got.reshape(n, width)


def gather_all(shards):
    return [lax.all_gather(lax.all_gather(w, "col", axis=1, tiled=True), "row", axis=0, tiled=True) for w in shards]


def body(names, tokens, cotangent, dest_slot, lengths, pad_mask, *params):
    ring = Ring(names) if len(names) == 4 else None
    rows, cols = (names[:2], names[2:]) if ring else names
    gain_a1, bq, bk, bv, bo_w, gain_m1, wg1, wu1, wd1 = params[:9]
    gain_a2, wq, wk, wv, wo2, gain_m2, wg2, wu2, wd2 = params[9:]
    shards1, shards2 = [bq, bk, bv, bo_w, wg1, wu1, wd1], [wq, wk, wv, wo2, wg2, wu2, wd2]
    send_order, local_slots, placing = route_plan(dest_slot, T, rows, cols)
    restore = jnp.argsort(send_order)
    outgoing = after(tokens[send_order], restore, placing) if ring else tokens[send_order]
    cot_going = cotangent[send_order]
    if ring:
        me = jnp.stack([lax.axis_index(names[1]), lax.axis_index(cols)]).astype(i32)
        packs = pack([join_qk(bq, bk, 1)] + shards1[2:], HALVES_ONE) + pack(shards2, HALVES_TWO)
        flat = [jnp.concatenate(p, axis=0) for p in packs]
        mid_d2 = ring.gather_down(packs[5])
        split = lambda k, v: [v[:, : packs[k][0].shape[0]], v[:, packs[k][0].shape[0] :]]
        each = lambda pair, *arrays: [after(v, *arrays) for v in pair]
        far = lambda halves: [half[1] for half in halves]
        near_a1 = ring.gather_z(flat[0])
        hi_a1 = ring.gather_hi(ring.gather_lo(each(split(0, near_a1), mid_d2)))
        near_gu1 = ring.gather_z(after(flat[1], near_a1))
        lo_gu1 = ring.gather_lo(each(split(1, near_gu1), *far(hi_a1)))
        outgoing = after(outgoing, near_gu1, *far(hi_a1))
        arrived = exchange(outgoing, rows)
        near_d1 = ring.gather_z(after(flat[2], arrived))
        start = arrived[placing]
    else:
        me = jnp.zeros((2,), i32)
        one, two = gather_all(shards1), gather_all(shards2)
        full = boxes_any([join_qk(one[0], one[1], COLS)] + one[2:], HALVES_ONE) + boxes_any(two, HALVES_TWO)
        start = exchange(outgoing, rows)[placing]
    position = jnp.arange(T, dtype=i32)
    segment, end = jnp.zeros((T,), i32), jnp.zeros((), i32)
    for j in range(lengths.shape[1]):
        end = end + lengths[0, j]
        segment = segment + (position >= end).astype(i32)
    seg_row, seg_col = segment.reshape(1, T), segment.reshape(T, 1)
    live_row, live_col = pad_mask.reshape(1, T), pad_mask.reshape(T, 1)

    tied = after if ring else (lambda value, *arrays: value)
    if ring:
        full_a1 = ring.gather_core(hi_a1)
        start = after(start, *lo_gu1)
    else:
        full_a1 = full[0]
    w_qk, w_v, w_o = attn_weights(full_a1, HALVES_ONE)
    xa1, qk1, v1 = norm_proj(me, start, gain_a1, [w_qk, w_v])
    o1, ou1, rden1 = based_fwd(qk1, v1, seg_row, seg_col, live_row)
    if ring:
        hi_gu1 = ring.gather_hi(lo_gu1, o1)
        near_a2 = ring.gather_z(after(flat[3], near_d1), o1)
    hm1, xf1 = attn_out(me, start, tied(o1, *(far(hi_gu1) + [near_a2] if ring else [])), w_o, gain_m1)
    if ring:
        full_gu1 = ring.gather_core(hi_gu1, xf1)
        lo_d1 = ring.gather_lo(each(split(2, near_d1), *far(hi_gu1)), xf1)
        xf1_late = after(xf1, *lo_d1)
    else:
        full_gu1, xf1_late = full[1], xf1
    w_g, w_u = gate_weights(full_gu1)
    g1, u1, hid1 = gate_up(me, xf1_late, w_g, w_u)
    if ring:
        hi_d1 = ring.gather_hi(lo_d1, hid1)
        lo_a2 = ring.gather_lo(each(split(3, near_a2), *lo_d1), hid1)
        near_gu2 = ring.gather_z(after(flat[4], near_a2), hid1)
        own_d1 = jnp.stack([jnp.stack(half) for half in hi_d1]).transpose(3, 0, 1, 2, 4, 5).reshape(4, FFP, 128)
        full_d1 = [own_d1, ring.swap(own_d1, "core")]
        hid1_late = after(hid1, *lo_a2)
        all_d2 = ring.gather_z_all(after(mid_d2, near_gu2))
        cot_going = after(cot_going, near_gu2)
    else:
        full_d1, hid1_late = full[2], hid1
    cot = exchange(cot_going, rows)[placing]
    w_d = DownRows(full_d1)
    h1 = down(me, hm1, hid1_late, w_d)
    if ring:
        hi_a2 = ring.gather_hi(lo_a2, h1)
        full_a2 = ring.gather_core(hi_a2)
        lo_gu2 = each(split(4, near_gu2), *far(hi_a2))
    else:
        full_a2 = full[3]
    v_q, v_k, v_v, v_o = attn_weights(full_a2, HALVES_TWO)
    xa2, q2, k2, v2 = norm_proj(me, h1, gain_a2, [v_q, v_k, v_v])
    if ring:
        lo_gu2 = ring.gather_lo(lo_gu2, q2)
    o2 = window_fwd(tied(q2, *(lo_gu2 if ring else [])), k2, v2, seg_row, seg_col, live_col)
    hm2, xf2 = attn_out(me, h1, o2, v_o, gain_m2)
    if ring:
        full_gu2 = ring.gather_core(ring.gather_hi(lo_gu2, xf2))
    else:
        full_gu2 = full[4]
    v_g, v_u = gate_weights(full_gu2)
    v_d = DownRows([all_d2, after(ring.swap(all_d2, "core"), xf2)] if ring else full[5])
    g2, u2, hid2 = gate_up(me, xf2, v_g, v_u)

    dg2, du2, *d2 = down_bwd(me, cot, v_d, hid2, g2, u2)
    if ring:
        r_d2 = ring.send(d2[1:], ("core",))
    h2 = down(me, hm2, hid2, v_d)
    outgoing = h2.astype(bf16)[local_slots]
    gu2 = gate_up_bwd(me, xf2, dg2, du2)
    if ring:
        dg2, du2, gu2, r_d2, outgoing = sync(dg2, du2, gu2, r_d2, outgoing)
        z_d2 = ring.scatter_z(d2[0] + r_d2[0])
        r_gu2 = ring.send(gu2[1::2], ("core", "core"))
    output = exchange(outgoing, rows)
    gm2, bo2, dor2, gg_m2 = mlp_dx(me, dg2, du2, v_g, v_u, hm2, gain_m2, cot, v_o, bf16)
    if ring:
        gm2, bo2, dor2, gg_m2, r_gu2 = sync(gm2, bo2, dor2, gg_m2, r_gu2)
        keep_gu2, go = add_core(gu2, r_gu2)
        r_gu2 = ring.send(go, ("x", "y"))
    dq2, dk2, dv2 = window_bwd(q2, k2, v2, dor2, seg_row, seg_col, live_col)
    *a2, gh1, gg_a2 = attn_bwd(me, xa2, [dq2, dk2, dv2], [v_q, v_k, v_v], o2, bo2, h1, gain_a2, gm2, HALVES_TWO)
    if ring:
        a2, gh1, gg_a2, r_gu2, z_d2, output = sync(a2, gh1, gg_a2, r_gu2, z_d2, output)
        keep_gu2, go = add_two(keep_gu2, r_gu2)
        r_gu2 = ring.send(go, ("y", "x"))
        r_a2 = ring.send(a2[1::2], ("core", "core"))
        keep_d2, go = far_rows(z_d2)
        r_d2 = ring.send(go, ("y", "x"))
    dg1, du1, *d1 = down_bwd(me, gh1, w_d, hid1, g1, u1)
    if ring:
        dg1, du1, d1, r_gu2, r_a2 = sync(dg1, du1, d1, r_gu2, r_a2)
        z_gu2 = ring.scatter_z(jnp.concatenate(add_one(keep_gu2, r_gu2), axis=1))
        keep_a2, go = add_core(a2, r_a2)
        r_a2 = ring.send(go, ("x", "y"))
        r_d1 = ring.send(d1[1:], ("core",))
    gu1 = gate_up_bwd(me, xf1, dg1, du1)
    if ring:
        gu1, r_a2, r_d1, r_d2 = sync(gu1, r_a2, r_d1, r_d2)
        keep_a2, go = add_two(keep_a2, r_a2)
        r_a2 = ring.send(go, ("y", "x"))
        keep_d2, go = near_rows(add_one(keep_d2, r_d2))
        r_d2 = ring.send(go, ("x", "y"))
        r_gu1 = ring.send(gu1[1::2], ("core", "core"))
        z_d1 = ring.scatter_z(d1[0] + r_d1[0])
    gm1, bo1, dou1, gg_m1 = mlp_dx(me, dg1, du1, w_g, w_u, hm1, gain_m1, gh1, w_o, f32)
    if ring:
        gm1, bo1, dou1, gg_m1, r_a2, r_gu1 = sync(gm1, bo1, dou1, gg_m1, r_a2, r_gu1)
        done_a2 = add_one(keep_a2, r_a2)
        keep_gu1, go = add_core(gu1, r_gu1)
        r_gu1 = ring.send(go, ("x", "y"))
    dqk1, dv1 = based_bwd(qk1, v1, dou1, ou1, rden1, seg_row, seg_col, live_col)
    if ring:
        dqk1, dv1, r_gu1, r_d2 = sync(dqk1, dv1, r_gu1, r_d2)
        sum_d2 = add_one(keep_d2, r_d2)
        keep_gu1, go = add_two(keep_gu1, r_gu1)
        r_gu1 = ring.send(go, ("y", "x"))
    *a1, g0, gg_a1 = attn_bwd(me, xa1, [dqk1, dv1], [w_qk, w_v], o1, bo1, start, gain_a1, gm1, HALVES_ONE)
    output = output[restore]
    gains = jnp.concatenate([gg_a1, gg_m1, gg_a2, gg_m2], axis=0)
    if ring:
        a1, g0, gains, r_gu1, z_gu2, z_d1 = sync(a1, g0, gains, r_gu1, z_gu2, z_d1)
        gu1 = jnp.concatenate(add_one(keep_gu1, r_gu1), axis=1)
        r_a1 = ring.send(a1[1::2], ("core", "core"))
        r_gains = ring.send([gains], ("core",))
        keep_d1, go = far_rows(z_d1)
        r_d1 = ring.send(go, ("y", "x"))
        r_z = ring.send_back(gu1)
        outgoing = g0.astype(bf16)[local_slots]
        r_a1, r_gains, r_d1, outgoing = sync(r_a1, r_gains, r_d1, outgoing)
        arrived = exchange(outgoing, rows)
        keep_a1, go = add_core(a1, r_a1)
        r_a1 = ring.send(go, ("x", "y"))
        gains = gains + r_gains[0]
        r_gains = ring.send([gains], ("x",))
        keep_d1, go = near_rows(add_one(keep_d1, r_d1))
        r_d1 = ring.send(go, ("x", "y"))
        r_a1, r_gains, r_d1, r_z = sync(r_a1, r_gains, r_d1, r_z)
        keep_a1, go = add_two(keep_a1, r_a1)
        r_a1 = ring.send(go, ("y", "x"))
        gains = gains + r_gains[0]
        r_gains = ring.send([gains], ("y",))
        sum_d1 = add_one(keep_d1, r_d1)
        last_gu1 = ring.add_back(gu1, r_z)
        r_a1, r_gains, arrived = sync(r_a1, r_gains, arrived)
        a1 = jnp.concatenate(add_one(keep_a1, r_a1), axis=1)
        last_a1 = ring.add_back(a1, ring.send_back(a1))
        gains = gains + r_gains[0]
        far_z = [ring.swap(gains, "z", by) for by in (1, 2, 3)]
        gains = (gains + far_z[0]) + (far_z[1] + far_z[2])
        z_a2 = ring.scatter_z(jnp.concatenate([after(v, z_d1) for v in done_a2], axis=1))
        z_a2 = after(z_a2, *far_z)
        cut = lambda v, n: [v[:n].astype(f32), v[n:].astype(f32)]
        sum_gu1, sum_a1 = cut(last_gu1, FC), cut(last_a1, 128 * len(HALVES_ONE[0]))
        sum_gu2, sum_a2 = cut(z_gu2, FC), cut(z_a2, done_a2[0].shape[1])
        tokens_grad = arrived
        wide = lambda halves: [h.astype(f32) for h in halves]
        sum_d1, sum_d2 = wide(sum_d1), wide(sum_d2)
        rest = sum_parts(sum_a2, sum_gu2, sum_d2, HALVES_TWO)
        sums1, sums2 = sum_parts(sum_a1, sum_gu1, sum_d1, HALVES_ONE), rest
        sums1 = [sums1[0][:, :64], sums1[0][:, 64:]] + sums1[1:]
        tokens_grad = tokens_grad[restore]
    else:
        sums1 = sum_any(d1, gu1, a1, HALVES_ONE)
        sums2 = sum_any(d2, gu2, a2, HALVES_TWO)
        gains = lax.psum(gains, ("row", "col"))
        tokens_grad = exchange(g0.astype(bf16)[local_slots], rows)[restore]
    return (
        output, tokens_grad,
        gains[0], *sums1[:4], gains[1], *sums1[4:],
        gains[2], *sums2[:4], gains[3], *sums2[4:],
    )


def solution(mesh):
    names, rows, cols = ("row", "col"), "row", "col"
    if (mesh.shape["row"], mesh.shape["col"]) == (ROWS, COLS):
        names = ("z", "y", "x", "core")
        rows, cols = names[:2], names[2:]
        mesh = Mesh(mesh.devices.reshape(4, 2, 2, 2), names)
    block, weight = P(names, None), P(rows, cols)
    layer_in = (P(),) + (weight,) * 4 + (P(),) + (weight,) * 3
    return jax.shard_map(
        functools.partial(body, names),
        mesh=mesh,
        in_specs=(block, block, P(), block, P(names)) + layer_in * 2,
        out_specs=(block, block) + layer_in * 2,
        check_vma=False,
    )
```

```python
import functools

import jax
import jax.numpy as jnp
from jax import lax
from jax.experimental import pallas as pl
from jax.experimental.pallas import tpu as pltpu
from jax.sharding import Mesh, PartitionSpec as P

HEADS = 16
FEAT = 16
HEAD_DIM = 64
WINDOW = 64
MAX_LEN = 256
D = 1024
T = 512
HALF = 256
EPS = 1e-05
NEG = -1e30
ROWS = 8
COLS = 4
FB = 344
FBP = 352
FFP = ROWS * FBP
FC = FFP // COLS

bf16, f32, i32 = jnp.bfloat16, jnp.float32, jnp.int32
NN, NT, TN = ((1,), (0,)), ((1,), (1,)), ((0,), (0,))


def dot(a, b, dims):
    return lax.dot_general(a, b, (dims, ((), ())), preferred_element_type=f32)


def call(body, grid, ins, outs, scratch=(), flops=0, prefetch=None):
    extra = 0 if prefetch is None else 1

    def spec(block, index):
        if block is None:
            return pl.BlockSpec(memory_space=pl.ANY)
        return pl.BlockSpec(block, index)

    in_specs, args = [], []
    for item in ins:
        if not isinstance(item, tuple):
            nd = item.ndim
            item = (item, item.shape, functools.partial(lambda n, *_: (0,) * n, nd))
        args.append(item[0])
        in_specs.append(spec(item[1], item[2]))
    out_specs = [spec(o[2], o[3]) for o in outs]
    out_shape = [jax.ShapeDtypeStruct(o[0], o[1]) for o in outs]
    moved = sum(a.size * a.dtype.itemsize for a in args)
    moved += sum(s.size * s.dtype.itemsize for s in out_shape)
    cost = pl.CostEstimate(flops=int(flops), bytes_accessed=int(moved), transcendentals=0)
    got = pl.pallas_call(
        body,
        out_shape=out_shape,
        grid_spec=pltpu.PrefetchScalarGridSpec(
            num_scalar_prefetch=extra,
            grid=grid,
            in_specs=in_specs,
            out_specs=out_specs,
            scratch_shapes=list(scratch),
        ),
        compiler_params=pltpu.CompilerParams(vmem_limit_bytes=56 * 2**20),
        cost_estimate=cost,
    )(*(([prefetch] if extra else []) + args))
    return got


def whole_map(*shape):
    zeros = (0,) * len(shape)
    return lambda *_: zeros


def norm_factor(h):
    return lax.rsqrt(jnp.mean(h * h, axis=-1, keepdims=True) + EPS)


class Strips:
    def __init__(self, half, swapped, at, n):
        self.bufs, self.swapped, self.at, self.n = half, swapped, at, n

    def scratch(self):
        return [pltpu.VMEM((2, 2, 2, 4, self.n, 128), bf16), pltpu.SemaphoreType.DMA((2, 2, 2))]

    def start(self, refs, box, sems):
        order = [(core, x, y) for core in range(2) for x in range(2) for y in range(2)]
        for core, x, y in order:
            hi, lo = (x, y) if self.swapped else (y, x)
            src = refs[core * 2 + hi].at[lo]
            if self.n != self.bufs[0].shape[2]:
                src = src.at[:, pl.ds(self.at, self.n)]
            pltpu.make_async_copy(src, box.at[core, hi, lo], sems.at[core, hi, lo]).start()

    def wait(self, box, sems, core, x):
        for y in range(2):
            hi, lo = (x, y) if self.swapped else (y, x)
            there = box.at[core, hi, lo]
            pltpu.make_async_copy(there, there, sems.at[core, hi, lo]).wait()

    def wait_all(self, box, sems):
        for core in range(2):
            for x in range(2):
                self.wait(box, sems, core, x)

    def piece(self, box, z, y, x, core):
        return box.at[core, x, y, z] if self.swapped else box.at[core, y, x, z]


class DownRows:
    def __init__(self, bufs):
        self.bufs = bufs

    def scratch(self):
        return [pltpu.VMEM((2, 4, FFP, 128), bf16), pltpu.SemaphoreType.DMA((2, 4))]

    def start(self, refs, box, sems):
        for z in range(4):
            for core in range(2):
                pltpu.make_async_copy(refs[core].at[z], box.at[core, z], sems.at[core, z]).start()

    def rows(self, box, sems, z, my):
        for core in range(2):
            there = box.at[core, z]
            pltpu.make_async_copy(there, there, sems.at[core, z]).wait()
        halves = []
        for y in range(2):
            parts = []
            for x, core in PLACES:
                for at in down_places(x, y ^ my):
                    parts.append(box[core, z, pl.ds(at, FBP), :])
            halves.append(jnp.concatenate(parts, axis=1))
        return jnp.concatenate(halves, axis=0)


def down_places(x, y):
    return [pl.multiple_of(p * FBP, 16) for p in (y * 2 + x, 4 + x * 2 + y)]


BLOCKS = [(z, y) for z in range(4) for y in range(2)]
PLACES = [(x, core) for x in range(2) for core in range(2)]


def step_place(i):
    return i % 2, i // 2


def step_col(i, me):
    return ((i % 2) * 2 + i // 2) ^ me[1]


def regroup(dst_ref, src_ref, count, me):
    width = D // count
    for j in range(count):
        at = pl.multiple_of((j ^ me) * width, 128)
        dst_ref[:, j * width : (j + 1) * width] = src_ref[:, pl.ds(at, width)]


class Kernel:
    def __init__(self, n_in, strips, n_out):
        self.n_in, self.strips, self.n_out = n_in, strips, n_out

    def split(self, refs):
        ins, refs = refs[: self.n_in], refs[self.n_in :]
        srcs = []
        for s in self.strips:
            srcs.append(refs[: len(s.bufs)])
            refs = refs[len(s.bufs) :]
        outs, refs = refs[: self.n_out], refs[self.n_out :]
        hold = [(s, srcs[j], refs[2 * j], refs[2 * j + 1]) for j, s in enumerate(self.strips)]
        return ins, hold, outs, refs[2 * len(self.strips) :]

    def ins(self):
        return [(b, None, None) for s in self.strips for b in s.bufs]

    def scratch(self):
        return [i for s in self.strips for i in s.scratch()]


def start_all(hold):
    for s, srcs, box, sems in hold:
        s.start(srcs, box, sems)


def col_block(s, box, x, core):
    strips = []
    for j in range(s.n // 128):
        strips.append(jnp.concatenate([s.piece(box, z, y, x, core)[j * 128 : (j + 1) * 128, :] for z, y in BLOCKS], axis=0))
    return strips[0] if len(strips) == 1 else jnp.concatenate(strips, axis=1)


def norm_proj(me, h, gain, strips):
    n = len(strips)
    kern = Kernel(2, strips, n + 1)

    def body(me_ref, *refs):
        (h_ref, gain_ref), hold, (xa_ref, *outs), (xr_ref,) = kern.split(refs)
        i = pl.program_id(0)

        @pl.when(i == 0)
        def _():
            start_all(hold)
            hv = h_ref[...].astype(f32)
            xa_ref[...] = (hv * norm_factor(hv) * gain_ref[...]).astype(bf16)
            regroup(xr_ref, xa_ref, ROWS, me_ref[0])

        x, core = step_place(i)
        for (s, _, box, sems), o_ref in zip(hold, outs):
            s.wait(box, sems, core, x)
            o_ref[...] = dot(xr_ref[...], col_block(s, box, x, core), NN).astype(bf16)

    outs = [((T, D), bf16, (T, D), whole_map(T, D))]
    for s in strips:
        outs.append(((T, s.n * COLS), bf16, (T, s.n), lambda i, me: (0, step_col(i, me))))
    total = sum(s.n * COLS for s in strips)
    return call(
        body, (COLS,), [h, gain.reshape(1, D)] + kern.ins(), outs,
        scratch=kern.scratch() + [pltpu.VMEM((T, D), bf16)], flops=2 * T * D * total, prefetch=me,
    )


def lanes(shape, width):
    return lax.broadcasted_iota(i32, shape, len(shape) - 1) // width


def fill_mask(mask_ref, seg_q, seg_k, live_k, q_axis, window):
    q = lax.broadcasted_iota(i32, (T, T), q_axis)
    k = lax.broadcasted_iota(i32, (T, T), 1 - q_axis)
    ok = (k <= q) & (k > q - window) & (seg_q == seg_k) & ((live_k > 0) | (k == q))
    mask_ref[...] = jnp.where(ok, 1.0, 0.0)


def based_fwd(qk, v, seg_row, seg_col, live_row):
    def body(qk_ref, v_ref, sr_ref, sc_ref, lr_ref, o_ref, ou_ref, rden_ref, mask_ref):
        @pl.when(pl.program_id(0) == 0)
        def _():
            fill_mask(mask_ref, sc_ref[...], sr_ref[...], lr_ref[...], 0, MAX_LEN)

        q4, k4 = qk_ref[:, 0:64], qk_ref[:, 64:128]
        qlane = lanes((T, 64), FEAT)
        first = lanes((HALF, 128), HEAD_DIM) == 0
        scaled = q4.astype(f32) * (FEAT**-0.5)
        for pair in range(2):
            v2 = v_ref[:, pair * 128 : pair * 128 + 128]
            for tb in range(2):
                t0, s1 = tb * HALF, (tb + 1) * HALF
                got = []
                for e in range(2):
                    qm = jnp.where(qlane == pair * 2 + e, scaled, 0.0).astype(bf16)
                    a = dot(qm[t0 : t0 + HALF], k4[0:s1], NT)
                    p = (1.0 + a * (1.0 + 0.5 * a)) * mask_ref[t0 : t0 + HALF, 0:s1]
                    den = jnp.sum(p, axis=-1, keepdims=True)
                    got.append((dot(p.astype(bf16), v2[0:s1], NN), den))
                rden = 1.0 / jnp.where(first, got[0][1], got[1][1])
                ou = jnp.where(first, got[0][0], got[1][0]) * rden
                at = (slice(t0, t0 + HALF), slice(pair * 128, pair * 128 + 128))
                ou_ref[at] = ou
                rden_ref[at] = rden
                o_ref[at] = ou.astype(bf16)

    wide = (T, 256)
    col = lambda c: (0, c)
    return call(
        body,
        (4,),
        [(qk, (T, 128), col), (v, wide, col), seg_row, seg_col, live_row],
        [((T, D), bf16, wide, col), ((T, D), f32, wide, col), ((T, D), f32, wide, col)],
        scratch=[pltpu.VMEM((T, T), f32)],
        flops=HEADS * T * T * 2 * 192,
    )


def based_bwd(qk, v, dou, ou, rden, seg_row, seg_col, live_col):
    def body(qk_ref, v_ref, dou_ref, ou_ref, rden_ref, sr_ref, sc_ref, lc_ref, dqk_ref, dv_ref, mask_ref, dk_ref, dva_ref):
        @pl.when(pl.program_id(0) == 0)
        def _():
            fill_mask(mask_ref, sr_ref[...], sc_ref[...], lc_ref[...], 1, MAX_LEN)

        q4, k4 = qk_ref[:, 0:64], qk_ref[:, 64:128]
        qlane = lanes((T, 64), FEAT)
        q_scaled = q4.astype(f32) * (FEAT**-0.5)
        k_scaled = k4.astype(f32) * (FEAT**-0.5)
        vlane = lanes((T, 128), HEAD_DIM)
        dnum_f = dou_ref[...] * rden_ref[...]
        term = dnum_f * ou_ref[...]
        high = term.astype(bf16)
        low = (term - high.astype(f32)).astype(bf16)
        pick = jnp.where(
            lax.broadcasted_iota(i32, (8, 256), 0) == lanes((8, 256), HEAD_DIM), 1.0, 0.0
        ).astype(bf16)
        dden = -(dot(pick, high, NT) + dot(pick, low, NT))
        dk_ref[...] = jnp.zeros((T, 64), f32)
        dva_ref[...] = jnp.zeros((T, 256), f32)
        dq = [jnp.zeros((HALF, 64), f32), jnp.zeros((HALF, 64), f32)]
        for pair in range(2):
            cols = slice(pair * 128, pair * 128 + 128)
            v2 = v_ref[:, cols]
            for e in range(2):
                head = pair * 2 + e
                qm = jnp.where(qlane == head, q_scaled, 0.0).astype(bf16)
                km = jnp.where(qlane == head, k_scaled, 0.0).astype(bf16)
                dn = jnp.where(vlane == e, dnum_f[:, cols], 0.0).astype(bf16)
                for tb in range(2):
                    t0, s1 = tb * HALF, (tb + 1) * HALF
                    at = slice(t0, t0 + HALF)
                    a = dot(k4[0:s1], qm[at], NT)
                    m = mask_ref[0:s1, at]
                    p = (1.0 + a * (1.0 + 0.5 * a)) * m
                    dp = dot(v2[0:s1], dn[at], NT) + dden[head : head + 1, at]
                    da = (dp * m * (1.0 + a)).astype(bf16)
                    dk_ref[0:s1, :] += dot(da, qm[at], NN)
                    dva_ref[0:s1, cols] += dot(p.astype(bf16), dn[at], NN)
                    dq[tb] += dot(da, km[0:s1], TN)
        for tb in range(2):
            at = slice(tb * HALF, tb * HALF + HALF)
            dqk_ref[at, 0:64] = dq[tb].astype(bf16)
        dqk_ref[:, 64:128] = dk_ref[...].astype(bf16)
        dv_ref[...] = dva_ref[...].astype(bf16)

    wide = (T, 256)
    col = lambda c: (0, c)
    return call(
        body,
        (4,),
        [(qk, (T, 128), col), (v, wide, col), (dou, wide, col), (ou, wide, col), (rden, wide, col), seg_row, seg_col, live_col],
        [((T, 512), bf16, (T, 128), col), ((T, D), bf16, wide, col)],
        scratch=[pltpu.VMEM((T, T), f32), pltpu.VMEM((T, 64), f32), pltpu.VMEM((T, 256), f32)],
        flops=HEADS * T * T * 2 * 480,
    )


SPAN = ((0, HALF), (HALF - WINDOW, T))


def window_fwd(q, k, v, seg_row, seg_col, live_col):
    def body(q_ref, k_ref, v_ref, sr_ref, sc_ref, lc_ref, o_ref, mask_ref):
        @pl.when(pl.program_id(0) == 0)
        def _():
            fill_mask(mask_ref, sr_ref[...], sc_ref[...], lc_ref[...], 1, WINDOW)

        first = lanes((HALF, 128), HEAD_DIM) == 0
        qlane = lanes((T, 128), HEAD_DIM)
        scaled = q_ref[...].astype(f32) * (HEAD_DIM**-0.5)
        for tb in range(2):
            at = slice(tb * HALF, tb * HALF + HALF)
            s0, s1 = SPAN[tb]
            ok = mask_ref[s0:s1, at] > 0.5
            got = []
            for e in range(2):
                qm = jnp.where(qlane == e, scaled, 0.0).astype(bf16)
                c = dot(k_ref[s0:s1, :], qm[at], NT)
                c = jnp.where(ok, c, NEG)
                w = jnp.exp(c - jnp.max(c, axis=0, keepdims=True))
                w = w * (1.0 / jnp.sum(w, axis=0, keepdims=True))
                got.append(dot(w.astype(bf16), v_ref[s0:s1, :], TN))
            o_ref[at, :] = jnp.where(first, got[0], got[1]).astype(bf16)

    blk = (T, 128)
    col = lambda c: (0, c)
    return call(
        body,
        (8,),
        [(q, blk, col), (k, blk, col), (v, blk, col), seg_row, seg_col, live_col],
        [((T, D), bf16, blk, col)],
        scratch=[pltpu.VMEM((T, T), f32)],
        flops=HEADS * T * T * 2 * 192,
    )[0]


def window_bwd(q, k, v, dor, seg_row, seg_col, live_col):
    def body(q_ref, k_ref, v_ref, do_ref, sr_ref, sc_ref, lc_ref, dq_ref, dk_ref, dv_ref, mask_ref, dka_ref, dva_ref):
        @pl.when(pl.program_id(0) == 0)
        def _():
            fill_mask(mask_ref, sr_ref[...], sc_ref[...], lc_ref[...], 1, WINDOW)

        lane = lanes((T, 128), HEAD_DIM)
        q_scaled = q_ref[...].astype(f32) * (HEAD_DIM**-0.5)
        k_scaled = k_ref[...].astype(f32) * (HEAD_DIM**-0.5)
        do = do_ref[...]
        dka_ref[...] = jnp.zeros((T, 128), f32)
        dva_ref[...] = jnp.zeros((T, 128), f32)
        for tb in range(2):
            at = slice(tb * HALF, tb * HALF + HALF)
            s0, s1 = SPAN[tb]
            ok = mask_ref[s0:s1, at] > 0.5
            dq = jnp.zeros((HALF, 128), f32)
            for e in range(2):
                qm = jnp.where(lane == e, q_scaled, 0.0).astype(bf16)
                km = jnp.where(lane == e, k_scaled, 0.0).astype(bf16)
                dm = jnp.where(lane == e, do, jnp.zeros_like(do))
                c = dot(k_ref[s0:s1, :], qm[at], NT)
                c = jnp.where(ok, c, NEG)
                w = jnp.exp(c - jnp.max(c, axis=0, keepdims=True))
                w = w * (1.0 / jnp.sum(w, axis=0, keepdims=True))
                dw = dot(v_ref[s0:s1, :], dm[at], NT)
                ds = (w * (dw - jnp.sum(w * dw, axis=0, keepdims=True))).astype(bf16)
                dka_ref[s0:s1, :] += dot(ds, qm[at], NN)
                dva_ref[s0:s1, :] += dot(w.astype(bf16), dm[at], NN)
                dq += dot(ds, km[s0:s1], TN)
            dq_ref[at, :] = dq.astype(bf16)
        dk_ref[...] = dka_ref[...].astype(bf16)
        dv_ref[...] = dva_ref[...].astype(bf16)

    blk = (T, 128)
    col = lambda c: (0, c)
    return call(
        body,
        (8,),
        [(q, blk, col), (k, blk, col), (v, blk, col), (dor, blk, col), seg_row, seg_col, live_col],
        [((T, D), bf16, blk, col)] * 3,
        scratch=[pltpu.VMEM((T, T), f32), pltpu.VMEM((T, 128), f32), pltpu.VMEM((T, 128), f32)],
        flops=HEADS * T * T * 2 * 480,
    )


def attn_out(me, h, o, strip, gain):
    kern = Kernel(3, [strip], 2)

    def body(me_ref, *refs):
        (h_ref, o_ref, gain_ref), hold, (hm_ref, xf_ref), (or_ref,) = kern.split(refs)
        i = pl.program_id(0)

        @pl.when(i == 0)
        def _():
            start_all(hold)
            regroup(or_ref, o_ref, ROWS, me_ref[0])

        x, core = step_place(i)
        s, _, box, sems = hold[0]
        s.wait(box, sems, core, x)
        at = pl.ds(pl.multiple_of(step_col(i, me_ref) * 256, 256), 256)
        hm_ref[:, at] = h_ref[:, at].astype(f32) + dot(or_ref[...], col_block(s, box, x, core), NN)

        @pl.when(i == COLS - 1)
        def _():
            hm = hm_ref[...]
            xf_ref[...] = (hm * norm_factor(hm) * gain_ref[...]).astype(bf16)

    full = whole_map(T, D)
    return call(
        body, (COLS,), [h, o, gain.reshape(1, D)] + kern.ins(),
        [((T, D), f32, (T, D), full), ((T, D), bf16, (T, D), full)],
        scratch=kern.scratch() + [pltpu.VMEM((T, D), bf16)], flops=2 * T * D * D, prefetch=me,
    )


def hidden_block(s, box, x, core):
    return jnp.concatenate([s.piece(box, z, y, x, core)[...] for z, y in BLOCKS], axis=1)


def gate_up(me, xf, w_gate, w_up):
    kern = Kernel(1, [w_gate, w_up], 3)

    def body(me_ref, *refs):
        (xf_ref,), hold, (g_ref, u_ref, hid_ref), (xr_ref,) = kern.split(refs)
        i = pl.program_id(0)

        @pl.when(i == 0)
        def _():
            start_all(hold)
            regroup(xr_ref, xf_ref, ROWS, me_ref[0])

        x, core = step_place(i)
        got = []
        for s, _, box, sems in hold:
            s.wait(box, sems, core, x)
            got.append(dot(hidden_block(s, box, x, core), xr_ref[...], NT))
        g, u = got
        g_ref[...] = g.astype(bf16)
        u_ref[...] = u.astype(bf16)
        hid_ref[...] = (g * (1.0 / (1.0 + jnp.exp(-g))) * u).astype(bf16)

    row = lambda i, me: (step_col(i, me), 0)
    return call(
        body, (COLS,), [xf] + kern.ins(), [((FFP, T), bf16, (FC, T), row)] * 3,
        scratch=kern.scratch() + [pltpu.VMEM((T, D), bf16)], flops=4 * T * D * FFP, prefetch=me,
    )


def down(me, hm, hid, w_down):
    kern = Kernel(2, [w_down], 1)

    def body(me_ref, *refs):
        (hm_ref, hid_ref), hold, (h_ref,), (acc_ref,) = kern.split(refs)
        i = pl.program_id(0)

        @pl.when(i == 0)
        def _():
            start_all(hold)
            regroup(acc_ref, hm_ref, COLS, me_ref[1])

        s, _, box, sems = hold[0]
        acc_ref[...] += dot(hid_ref[...], s.rows(box, sems, i, me_ref[0]), TN)

        @pl.when(i == COLS - 1)
        def _():
            regroup(h_ref, acc_ref, COLS, me_ref[1])

    return call(
        body, (COLS,), [hm, (hid, (FC, T), lambda i, me: (i, 0))] + kern.ins(),
        [((T, D), f32, (T, D), whole_map(T, D))],
        scratch=kern.scratch() + [pltpu.VMEM((T, D), f32)], flops=2 * T * D * FFP, prefetch=me,
    )[0]


def down_bwd(me, bd, w_down, hid, g, u):
    kern = Kernel(4, [w_down], 4)

    def body(me_ref, *refs):
        (bd_ref, hid_ref, g_ref, u_ref), hold, (dg_ref, du_ref, *p_refs), (br_ref,) = kern.split(refs)
        i = pl.program_id(0)

        @pl.when(i == 0)
        def _():
            start_all(hold)
            regroup(br_ref, bd_ref, COLS, me_ref[1])

        bdv = br_ref[...].astype(bf16)
        gwd = dot(hid_ref[...], bdv, NN).astype(bf16)
        for x, core in PLACES:
            at = (x * 2 + core) * 256
            for y in range(2):
                rows = slice(y * FBP, (y + 1) * FBP)
                for half, to in enumerate(down_places(x, y ^ me_ref[0])):
                    p_refs[core][0, pl.ds(to, FBP), :] = gwd[rows, at + half * 128 : at + half * 128 + 128]
        s, _, box, sems = hold[0]
        dhid = dot(s.rows(box, sems, i, me_ref[0]), bdv, NT)
        gv, uv = g_ref[...].astype(f32), u_ref[...].astype(f32)
        sig = 1.0 / (1.0 + jnp.exp(-gv))
        act = gv * sig
        du_ref[...] = (dhid * act).astype(bf16)
        dg_ref[...] = (dhid * uv * (sig + act * (1.0 - sig))).astype(bf16)

    row = lambda i, me: (i, 0)
    hblk = (FC, T)
    pieces = ((4, FFP, 128), bf16, (1, FFP, 128), lambda i, me: (i, 0, 0))
    return call(
        body, (COLS,), [bd, (hid, hblk, row), (g, hblk, row), (u, hblk, row)] + kern.ins(),
        [((FFP, T), bf16, hblk, row), ((FFP, T), bf16, hblk, row)] + [pieces] * 2,
        scratch=kern.scratch() + [pltpu.VMEM((T, D), bd.dtype)], flops=4 * T * D * FFP, prefetch=me,
    )


def piece_specs(n1, n2):
    out = []
    for n, block, place in ((n1, (1, 2, 4), lambda j: (j, 0)), (n2, (2, 1, 4), lambda j: (0, j))):
        for step in (lambda i: jnp.minimum(i, 1), lambda i: jnp.maximum(i - 2, 0)):
            index = functools.partial(lambda place, step, i, me: (*place(step(i)), 0, 0, 0), place, step)
            out.append(((2, 2, 4, n, 128), bf16, (*block, n, 128), index))
    return out


def for_core(refs, write):
    for core in range(2):

        @pl.when(pl.program_id(0) // 2 == core)
        def _():
            write(refs[core], refs[2 + core])


def gate_up_bwd(me, xf, dg, du):
    def body(me_ref, xf_ref, dg_ref, du_ref, *refs):
        *p_refs, xr_ref = refs

        @pl.when(pl.program_id(0) == 0)
        def _():
            regroup(xr_ref, xf_ref, ROWS, me_ref[0])

        gwg = dot(dg_ref[...], xr_ref[...], NN).astype(bf16)
        gwu = dot(du_ref[...], xr_ref[...], NN).astype(bf16)

        def write(one, two):
            for r, (z, y) in enumerate(BLOCKS):
                one[0, y, z] = gwg[:, r * 128 : (r + 1) * 128]
                two[y, 0, z] = gwu[:, r * 128 : (r + 1) * 128]

        for_core(p_refs, write)

    row = lambda i, me: (step_col(i, me), 0)
    return call(
        body, (COLS,), [xf, (dg, (FC, T), row), (du, (FC, T), row)], piece_specs(FC, FC),
        scratch=[pltpu.VMEM((T, D), bf16)], flops=4 * T * D * FFP, prefetch=me,
    )


def norm_bwd(dx, h, gain, g):
    rf = norm_factor(h)
    hr = h * rf
    dgain = jnp.sum(dx * hr, axis=0, keepdims=True)
    gd = gain * dx
    mean = jnp.sum(gd * hr, axis=-1, keepdims=True) * (1.0 / D)
    return dgain, g + rf * (gd - hr * mean)


def add_to(acc_ref, part):
    @pl.when(pl.program_id(0) == 0)
    def _():
        acc_ref[...] = part

    @pl.when(pl.program_id(0) > 0)
    def _():
        acc_ref[...] += part


def mlp_dx(me, dg, du, w_gate, w_up, hm, gain, g, w_out, kind):
    kern = Kernel(5, [w_gate, w_up, w_out], 4)

    def body(me_ref, *refs):
        (dg_ref, du_ref, hm_ref, gain_ref, g_ref), hold, outs, rest = kern.split(refs)
        acc_ref, un_ref, br_ref, hl_ref, gl_ref, late = rest
        gm_ref, bo_ref, dou_ref, gg_ref = outs
        i = pl.program_id(0)

        @pl.when(i == 0)
        def _():
            start_all(hold)
            for k, (src, dst) in enumerate(((hm_ref, hl_ref), (g_ref, gl_ref))):
                pltpu.make_async_copy(src, dst, late.at[k]).start()

        x, core = step_place(i)
        part = None
        for (s, _, box, sems), d_ref in zip(hold[:2], (dg_ref, du_ref)):
            s.wait(box, sems, core, x)
            term = dot(d_ref[...], hidden_block(s, box, x, core), TN)
            part = term if part is None else part + term
        add_to(acc_ref, part)

        @pl.when(i == COLS - 1)
        def _():
            regroup(un_ref, acc_ref, ROWS, me_ref[0])
            for k, (src, dst) in enumerate(((hm_ref, hl_ref), (g_ref, gl_ref))):
                pltpu.make_async_copy(src, dst, late.at[k]).wait()
            gg, gm = norm_bwd(un_ref[...], hl_ref[...], gain_ref[...], gl_ref[...].astype(f32))
            gg_ref[...] = gg
            gm_ref[...] = gm
            bo_ref[...] = gm.astype(bf16)
            regroup(br_ref, bo_ref, COLS, me_ref[1])
            s, _, box, sems = hold[2]
            s.wait_all(box, sems)
            w = jnp.concatenate([col_block(s, box, x, core) for x, core in PLACES], axis=1)
            acc_ref[...] = dot(br_ref[...], w, NT)
            regroup(un_ref, acc_ref, ROWS, me_ref[0])
            dou_ref[...] = un_ref[...].astype(kind)

    row = lambda i, me: (step_col(i, me), 0)
    full = whole_map(T, D)
    return call(
        body, (COLS,), [(dg, (FC, T), row), (du, (FC, T), row), (hm, None, None), gain.reshape(1, D), (g, None, None)] + kern.ins(),
        [((T, D), f32, (T, D), full), ((T, D), bf16, (T, D), full), ((T, D), kind, (T, D), full), ((1, D), f32, (1, D), full)],
        scratch=kern.scratch()
        + [pltpu.VMEM((T, D), f32), pltpu.VMEM((T, D), f32), pltpu.VMEM((T, D), bf16)]
        + [pltpu.VMEM((T, D), f32), pltpu.VMEM((T, D), g.dtype), pltpu.SemaphoreType.DMA((2,))],
        flops=4 * T * D * FFP + 2 * T * D * D, prefetch=me,
    )


def attn_bwd(me, xa, grads, strips, o, bo, h, gain, gm, halves):
    n = len(grads)
    kern = Kernel(6 + n, strips, 6)

    def body(me_ref, *refs):
        ins, hold, (*p_refs, g_ref, gg_ref), rest = kern.split(refs)
        xr_ref, or_ref, xt_ref, ot_ref, acc_ref, hl_ref, gl_ref, late = rest
        xa_ref, o_ref, h_ref, gain_ref, gm_ref, bo_ref, *d_refs = ins
        i = pl.program_id(0)

        @pl.when(i == 0)
        def _():
            start_all(hold)
            regroup(xr_ref, xa_ref, ROWS, me_ref[0])
            regroup(or_ref, o_ref, ROWS, me_ref[0])
            for k, (src, dst) in enumerate(((h_ref, hl_ref), (gm_ref, gl_ref))):
                pltpu.make_async_copy(src, dst, late.at[k]).start()
            xt_ref[...] = xr_ref[...].T
            ot_ref[...] = or_ref[...].T

        tiles = [dot(xt_ref[...], d[...], NN).astype(bf16) for d in d_refs]
        tiles.append(dot(ot_ref[...], bo_ref[...], NN).astype(bf16))

        def write(one, two):
            for j, (which, at) in enumerate(halves[0]):
                for r, (z, y) in enumerate(BLOCKS):
                    one[0, y, z, j * 128 : (j + 1) * 128] = tiles[which][r * 128 : (r + 1) * 128, at : at + 128]
            for j, (which, at) in enumerate(halves[1]):
                for r, (z, y) in enumerate(BLOCKS):
                    two[y, 0, z, j * 128 : (j + 1) * 128] = tiles[which][r * 128 : (r + 1) * 128, at : at + 128]

        for_core(p_refs, write)
        x, core = step_place(i)
        part = None
        for (s, _, box, sems), d in zip(hold, d_refs):
            s.wait(box, sems, core, x)
            term = dot(d[...], col_block(s, box, x, core), NT)
            part = term if part is None else part + term
        add_to(acc_ref, part)

        @pl.when(i == COLS - 1)
        def _():
            regroup(g_ref, acc_ref, ROWS, me_ref[0])
            for k, (src, dst) in enumerate(((h_ref, hl_ref), (gm_ref, gl_ref))):
                pltpu.make_async_copy(src, dst, late.at[k]).wait()
            gg, g = norm_bwd(g_ref[...], hl_ref[...].astype(f32), gain_ref[...], gl_ref[...])
            gg_ref[...] = gg
            g_ref[...] = g

    col = lambda i, me: (0, step_col(i, me))
    full = whole_map(T, D)
    ins = [xa, o, (h, None, None), gain.reshape(1, D), (gm, None, None), (bo, (T, 256), col)]
    ins += [(d, (T, d.shape[1] // COLS), col) for d in grads]
    total = sum(d.shape[1] for d in grads)
    return call(
        body, (COLS,), ins + kern.ins(),
        piece_specs(128 * len(halves[0]), 128 * len(halves[1])) + [((T, D), f32, (T, D), full), ((1, D), f32, (1, D), full)],
        scratch=kern.scratch()
        + [pltpu.VMEM((T, D), bf16)] * 2
        + [pltpu.VMEM((D, T), bf16)] * 2
        + [pltpu.VMEM((T, D), f32), pltpu.VMEM((T, D), h.dtype), pltpu.VMEM((T, D), f32), pltpu.SemaphoreType.DMA((2,))],
        flops=4 * T * D * total + 2 * T * D * D, prefetch=me,
    )


HALVES_ONE = (((1, 0), (1, 128)), ((0, 0), (2, 0), (2, 128)))
HALVES_TWO = (((0, 0), (0, 128), (1, 0), (1, 128)), ((2, 0), (2, 128), (3, 0), (3, 128)))


def attn_weights(bufs, halves):
    out = []
    for which in range(1 + max(w for half in halves for w, _ in half)):
        for k, half in enumerate(halves):
            at = [j for j, (w, _) in enumerate(half) if w == which]
            if at:
                out.append(Strips(bufs[k], k == 1, at[0] * 128, len(at) * 128))
    return out


def gate_weights(bufs):
    return Strips(bufs[0], False, 0, FC), Strips(bufs[1], True, 0, FC)


def pad_hidden(w):
    k = w.shape[0]
    return jnp.pad(w.reshape(k, -1, FB), ((0, 0), (0, 0), (0, FBP - FB))).reshape(k, -1).T


def pad_rows(w):
    n = w.shape[1]
    return jnp.pad(w.reshape(-1, FB, n), ((0, 0), (0, FBP - FB), (0, 0))).reshape(-1, n)


def strips_of(blocks, halves):
    return tuple(
        jnp.concatenate([blocks[which][..., at : at + 128] for which, at in strips], axis=-2) for strips in halves
    )


def after(value, *arrays):
    return lax.optimization_barrier((value, *arrays))[0] if arrays else value


def sync(*groups):
    flat, tree = jax.tree.flatten(groups)
    return jax.tree.unflatten(tree, lax.optimization_barrier(flat))


def add_core(four, got):
    keep = [four[0][0] + got[0][0], four[2][0] + got[1][0]]
    return keep, [four[0][1] + got[0][1], four[2][1] + got[1][1]]


def add_two(keep, got):
    return [k[0] + g[0] for k, g in zip(keep, got)], [k[1] + g[1] for k, g in zip(keep, got)]


def add_one(keep, got):
    return [k + g for k, g in zip(keep, got)]


def far_rows(total):
    parts = jnp.split(total, 4, axis=-2)
    return parts[0::2], parts[1::2]


def near_rows(halves):
    parts = [jnp.split(h, 2, axis=-2) for h in halves]
    return [p[0] for p in parts], [p[1] for p in parts]


class Ring:
    def __init__(self, names):
        self.axes = names
        self.z = lax.axis_index(names[0])

    def swap(self, value, axis, by=1):
        shift = {"z": 3, "y": 2, "x": 1, "core": 0}[axis]
        return lax.ppermute(value, self.axes, [(i, i ^ (by << shift)) for i in range(32)])

    def gather_z(self, both, *behind):
        near = [both] + [after(self.swap(both, "z", by), *behind) for by in (1, 2, 3)]
        low, high = self.z % 2 == 1, self.z >= 2
        a, b = jnp.where(low, near[1], near[0]), jnp.where(low, near[0], near[1])
        c, d = jnp.where(low, near[3], near[2]), jnp.where(low, near[2], near[3])
        pick = lambda p, q: jnp.where(high, q, p)
        return jnp.stack([pick(a, c), pick(b, d), pick(c, a), pick(d, b)])

    def gather_z_all(self, both):
        return lax.all_gather(both, self.axes[0], axis=0, tiled=False)

    def gather_lo(self, pair, *behind):
        got = [after(self.swap(v, axis), *behind) for v, axis in zip(pair, ("x", "y"))]
        return [jnp.stack([v, g]) for v, g in zip(pair, got)]

    def gather_hi(self, pair, *behind):
        return [[v, after(self.swap(v, axis), *behind)] for v, axis in zip(pair, ("y", "x"))]

    def gather_core(self, full, *behind):
        return [half + [after(self.swap(b, "core"), *behind) for b in half] for half in full]

    def gather_down(self, pair):
        return jnp.stack([jnp.stack(half) for half in self.gather_hi(self.gather_lo(pair))]).reshape(-1, 128)

    def scatter_z(self, value):
        return lax.psum_scatter(value, self.axes[0], scatter_dimension=0, tiled=False)

    def send(self, values, axes):
        return [self.swap(v, axis) for v, axis in zip(values, axes)]

    def send_back(self, value):
        part = lambda by: lax.dynamic_index_in_dim(value, self.z ^ by, 0, False)
        return [self.swap(part(by), "z", by) for by in (1, 2, 3)]

    def add_back(self, value, got):
        total = lax.dynamic_index_in_dim(value, self.z, 0, False).astype(f32)
        for g in got:
            total = total + g.astype(f32)
        return total

    def reduce_z_all(self, pair):
        n1 = pair[0].shape[1]
        both = jnp.concatenate(pair, axis=1)
        total = lax.psum_scatter(both, self.axes[0], scatter_dimension=0, tiled=False).astype(f32)
        return total[:n1], total[n1:]


def pack(shards, halves):
    *attn, gate, up, dn = shards
    dp = pad_rows(dn)
    return [strips_of(attn, halves), (pad_hidden(gate), pad_hidden(up)), (dp[:, :128], dp[:, 128:])]


def boxes_any(weights, halves):
    *attn, gate, up, dn = weights

    def cut(w, rows, cols):
        return w.reshape(4, 2, rows, 2, 2, cols).transpose(0, 1, 3, 4, 2, 5)

    def boxes(one, two):
        first = [one[:, y, :, core].transpose(1, 0, 2, 3) for core in range(2) for y in range(2)]
        second = [two[:, :, x, core].transpose(1, 0, 2, 3) for core in range(2) for x in range(2)]
        return first, second

    a = boxes(*strips_of([cut(w, D // ROWS, w.shape[1] // COLS) for w in attn], halves))
    hidden = lambda w: pad_hidden(w).reshape(2, 2, FC, 4, 2, 128).transpose(3, 4, 0, 1, 2, 5)
    d = cut(pad_rows(dn), FBP, 256)
    one = d[..., :128].transpose(3, 0, 1, 2, 4, 5)
    two = d[..., 128:].transpose(3, 0, 2, 1, 4, 5)
    d = jnp.stack([one, two], axis=2).reshape(2, 4, FFP, 128)
    return [a, boxes(hidden(gate), hidden(up)), [d[0], d[1]]]


def unpad_hidden(g):
    k = g.shape[1]
    return g.reshape(-1, FBP, k)[:, :FB].reshape(-1, k).T


def unpad_rows(g):
    n = g.shape[1]
    return g.reshape(-1, FBP, n)[:, :FB].reshape(-1, n)


def whole_grad(own, send, swapped):
    p = jnp.stack([own, send])
    if swapped:
        p = jnp.swapaxes(p, 1, 2)
    core, x, y, z, n, w = p.shape
    return p.transpose(3, 2, 1, 0, 4, 5).reshape(z * y, x * core, n, w)


def join_strips(one, two, halves):
    out = []
    for which in range(1 + max(w for half in halves for w, _ in half)):
        got = {}
        for src, strips in ((one, halves[0]), (two, halves[1])):
            for j, (w, at) in enumerate(strips):
                if w == which:
                    got[at] = src[..., j * 128 : j * 128 + 128, :]
        out.append(jnp.concatenate([got[a] for a in sorted(got)], axis=-1))
    return out


def sum_parts(a, gu, d, halves):
    return join_strips(*a, halves) + [unpad_hidden(gu[0]), unpad_hidden(gu[1]), unpad_rows(jnp.concatenate(d, axis=1))]


def scatter_any(w):
    part = lax.psum_scatter(w, "row", scatter_dimension=0, tiled=True)
    return lax.psum_scatter(part, "col", scatter_dimension=1, tiled=True).astype(f32)


def natural(blocks):
    r, c, n, w = blocks.shape
    return blocks.transpose(0, 2, 1, 3).reshape(r * n, c * w)


def sum_any(pd, pgu, pa, halves):
    pairs = lambda p: (whole_grad(*p[:2], False), whole_grad(*p[2:], True))
    one, two = jnp.split(jnp.stack(pd).reshape(2, 4, 2, 2, 2, FBP, 128), 2, axis=2)
    dn = jnp.concatenate([one[:, :, 0], jnp.swapaxes(two[:, :, 0], 2, 3)], axis=-1)
    dn = dn.transpose(1, 2, 3, 0, 4, 5).reshape(ROWS, COLS, FBP, 256)
    dn = scatter_any(unpad_rows(natural(dn)))
    gu = [scatter_any(unpad_hidden(g.transpose(1, 2, 0, 3).reshape(FFP, D))) for g in pairs(pgu)]
    blocks = join_strips(*pairs(pa), halves)
    if len(blocks) == 3:
        blocks = [blocks[0][..., :64], blocks[0][..., 64:]] + blocks[1:]
    return [scatter_any(natural(b)) for b in blocks] + gu + [dn]


def join_qk(q, k, parts):
    n = q.shape[0]
    both = jnp.concatenate([q.reshape(n, parts, -1), k.reshape(n, parts, -1)], axis=2)
    return both.reshape(n, -1)

def route_plan(dest_slot, block_tokens, rows, cols):
    row_count = lax.axis_size(rows)
    col_count = lax.axis_size(cols)
    per_peer = block_tokens // row_count
    row_at = lax.axis_index(rows)
    col_at = lax.axis_index(cols)
    slot_table = dest_slot.reshape(row_count, col_count, block_tokens)
    column = lax.dynamic_index_in_dim(slot_table, col_at, 1, False)
    own_slots = lax.dynamic_index_in_dim(column, row_at, 0, False)
    send_order = jnp.argsort(own_slots)
    arrived = jnp.sort(column, axis=1)
    incoming = lax.dynamic_slice_in_dim(arrived, row_at * per_peer, per_peer, 1)
    local_slots = incoming.reshape(-1) - (row_at * col_count + col_at) * block_tokens
    placing = jnp.argsort(local_slots)
    return (send_order, local_slots, placing)


def exchange(value, axis):
    n, width = value.shape
    row_count = lax.axis_size(axis)
    got = lax.all_to_all(value.reshape(row_count, n // row_count, width), axis, split_axis=0, concat_axis=0, tiled=True)
    return got.reshape(n, width)


def gather_all(shards):
    return [lax.all_gather(lax.all_gather(w, "col", axis=1, tiled=True), "row", axis=0, tiled=True) for w in shards]


def body(names, tokens, cotangent, dest_slot, lengths, pad_mask, *params):
    ring = Ring(names) if len(names) == 4 else None
    rows, cols = (names[:2], names[2:]) if ring else names
    gain_a1, bq, bk, bv, bo_w, gain_m1, wg1, wu1, wd1 = params[:9]
    gain_a2, wq, wk, wv, wo2, gain_m2, wg2, wu2, wd2 = params[9:]
    shards1, shards2 = [bq, bk, bv, bo_w, wg1, wu1, wd1], [wq, wk, wv, wo2, wg2, wu2, wd2]
    send_order, local_slots, placing = route_plan(dest_slot, T, rows, cols)
    restore = jnp.argsort(send_order)
    outgoing = after(tokens[send_order], restore, placing) if ring else tokens[send_order]
    cot_going = cotangent[send_order]
    if ring:
        me = jnp.stack([lax.axis_index(names[1]), lax.axis_index(cols)]).astype(i32)
        packs = pack([join_qk(bq, bk, 1)] + shards1[2:], HALVES_ONE) + pack(shards2, HALVES_TWO)
        flat = [jnp.concatenate(p, axis=0) for p in packs]
        mid_d2 = ring.gather_down(packs[5])
        split = lambda k, v: [v[:, : packs[k][0].shape[0]], v[:, packs[k][0].shape[0] :]]
        each = lambda pair, *arrays: [after(v, *arrays) for v in pair]
        far = lambda halves: [half[1] for half in halves]
        near_a1 = ring.gather_z(flat[0])
        hi_a1 = ring.gather_hi(ring.gather_lo(each(split(0, near_a1), mid_d2)))
        near_gu1 = ring.gather_z(after(flat[1], near_a1))
        lo_gu1 = ring.gather_lo(each(split(1, near_gu1), *far(hi_a1)))
        outgoing = after(outgoing, near_gu1, *far(hi_a1))
        arrived = exchange(outgoing, rows)
        near_d1 = ring.gather_z(after(flat[2], arrived))
        start = arrived[placing]
    else:
        me = jnp.zeros((2,), i32)
        one, two = gather_all(shards1), gather_all(shards2)
        full = boxes_any([join_qk(one[0], one[1], COLS)] + one[2:], HALVES_ONE) + boxes_any(two, HALVES_TWO)
        start = exchange(outgoing, rows)[placing]
    position = jnp.arange(T, dtype=i32)
    segment, end = jnp.zeros((T,), i32), jnp.zeros((), i32)
    for j in range(lengths.shape[1]):
        end = end + lengths[0, j]
        segment = segment + (position >= end).astype(i32)
    seg_row, seg_col = segment.reshape(1, T), segment.reshape(T, 1)
    live_row, live_col = pad_mask.reshape(1, T), pad_mask.reshape(T, 1)

    tied = after if ring else (lambda value, *arrays: value)
    if ring:
        full_a1 = ring.gather_core(hi_a1)
        start = after(start, *lo_gu1)
    else:
        full_a1 = full[0]
    w_qk, w_v, w_o = attn_weights(full_a1, HALVES_ONE)
    xa1, qk1, v1 = norm_proj(me, start, gain_a1, [w_qk, w_v])
    o1, ou1, rden1 = based_fwd(qk1, v1, seg_row, seg_col, live_row)
    if ring:
        hi_gu1 = ring.gather_hi(lo_gu1, o1)
        near_a2 = ring.gather_z(after(flat[3], near_d1), o1)
    hm1, xf1 = attn_out(me, start, tied(o1, *(far(hi_gu1) + [near_a2] if ring else [])), w_o, gain_m1)
    if ring:
        full_gu1 = ring.gather_core(hi_gu1, xf1)
        lo_d1 = ring.gather_lo(each(split(2, near_d1), *far(hi_gu1)), xf1)
        xf1_late = after(xf1, *lo_d1)
    else:
        full_gu1, xf1_late = full[1], xf1
    w_g, w_u = gate_weights(full_gu1)
    g1, u1, hid1 = gate_up(me, xf1_late, w_g, w_u)
    if ring:
        hi_d1 = ring.gather_hi(lo_d1, hid1)
        lo_a2 = ring.gather_lo(each(split(3, near_a2), *lo_d1), hid1)
        near_gu2 = ring.gather_z(after(flat[4], near_a2), hid1)
        own_d1 = jnp.stack([jnp.stack(half) for half in hi_d1]).transpose(3, 0, 1, 2, 4, 5).reshape(4, FFP, 128)
        full_d1 = [own_d1, ring.swap(own_d1, "core")]
        hid1_late = after(hid1, *lo_a2)
        all_d2 = ring.gather_z_all(after(mid_d2, near_gu2))
        cot_going = after(cot_going, near_gu2)
    else:
        full_d1, hid1_late = full[2], hid1
    cot = exchange(cot_going, rows)[placing]
    w_d = DownRows(full_d1)
    h1 = down(me, hm1, hid1_late, w_d)
    if ring:
        hi_a2 = ring.gather_hi(lo_a2, h1)
        full_a2 = ring.gather_core(hi_a2)
        lo_gu2 = each(split(4, near_gu2), *far(hi_a2))
    else:
        full_a2 = full[3]
    v_q, v_k, v_v, v_o = attn_weights(full_a2, HALVES_TWO)
    xa2, q2, k2, v2 = norm_proj(me, h1, gain_a2, [v_q, v_k, v_v])
    if ring:
        lo_gu2 = ring.gather_lo(lo_gu2, q2)
    o2 = window_fwd(tied(q2, *(lo_gu2 if ring else [])), k2, v2, seg_row, seg_col, live_col)
    hm2, xf2 = attn_out(me, h1, o2, v_o, gain_m2)
    if ring:
        full_gu2 = ring.gather_core(ring.gather_hi(lo_gu2, xf2))
    else:
        full_gu2 = full[4]
    v_g, v_u = gate_weights(full_gu2)
    v_d = DownRows([all_d2, after(ring.swap(all_d2, "core"), xf2)] if ring else full[5])
    g2, u2, hid2 = gate_up(me, xf2, v_g, v_u)

    dg2, du2, *d2 = down_bwd(me, cot, v_d, hid2, g2, u2)
    if ring:
        r_d2 = ring.send(d2[1:], ("core",))
    h2 = down(me, hm2, hid2, v_d)
    outgoing = h2.astype(bf16)[local_slots]
    gu2 = gate_up_bwd(me, xf2, dg2, du2)
    if ring:
        dg2, du2, gu2, r_d2, outgoing = sync(dg2, du2, gu2, r_d2, outgoing)
        z_d2 = ring.scatter_z(d2[0] + r_d2[0])
        r_gu2 = ring.send(gu2[1::2], ("core", "core"))
    output = exchange(outgoing, rows)
    gm2, bo2, dor2, gg_m2 = mlp_dx(me, dg2, du2, v_g, v_u, hm2, gain_m2, cot, v_o, bf16)
    if ring:
        gm2, bo2, dor2, gg_m2, r_gu2 = sync(gm2, bo2, dor2, gg_m2, r_gu2)
        keep_gu2, go = add_core(gu2, r_gu2)
        r_gu2 = ring.send(go, ("x", "y"))
    dq2, dk2, dv2 = window_bwd(q2, k2, v2, dor2, seg_row, seg_col, live_col)
    *a2, gh1, gg_a2 = attn_bwd(me, xa2, [dq2, dk2, dv2], [v_q, v_k, v_v], o2, bo2, h1, gain_a2, gm2, HALVES_TWO)
    if ring:
        a2, gh1, gg_a2, r_gu2, z_d2, output = sync(a2, gh1, gg_a2, r_gu2, z_d2, output)
        keep_gu2, go = add_two(keep_gu2, r_gu2)
        r_gu2 = ring.send(go, ("y", "x"))
        r_a2 = ring.send(a2[1::2], ("core", "core"))
    dg1, du1, *d1 = down_bwd(me, gh1, w_d, hid1, g1, u1)
    if ring:
        dg1, du1, d1, r_gu2, r_a2 = sync(dg1, du1, d1, r_gu2, r_a2)
        z_gu2 = ring.scatter_z(jnp.concatenate(add_one(keep_gu2, r_gu2), axis=1))
        keep_a2, go = add_core(a2, r_a2)
        r_a2 = ring.send(go, ("x", "y"))
        r_d1 = ring.send(d1[1:], ("core",))
    gu1 = gate_up_bwd(me, xf1, dg1, du1)
    if ring:
        gu1, r_a2, r_d1 = sync(gu1, r_a2, r_d1)
        keep_a2, go = add_two(keep_a2, r_a2)
        r_a2 = ring.send(go, ("y", "x"))
        r_gu1 = ring.send(gu1[1::2], ("core", "core"))
        z_d1 = ring.scatter_z(d1[0] + r_d1[0])
    gm1, bo1, dou1, gg_m1 = mlp_dx(me, dg1, du1, w_g, w_u, hm1, gain_m1, gh1, w_o, f32)
    if ring:
        gm1, bo1, dou1, gg_m1, r_a2, r_gu1 = sync(gm1, bo1, dou1, gg_m1, r_a2, r_gu1)
        n_a2 = keep_a2[0].shape[1]
        z_a2 = ring.scatter_z(jnp.concatenate(add_one(keep_a2, r_a2), axis=1))
        keep_gu1, go = add_core(gu1, r_gu1)
        r_gu1 = ring.send(go, ("x", "y"))
    dqk1, dv1 = based_bwd(qk1, v1, dou1, ou1, rden1, seg_row, seg_col, live_col)
    if ring:
        dqk1, dv1, r_gu1 = sync(dqk1, dv1, r_gu1)
        keep_gu1, go = add_two(keep_gu1, r_gu1)
        r_gu1 = ring.send(go, ("y", "x"))
    *a1, g0, gg_a1 = attn_bwd(me, xa1, [dqk1, dv1], [w_qk, w_v], o1, bo1, start, gain_a1, gm1, HALVES_ONE)
    output = output[restore]
    gains = jnp.concatenate([gg_a1, gg_m1, gg_a2, gg_m2], axis=0)
    if ring:
        a1, g0, gains, r_gu1, z_gu2, z_d1 = sync(a1, g0, gains, r_gu1, z_gu2, z_d1)
        gu1 = jnp.concatenate(add_one(keep_gu1, r_gu1), axis=1)
        r_a1 = ring.send(a1[1::2], ("core", "core"))
        r_gains = ring.send([gains], ("core",))
        keep_d1, go = far_rows(jnp.stack([z_d1, z_d2]))
        r_d1 = ring.send(go, ("y", "x"))
        r_z = ring.send_back(gu1)
        outgoing = g0.astype(bf16)[local_slots]
        r_a1, r_gains, r_d1, r_z, outgoing, z_a2 = sync(r_a1, r_gains, r_d1, r_z, outgoing, z_a2)
        arrived = exchange(outgoing, rows)
        keep_a1, go = add_core(a1, r_a1)
        r_a1 = ring.send(go, ("x", "y"))
        gains = gains + r_gains[0]
        r_gains = ring.send([gains], ("x",))
        keep_d1, go = near_rows(add_one(keep_d1, r_d1))
        r_d1 = ring.send(go, ("x", "y"))
        r_a1, r_gains, r_d1 = sync(r_a1, r_gains, r_d1)
        keep_a1, go = add_two(keep_a1, r_a1)
        r_a1 = ring.send(go, ("y", "x"))
        gains = gains + r_gains[0]
        r_gains = ring.send([gains], ("y",))
        sum_d1, sum_d2 = ([v[k] for v in add_one(keep_d1, r_d1)] for k in range(2))
        last_gu1 = ring.add_back(gu1, r_z)
        r_a1, r_gains, arrived = sync(r_a1, r_gains, arrived)
        a1 = jnp.concatenate(add_one(keep_a1, r_a1), axis=1)
        last_a1 = ring.add_back(a1, ring.send_back(a1))
        gains = gains + r_gains[0]
        far_z = [ring.swap(gains, "z", by) for by in (1, 2, 3)]
        gains = (gains + far_z[0]) + (far_z[1] + far_z[2])
        cut = lambda v, n: [v[:n].astype(f32), v[n:].astype(f32)]
        sum_gu1, sum_a1 = cut(last_gu1, FC), cut(last_a1, 128 * len(HALVES_ONE[0]))
        sum_gu2, sum_a2 = cut(z_gu2, FC), cut(z_a2, n_a2)
        tokens_grad = arrived
        wide = lambda halves: [h.astype(f32) for h in halves]
        sum_d1, sum_d2 = wide(sum_d1), wide(sum_d2)
        rest = sum_parts(sum_a2, sum_gu2, sum_d2, HALVES_TWO)
        sums1, sums2 = sum_parts(sum_a1, sum_gu1, sum_d1, HALVES_ONE), rest
        sums1 = [sums1[0][:, :64], sums1[0][:, 64:]] + sums1[1:]
        tokens_grad = tokens_grad[restore]
    else:
        sums1 = sum_any(d1, gu1, a1, HALVES_ONE)
        sums2 = sum_any(d2, gu2, a2, HALVES_TWO)
        gains = lax.psum(gains, ("row", "col"))
        tokens_grad = exchange(g0.astype(bf16)[local_slots], rows)[restore]
    return (
        output, tokens_grad,
        gains[0], *sums1[:4], gains[1], *sums1[4:],
        gains[2], *sums2[:4], gains[3], *sums2[4:],
    )


def solution(mesh):
    names, rows, cols = ("row", "col"), "row", "col"
    if (mesh.shape["row"], mesh.shape["col"]) == (ROWS, COLS):
        names = ("z", "y", "x", "core")
        rows, cols = names[:2], names[2:]
        mesh = Mesh(mesh.devices.reshape(4, 2, 2, 2), names)
    block, weight = P(names, None), P(rows, cols)
    layer_in = (P(),) + (weight,) * 4 + (P(),) + (weight,) * 3
    return jax.shard_map(
        functools.partial(body, names),
        mesh=mesh,
        in_specs=(block, block, P(), block, P(names)) + layer_in * 2,
        out_specs=(block, block) + layer_in * 2,
        check_vma=False,
    )
```

```python
import functools

import jax
import jax.numpy as jnp
from jax import lax
from jax.experimental import pallas as pl
from jax.experimental.pallas import tpu as pltpu
from jax.sharding import Mesh, PartitionSpec as P

HEADS = 16
FEAT = 16
HEAD_DIM = 64
WINDOW = 64
MAX_LEN = 256
D = 1024
T = 512
HALF = 256
EPS = 1e-05
NEG = -1e30
ROWS = 8
COLS = 4
FB = 344
FBP = 352
FFP = ROWS * FBP
FC = FFP // COLS

bf16, f32, i32 = jnp.bfloat16, jnp.float32, jnp.int32
NN, NT, TN = ((1,), (0,)), ((1,), (1,)), ((0,), (0,))


def dot(a, b, dims):
    return lax.dot_general(a, b, (dims, ((), ())), preferred_element_type=f32)


def call(body, grid, ins, outs, scratch=(), flops=0, prefetch=None):
    extra = 0 if prefetch is None else 1

    def spec(block, index):
        if block is None:
            return pl.BlockSpec(memory_space=pl.ANY)
        return pl.BlockSpec(block, index)

    in_specs, args = [], []
    for item in ins:
        if not isinstance(item, tuple):
            nd = item.ndim
            item = (item, item.shape, functools.partial(lambda n, *_: (0,) * n, nd))
        args.append(item[0])
        in_specs.append(spec(item[1], item[2]))
    out_specs = [spec(o[2], o[3]) for o in outs]
    out_shape = [jax.ShapeDtypeStruct(o[0], o[1]) for o in outs]
    moved = sum(a.size * a.dtype.itemsize for a in args)
    moved += sum(s.size * s.dtype.itemsize for s in out_shape)
    cost = pl.CostEstimate(flops=int(flops), bytes_accessed=int(moved), transcendentals=0)
    got = pl.pallas_call(
        body,
        out_shape=out_shape,
        grid_spec=pltpu.PrefetchScalarGridSpec(
            num_scalar_prefetch=extra,
            grid=grid,
            in_specs=in_specs,
            out_specs=out_specs,
            scratch_shapes=list(scratch),
        ),
        compiler_params=pltpu.CompilerParams(vmem_limit_bytes=56 * 2**20),
        cost_estimate=cost,
    )(*(([prefetch] if extra else []) + args))
    return got


def whole_map(*shape):
    zeros = (0,) * len(shape)
    return lambda *_: zeros


def norm_factor(h):
    return lax.rsqrt(jnp.mean(h * h, axis=-1, keepdims=True) + EPS)


class Strips:
    def __init__(self, half, swapped, at, n):
        self.bufs, self.swapped, self.at, self.n = half, swapped, at, n

    def scratch(self):
        return [pltpu.VMEM((2, 2, 2, 4, self.n, 128), bf16), pltpu.SemaphoreType.DMA((2, 2, 2))]

    def start(self, refs, box, sems):
        order = [(core, x, y) for core in range(2) for x in range(2) for y in range(2)]
        for core, x, y in order:
            hi, lo = (x, y) if self.swapped else (y, x)
            src = refs[core * 2 + hi].at[lo]
            if self.n != self.bufs[0].shape[2]:
                src = src.at[:, pl.ds(self.at, self.n)]
            pltpu.make_async_copy(src, box.at[core, hi, lo], sems.at[core, hi, lo]).start()

    def wait(self, box, sems, core, x):
        for y in range(2):
            hi, lo = (x, y) if self.swapped else (y, x)
            there = box.at[core, hi, lo]
            pltpu.make_async_copy(there, there, sems.at[core, hi, lo]).wait()

    def wait_all(self, box, sems):
        for core in range(2):
            for x in range(2):
                self.wait(box, sems, core, x)

    def piece(self, box, z, y, x, core):
        return box.at[core, x, y, z] if self.swapped else box.at[core, y, x, z]


class DownRows:
    def __init__(self, bufs):
        self.bufs = bufs

    def scratch(self):
        return [pltpu.VMEM((2, 4, FFP, 128), bf16), pltpu.SemaphoreType.DMA((2, 4))]

    def start(self, refs, box, sems):
        for z in range(4):
            for core in range(2):
                pltpu.make_async_copy(refs[core].at[z], box.at[core, z], sems.at[core, z]).start()

    def rows(self, box, sems, z, my):
        for core in range(2):
            there = box.at[core, z]
            pltpu.make_async_copy(there, there, sems.at[core, z]).wait()
        halves = []
        for y in range(2):
            parts = []
            for x, core in PLACES:
                for at in down_places(x, y ^ my):
                    parts.append(box[core, z, pl.ds(at, FBP), :])
            halves.append(jnp.concatenate(parts, axis=1))
        return jnp.concatenate(halves, axis=0)


def down_places(x, y):
    return [pl.multiple_of(p * FBP, 16) for p in (y * 2 + x, 4 + x * 2 + y)]


BLOCKS = [(z, y) for z in range(4) for y in range(2)]
PLACES = [(x, core) for x in range(2) for core in range(2)]


def step_place(i):
    return i % 2, i // 2


def step_col(i, me):
    return ((i % 2) * 2 + i // 2) ^ me[1]


def regroup(dst_ref, src_ref, count, me):
    width = D // count
    for j in range(count):
        at = pl.multiple_of((j ^ me) * width, 128)
        dst_ref[:, j * width : (j + 1) * width] = src_ref[:, pl.ds(at, width)]


class Kernel:
    def __init__(self, n_in, strips, n_out):
        self.n_in, self.strips, self.n_out = n_in, strips, n_out

    def split(self, refs):
        ins, refs = refs[: self.n_in], refs[self.n_in :]
        srcs = []
        for s in self.strips:
            srcs.append(refs[: len(s.bufs)])
            refs = refs[len(s.bufs) :]
        outs, refs = refs[: self.n_out], refs[self.n_out :]
        hold = [(s, srcs[j], refs[2 * j], refs[2 * j + 1]) for j, s in enumerate(self.strips)]
        return ins, hold, outs, refs[2 * len(self.strips) :]

    def ins(self):
        return [(b, None, None) for s in self.strips for b in s.bufs]

    def scratch(self):
        return [i for s in self.strips for i in s.scratch()]


def start_all(hold):
    for s, srcs, box, sems in hold:
        s.start(srcs, box, sems)


def col_block(s, box, x, core):
    strips = []
    for j in range(s.n // 128):
        strips.append(jnp.concatenate([s.piece(box, z, y, x, core)[j * 128 : (j + 1) * 128, :] for z, y in BLOCKS], axis=0))
    return strips[0] if len(strips) == 1 else jnp.concatenate(strips, axis=1)


def norm_proj(me, h, gain, strips):
    n = len(strips)
    kern = Kernel(2, strips, n + 1)

    def body(me_ref, *refs):
        (h_ref, gain_ref), hold, (xa_ref, *outs), (xr_ref,) = kern.split(refs)
        i = pl.program_id(0)

        @pl.when(i == 0)
        def _():
            start_all(hold)
            hv = h_ref[...].astype(f32)
            xa_ref[...] = (hv * norm_factor(hv) * gain_ref[...]).astype(bf16)
            regroup(xr_ref, xa_ref, ROWS, me_ref[0])

        x, core = step_place(i)
        for (s, _, box, sems), o_ref in zip(hold, outs):
            s.wait(box, sems, core, x)
            o_ref[...] = dot(xr_ref[...], col_block(s, box, x, core), NN).astype(bf16)

    outs = [((T, D), bf16, (T, D), whole_map(T, D))]
    for s in strips:
        outs.append(((T, s.n * COLS), bf16, (T, s.n), lambda i, me: (0, step_col(i, me))))
    total = sum(s.n * COLS for s in strips)
    return call(
        body, (COLS,), [h, gain.reshape(1, D)] + kern.ins(), outs,
        scratch=kern.scratch() + [pltpu.VMEM((T, D), bf16)], flops=2 * T * D * total, prefetch=me,
    )


def lanes(shape, width):
    return lax.broadcasted_iota(i32, shape, len(shape) - 1) // width


def fill_mask(mask_ref, seg_q, seg_k, live_k, q_axis, window):
    q = lax.broadcasted_iota(i32, (T, T), q_axis)
    k = lax.broadcasted_iota(i32, (T, T), 1 - q_axis)
    ok = (k <= q) & (k > q - window) & (seg_q == seg_k) & ((live_k > 0) | (k == q))
    mask_ref[...] = jnp.where(ok, 1.0, 0.0)


def based_fwd(qk, v, seg_row, seg_col, live_row):
    def body(qk_ref, v_ref, sr_ref, sc_ref, lr_ref, o_ref, ou_ref, rden_ref, mask_ref):
        @pl.when(pl.program_id(0) == 0)
        def _():
            fill_mask(mask_ref, sc_ref[...], sr_ref[...], lr_ref[...], 0, MAX_LEN)

        q4, k4 = qk_ref[:, 0:64], qk_ref[:, 64:128]
        qlane = lanes((T, 64), FEAT)
        first = lanes((HALF, 128), HEAD_DIM) == 0
        scaled = q4.astype(f32) * (FEAT**-0.5)
        for pair in range(2):
            v2 = v_ref[:, pair * 128 : pair * 128 + 128]
            for tb in range(2):
                t0, s1 = tb * HALF, (tb + 1) * HALF
                got = []
                for e in range(2):
                    qm = jnp.where(qlane == pair * 2 + e, scaled, 0.0).astype(bf16)
                    a = dot(qm[t0 : t0 + HALF], k4[0:s1], NT)
                    p = (1.0 + a * (1.0 + 0.5 * a)) * mask_ref[t0 : t0 + HALF, 0:s1]
                    den = jnp.sum(p, axis=-1, keepdims=True)
                    got.append((dot(p.astype(bf16), v2[0:s1], NN), den))
                rden = 1.0 / jnp.where(first, got[0][1], got[1][1])
                ou = jnp.where(first, got[0][0], got[1][0]) * rden
                at = (slice(t0, t0 + HALF), slice(pair * 128, pair * 128 + 128))
                ou_ref[at] = ou
                rden_ref[at] = rden
                o_ref[at] = ou.astype(bf16)

    wide = (T, 256)
    col = lambda c: (0, c)
    return call(
        body,
        (4,),
        [(qk, (T, 128), col), (v, wide, col), seg_row, seg_col, live_row],
        [((T, D), bf16, wide, col), ((T, D), f32, wide, col), ((T, D), f32, wide, col)],
        scratch=[pltpu.VMEM((T, T), f32)],
        flops=HEADS * T * T * 2 * 192,
    )


def based_bwd(qk, v, dou, ou, rden, seg_row, seg_col, live_col):
    def body(qk_ref, v_ref, dou_ref, ou_ref, rden_ref, sr_ref, sc_ref, lc_ref, dqk_ref, dv_ref, mask_ref, dk_ref, dva_ref):
        @pl.when(pl.program_id(0) == 0)
        def _():
            fill_mask(mask_ref, sr_ref[...], sc_ref[...], lc_ref[...], 1, MAX_LEN)

        q4, k4 = qk_ref[:, 0:64], qk_ref[:, 64:128]
        qlane = lanes((T, 64), FEAT)
        q_scaled = q4.astype(f32) * (FEAT**-0.5)
        k_scaled = k4.astype(f32) * (FEAT**-0.5)
        vlane = lanes((T, 128), HEAD_DIM)
        dnum_f = dou_ref[...] * rden_ref[...]
        term = dnum_f * ou_ref[...]
        high = term.astype(bf16)
        low = (term - high.astype(f32)).astype(bf16)
        pick = jnp.where(
            lax.broadcasted_iota(i32, (8, 256), 0) == lanes((8, 256), HEAD_DIM), 1.0, 0.0
        ).astype(bf16)
        dden = -(dot(pick, high, NT) + dot(pick, low, NT))
        dk_ref[...] = jnp.zeros((T, 64), f32)
        dva_ref[...] = jnp.zeros((T, 256), f32)
        dq = [jnp.zeros((HALF, 64), f32), jnp.zeros((HALF, 64), f32)]
        for pair in range(2):
            cols = slice(pair * 128, pair * 128 + 128)
            v2 = v_ref[:, cols]
            for e in range(2):
                head = pair * 2 + e
                qm = jnp.where(qlane == head, q_scaled, 0.0).astype(bf16)
                km = jnp.where(qlane == head, k_scaled, 0.0).astype(bf16)
                dn = jnp.where(vlane == e, dnum_f[:, cols], 0.0).astype(bf16)
                for tb in range(2):
                    t0, s1 = tb * HALF, (tb + 1) * HALF
                    at = slice(t0, t0 + HALF)
                    a = dot(k4[0:s1], qm[at], NT)
                    m = mask_ref[0:s1, at]
                    p = (1.0 + a * (1.0 + 0.5 * a)) * m
                    dp = dot(v2[0:s1], dn[at], NT) + dden[head : head + 1, at]
                    da = (dp * m * (1.0 + a)).astype(bf16)
                    dk_ref[0:s1, :] += dot(da, qm[at], NN)
                    dva_ref[0:s1, cols] += dot(p.astype(bf16), dn[at], NN)
                    dq[tb] += dot(da, km[0:s1], TN)
        for tb in range(2):
            at = slice(tb * HALF, tb * HALF + HALF)
            dqk_ref[at, 0:64] = dq[tb].astype(bf16)
        dqk_ref[:, 64:128] = dk_ref[...].astype(bf16)
        dv_ref[...] = dva_ref[...].astype(bf16)

    wide = (T, 256)
    col = lambda c: (0, c)
    return call(
        body,
        (4,),
        [(qk, (T, 128), col), (v, wide, col), (dou, wide, col), (ou, wide, col), (rden, wide, col), seg_row, seg_col, live_col],
        [((T, 512), bf16, (T, 128), col), ((T, D), bf16, wide, col)],
        scratch=[pltpu.VMEM((T, T), f32), pltpu.VMEM((T, 64), f32), pltpu.VMEM((T, 256), f32)],
        flops=HEADS * T * T * 2 * 480,
    )


SPAN = ((0, HALF), (HALF - WINDOW, T))


def window_fwd(q, k, v, seg_row, seg_col, live_col):
    def body(q_ref, k_ref, v_ref, sr_ref, sc_ref, lc_ref, o_ref, mask_ref):
        @pl.when(pl.program_id(0) == 0)
        def _():
            fill_mask(mask_ref, sr_ref[...], sc_ref[...], lc_ref[...], 1, WINDOW)

        first = lanes((HALF, 128), HEAD_DIM) == 0
        qlane = lanes((T, 128), HEAD_DIM)
        scaled = q_ref[...].astype(f32) * (HEAD_DIM**-0.5)
        for tb in range(2):
            at = slice(tb * HALF, tb * HALF + HALF)
            s0, s1 = SPAN[tb]
            ok = mask_ref[s0:s1, at] > 0.5
            got = []
            for e in range(2):
                qm = jnp.where(qlane == e, scaled, 0.0).astype(bf16)
                c = dot(k_ref[s0:s1, :], qm[at], NT)
                c = jnp.where(ok, c, NEG)
                w = jnp.exp(c - jnp.max(c, axis=0, keepdims=True))
                w = w * (1.0 / jnp.sum(w, axis=0, keepdims=True))
                got.append(dot(w.astype(bf16), v_ref[s0:s1, :], TN))
            o_ref[at, :] = jnp.where(first, got[0], got[1]).astype(bf16)

    blk = (T, 128)
    col = lambda c: (0, c)
    return call(
        body,
        (8,),
        [(q, blk, col), (k, blk, col), (v, blk, col), seg_row, seg_col, live_col],
        [((T, D), bf16, blk, col)],
        scratch=[pltpu.VMEM((T, T), f32)],
        flops=HEADS * T * T * 2 * 192,
    )[0]


def window_bwd(q, k, v, dor, seg_row, seg_col, live_col):
    def body(q_ref, k_ref, v_ref, do_ref, sr_ref, sc_ref, lc_ref, dq_ref, dk_ref, dv_ref, mask_ref, dka_ref, dva_ref):
        @pl.when(pl.program_id(0) == 0)
        def _():
            fill_mask(mask_ref, sr_ref[...], sc_ref[...], lc_ref[...], 1, WINDOW)

        lane = lanes((T, 128), HEAD_DIM)
        q_scaled = q_ref[...].astype(f32) * (HEAD_DIM**-0.5)
        k_scaled = k_ref[...].astype(f32) * (HEAD_DIM**-0.5)
        do = do_ref[...]
        dka_ref[...] = jnp.zeros((T, 128), f32)
        dva_ref[...] = jnp.zeros((T, 128), f32)
        for tb in range(2):
            at = slice(tb * HALF, tb * HALF + HALF)
            s0, s1 = SPAN[tb]
            ok = mask_ref[s0:s1, at] > 0.5
            dq = jnp.zeros((HALF, 128), f32)
            for e in range(2):
                qm = jnp.where(lane == e, q_scaled, 0.0).astype(bf16)
                km = jnp.where(lane == e, k_scaled, 0.0).astype(bf16)
                dm = jnp.where(lane == e, do, jnp.zeros_like(do))
                c = dot(k_ref[s0:s1, :], qm[at], NT)
                c = jnp.where(ok, c, NEG)
                w = jnp.exp(c - jnp.max(c, axis=0, keepdims=True))
                w = w * (1.0 / jnp.sum(w, axis=0, keepdims=True))
                dw = dot(v_ref[s0:s1, :], dm[at], NT)
                ds = (w * (dw - jnp.sum(w * dw, axis=0, keepdims=True))).astype(bf16)
                dka_ref[s0:s1, :] += dot(ds, qm[at], NN)
                dva_ref[s0:s1, :] += dot(w.astype(bf16), dm[at], NN)
                dq += dot(ds, km[s0:s1], TN)
            dq_ref[at, :] = dq.astype(bf16)
        dk_ref[...] = dka_ref[...].astype(bf16)
        dv_ref[...] = dva_ref[...].astype(bf16)

    blk = (T, 128)
    col = lambda c: (0, c)
    return call(
        body,
        (8,),
        [(q, blk, col), (k, blk, col), (v, blk, col), (dor, blk, col), seg_row, seg_col, live_col],
        [((T, D), bf16, blk, col)] * 3,
        scratch=[pltpu.VMEM((T, T), f32), pltpu.VMEM((T, 128), f32), pltpu.VMEM((T, 128), f32)],
        flops=HEADS * T * T * 2 * 480,
    )


def attn_out(me, h, o, strip, gain):
    kern = Kernel(3, [strip], 2)

    def body(me_ref, *refs):
        (h_ref, o_ref, gain_ref), hold, (hm_ref, xf_ref), (or_ref,) = kern.split(refs)
        i = pl.program_id(0)

        @pl.when(i == 0)
        def _():
            start_all(hold)
            regroup(or_ref, o_ref, ROWS, me_ref[0])

        x, core = step_place(i)
        s, _, box, sems = hold[0]
        s.wait(box, sems, core, x)
        at = pl.ds(pl.multiple_of(step_col(i, me_ref) * 256, 256), 256)
        hm_ref[:, at] = h_ref[:, at].astype(f32) + dot(or_ref[...], col_block(s, box, x, core), NN)

        @pl.when(i == COLS - 1)
        def _():
            hm = hm_ref[...]
            xf_ref[...] = (hm * norm_factor(hm) * gain_ref[...]).astype(bf16)

    full = whole_map(T, D)
    return call(
        body, (COLS,), [h, o, gain.reshape(1, D)] + kern.ins(),
        [((T, D), f32, (T, D), full), ((T, D), bf16, (T, D), full)],
        scratch=kern.scratch() + [pltpu.VMEM((T, D), bf16)], flops=2 * T * D * D, prefetch=me,
    )


def hidden_block(s, box, x, core):
    return jnp.concatenate([s.piece(box, z, y, x, core)[...] for z, y in BLOCKS], axis=1)


def gate_up(me, xf, w_gate, w_up):
    kern = Kernel(1, [w_gate, w_up], 3)

    def body(me_ref, *refs):
        (xf_ref,), hold, (g_ref, u_ref, hid_ref), (xr_ref,) = kern.split(refs)
        i = pl.program_id(0)

        @pl.when(i == 0)
        def _():
            start_all(hold)
            regroup(xr_ref, xf_ref, ROWS, me_ref[0])

        x, core = step_place(i)
        got = []
        for s, _, box, sems in hold:
            s.wait(box, sems, core, x)
            got.append(dot(hidden_block(s, box, x, core), xr_ref[...], NT))
        g, u = got
        g_ref[...] = g.astype(bf16)
        u_ref[...] = u.astype(bf16)
        hid_ref[...] = (g * (1.0 / (1.0 + jnp.exp(-g))) * u).astype(bf16)

    row = lambda i, me: (step_col(i, me), 0)
    return call(
        body, (COLS,), [xf] + kern.ins(), [((FFP, T), bf16, (FC, T), row)] * 3,
        scratch=kern.scratch() + [pltpu.VMEM((T, D), bf16)], flops=4 * T * D * FFP, prefetch=me,
    )


def down(me, hm, hid, w_down):
    kern = Kernel(2, [w_down], 1)

    def body(me_ref, *refs):
        (hm_ref, hid_ref), hold, (h_ref,), (acc_ref,) = kern.split(refs)
        i = pl.program_id(0)

        @pl.when(i == 0)
        def _():
            start_all(hold)
            regroup(acc_ref, hm_ref, COLS, me_ref[1])

        s, _, box, sems = hold[0]
        acc_ref[...] += dot(hid_ref[...], s.rows(box, sems, i, me_ref[0]), TN)

        @pl.when(i == COLS - 1)
        def _():
            regroup(h_ref, acc_ref, COLS, me_ref[1])

    return call(
        body, (COLS,), [hm, (hid, (FC, T), lambda i, me: (i, 0))] + kern.ins(),
        [((T, D), f32, (T, D), whole_map(T, D))],
        scratch=kern.scratch() + [pltpu.VMEM((T, D), f32)], flops=2 * T * D * FFP, prefetch=me,
    )[0]


def down_bwd(me, bd, w_down, hid, g, u):
    kern = Kernel(4, [w_down], 4)

    def body(me_ref, *refs):
        (bd_ref, hid_ref, g_ref, u_ref), hold, (dg_ref, du_ref, *p_refs), (br_ref,) = kern.split(refs)
        i = pl.program_id(0)

        @pl.when(i == 0)
        def _():
            start_all(hold)
            regroup(br_ref, bd_ref, COLS, me_ref[1])

        bdv = br_ref[...].astype(bf16)
        gwd = dot(hid_ref[...], bdv, NN).astype(bf16)
        for x, core in PLACES:
            at = (x * 2 + core) * 256
            for y in range(2):
                rows = slice(y * FBP, (y + 1) * FBP)
                for half, to in enumerate(down_places(x, y ^ me_ref[0])):
                    p_refs[core][0, pl.ds(to, FBP), :] = gwd[rows, at + half * 128 : at + half * 128 + 128]
        s, _, box, sems = hold[0]
        dhid = dot(s.rows(box, sems, i, me_ref[0]), bdv, NT)
        gv, uv = g_ref[...].astype(f32), u_ref[...].astype(f32)
        sig = 1.0 / (1.0 + jnp.exp(-gv))
        act = gv * sig
        du_ref[...] = (dhid * act).astype(bf16)
        dg_ref[...] = (dhid * uv * (sig + act * (1.0 - sig))).astype(bf16)

    row = lambda i, me: (i, 0)
    hblk = (FC, T)
    pieces = ((4, FFP, 128), bf16, (1, FFP, 128), lambda i, me: (i, 0, 0))
    return call(
        body, (COLS,), [bd, (hid, hblk, row), (g, hblk, row), (u, hblk, row)] + kern.ins(),
        [((FFP, T), bf16, hblk, row), ((FFP, T), bf16, hblk, row)] + [pieces] * 2,
        scratch=kern.scratch() + [pltpu.VMEM((T, D), bd.dtype)], flops=4 * T * D * FFP, prefetch=me,
    )


def piece_specs(n1, n2):
    out = []
    for n, block, place in ((n1, (1, 2, 4), lambda j: (j, 0)), (n2, (2, 1, 4), lambda j: (0, j))):
        for step in (lambda i: jnp.minimum(i, 1), lambda i: jnp.maximum(i - 2, 0)):
            index = functools.partial(lambda place, step, i, me: (*place(step(i)), 0, 0, 0), place, step)
            out.append(((2, 2, 4, n, 128), bf16, (*block, n, 128), index))
    return out


def for_core(refs, write):
    for core in range(2):

        @pl.when(pl.program_id(0) // 2 == core)
        def _():
            write(refs[core], refs[2 + core])


def gate_up_bwd(me, xf, dg, du):
    def body(me_ref, xf_ref, dg_ref, du_ref, *refs):
        *p_refs, xr_ref = refs

        @pl.when(pl.program_id(0) == 0)
        def _():
            regroup(xr_ref, xf_ref, ROWS, me_ref[0])

        gwg = dot(dg_ref[...], xr_ref[...], NN).astype(bf16)
        gwu = dot(du_ref[...], xr_ref[...], NN).astype(bf16)

        def write(one, two):
            for r, (z, y) in enumerate(BLOCKS):
                one[0, y, z] = gwg[:, r * 128 : (r + 1) * 128]
                two[y, 0, z] = gwu[:, r * 128 : (r + 1) * 128]

        for_core(p_refs, write)

    row = lambda i, me: (step_col(i, me), 0)
    return call(
        body, (COLS,), [xf, (dg, (FC, T), row), (du, (FC, T), row)], piece_specs(FC, FC),
        scratch=[pltpu.VMEM((T, D), bf16)], flops=4 * T * D * FFP, prefetch=me,
    )


def norm_bwd(dx, h, gain, g):
    rf = norm_factor(h)
    hr = h * rf
    dgain = jnp.sum(dx * hr, axis=0, keepdims=True)
    gd = gain * dx
    mean = jnp.sum(gd * hr, axis=-1, keepdims=True) * (1.0 / D)
    return dgain, g + rf * (gd - hr * mean)


def add_to(acc_ref, part):
    @pl.when(pl.program_id(0) == 0)
    def _():
        acc_ref[...] = part

    @pl.when(pl.program_id(0) > 0)
    def _():
        acc_ref[...] += part


def mlp_dx(me, dg, du, w_gate, w_up, hm, gain, g, w_out, kind):
    kern = Kernel(5, [w_gate, w_up, w_out], 4)

    def body(me_ref, *refs):
        (dg_ref, du_ref, hm_ref, gain_ref, g_ref), hold, outs, rest = kern.split(refs)
        acc_ref, un_ref, br_ref, hl_ref, gl_ref, late = rest
        gm_ref, bo_ref, dou_ref, gg_ref = outs
        i = pl.program_id(0)

        @pl.when(i == 0)
        def _():
            start_all(hold)
            for k, (src, dst) in enumerate(((hm_ref, hl_ref), (g_ref, gl_ref))):
                pltpu.make_async_copy(src, dst, late.at[k]).start()

        x, core = step_place(i)
        part = None
        for (s, _, box, sems), d_ref in zip(hold[:2], (dg_ref, du_ref)):
            s.wait(box, sems, core, x)
            term = dot(d_ref[...], hidden_block(s, box, x, core), TN)
            part = term if part is None else part + term
        add_to(acc_ref, part)

        @pl.when(i == COLS - 1)
        def _():
            regroup(un_ref, acc_ref, ROWS, me_ref[0])
            for k, (src, dst) in enumerate(((hm_ref, hl_ref), (g_ref, gl_ref))):
                pltpu.make_async_copy(src, dst, late.at[k]).wait()
            gg, gm = norm_bwd(un_ref[...], hl_ref[...], gain_ref[...], gl_ref[...].astype(f32))
            gg_ref[...] = gg
            gm_ref[...] = gm
            bo_ref[...] = gm.astype(bf16)
            regroup(br_ref, bo_ref, COLS, me_ref[1])
            s, _, box, sems = hold[2]
            s.wait_all(box, sems)
            w = jnp.concatenate([col_block(s, box, x, core) for x, core in PLACES], axis=1)
            acc_ref[...] = dot(br_ref[...], w, NT)
            regroup(un_ref, acc_ref, ROWS, me_ref[0])
            dou_ref[...] = un_ref[...].astype(kind)

    row = lambda i, me: (step_col(i, me), 0)
    full = whole_map(T, D)
    return call(
        body, (COLS,), [(dg, (FC, T), row), (du, (FC, T), row), (hm, None, None), gain.reshape(1, D), (g, None, None)] + kern.ins(),
        [((T, D), f32, (T, D), full), ((T, D), bf16, (T, D), full), ((T, D), kind, (T, D), full), ((1, D), f32, (1, D), full)],
        scratch=kern.scratch()
        + [pltpu.VMEM((T, D), f32), pltpu.VMEM((T, D), f32), pltpu.VMEM((T, D), bf16)]
        + [pltpu.VMEM((T, D), f32), pltpu.VMEM((T, D), g.dtype), pltpu.SemaphoreType.DMA((2,))],
        flops=4 * T * D * FFP + 2 * T * D * D, prefetch=me,
    )


def attn_bwd(me, xa, grads, strips, o, bo, h, gain, gm, halves):
    n = len(grads)
    kern = Kernel(6 + n, strips, 6)

    def body(me_ref, *refs):
        ins, hold, (*p_refs, g_ref, gg_ref), rest = kern.split(refs)
        xr_ref, or_ref, xt_ref, ot_ref, acc_ref, hl_ref, gl_ref, late = rest
        xa_ref, o_ref, h_ref, gain_ref, gm_ref, bo_ref, *d_refs = ins
        i = pl.program_id(0)

        @pl.when(i == 0)
        def _():
            start_all(hold)
            regroup(xr_ref, xa_ref, ROWS, me_ref[0])
            regroup(or_ref, o_ref, ROWS, me_ref[0])
            for k, (src, dst) in enumerate(((h_ref, hl_ref), (gm_ref, gl_ref))):
                pltpu.make_async_copy(src, dst, late.at[k]).start()
            xt_ref[...] = xr_ref[...].T
            ot_ref[...] = or_ref[...].T

        tiles = [dot(xt_ref[...], d[...], NN).astype(bf16) for d in d_refs]
        tiles.append(dot(ot_ref[...], bo_ref[...], NN).astype(bf16))

        def write(one, two):
            for j, (which, at) in enumerate(halves[0]):
                for r, (z, y) in enumerate(BLOCKS):
                    one[0, y, z, j * 128 : (j + 1) * 128] = tiles[which][r * 128 : (r + 1) * 128, at : at + 128]
            for j, (which, at) in enumerate(halves[1]):
                for r, (z, y) in enumerate(BLOCKS):
                    two[y, 0, z, j * 128 : (j + 1) * 128] = tiles[which][r * 128 : (r + 1) * 128, at : at + 128]

        for_core(p_refs, write)
        x, core = step_place(i)
        part = None
        for (s, _, box, sems), d in zip(hold, d_refs):
            s.wait(box, sems, core, x)
            term = dot(d[...], col_block(s, box, x, core), NT)
            part = term if part is None else part + term
        add_to(acc_ref, part)

        @pl.when(i == COLS - 1)
        def _():
            regroup(g_ref, acc_ref, ROWS, me_ref[0])
            for k, (src, dst) in enumerate(((h_ref, hl_ref), (gm_ref, gl_ref))):
                pltpu.make_async_copy(src, dst, late.at[k]).wait()
            gg, g = norm_bwd(g_ref[...], hl_ref[...].astype(f32), gain_ref[...], gl_ref[...])
            gg_ref[...] = gg
            g_ref[...] = g

    col = lambda i, me: (0, step_col(i, me))
    full = whole_map(T, D)
    ins = [xa, o, (h, None, None), gain.reshape(1, D), (gm, None, None), (bo, (T, 256), col)]
    ins += [(d, (T, d.shape[1] // COLS), col) for d in grads]
    total = sum(d.shape[1] for d in grads)
    return call(
        body, (COLS,), ins + kern.ins(),
        piece_specs(128 * len(halves[0]), 128 * len(halves[1])) + [((T, D), f32, (T, D), full), ((1, D), f32, (1, D), full)],
        scratch=kern.scratch()
        + [pltpu.VMEM((T, D), bf16)] * 2
        + [pltpu.VMEM((D, T), bf16)] * 2
        + [pltpu.VMEM((T, D), f32), pltpu.VMEM((T, D), h.dtype), pltpu.VMEM((T, D), f32), pltpu.SemaphoreType.DMA((2,))],
        flops=4 * T * D * total + 2 * T * D * D, prefetch=me,
    )


HALVES_ONE = (((1, 0), (1, 128)), ((0, 0), (2, 0), (2, 128)))
HALVES_TWO = (((0, 0), (0, 128), (1, 0), (1, 128)), ((2, 0), (2, 128), (3, 0), (3, 128)))


def attn_weights(bufs, halves):
    out = []
    for which in range(1 + max(w for half in halves for w, _ in half)):
        for k, half in enumerate(halves):
            at = [j for j, (w, _) in enumerate(half) if w == which]
            if at:
                out.append(Strips(bufs[k], k == 1, at[0] * 128, len(at) * 128))
    return out


def gate_weights(bufs):
    return Strips(bufs[0], False, 0, FC), Strips(bufs[1], True, 0, FC)


def pad_hidden(w):
    k = w.shape[0]
    return jnp.pad(w.reshape(k, -1, FB), ((0, 0), (0, 0), (0, FBP - FB))).reshape(k, -1).T


def pad_rows(w):
    n = w.shape[1]
    return jnp.pad(w.reshape(-1, FB, n), ((0, 0), (0, FBP - FB), (0, 0))).reshape(-1, n)


def strips_of(blocks, halves):
    return tuple(
        jnp.concatenate([blocks[which][..., at : at + 128] for which, at in strips], axis=-2) for strips in halves
    )


def after(value, *arrays):
    return lax.optimization_barrier((value, *arrays))[0] if arrays else value


def sync(*groups):
    flat, tree = jax.tree.flatten(groups)
    return jax.tree.unflatten(tree, lax.optimization_barrier(flat))


def add_core(four, got):
    keep = [four[0][0] + got[0][0], four[2][0] + got[1][0]]
    return keep, [four[0][1] + got[0][1], four[2][1] + got[1][1]]


def add_two(keep, got):
    return [k[0] + g[0] for k, g in zip(keep, got)], [k[1] + g[1] for k, g in zip(keep, got)]


def add_one(keep, got):
    return [k + g for k, g in zip(keep, got)]


def far_rows(total):
    parts = jnp.split(total, 4, axis=-2)
    return parts[0::2], parts[1::2]


def near_rows(halves):
    parts = [jnp.split(h, 2, axis=-2) for h in halves]
    return [p[0] for p in parts], [p[1] for p in parts]


class Ring:
    def __init__(self, names):
        self.axes = names
        self.z = lax.axis_index(names[0])

    def swap(self, value, axis, by=1):
        shift = {"z": 3, "y": 2, "x": 1, "core": 0}[axis]
        return lax.ppermute(value, self.axes, [(i, i ^ (by << shift)) for i in range(32)])

    def gather_z(self, both, *behind):
        near = [both] + [after(self.swap(both, "z", by), *behind) for by in (1, 2, 3)]
        low, high = self.z % 2 == 1, self.z >= 2
        a, b = jnp.where(low, near[1], near[0]), jnp.where(low, near[0], near[1])
        c, d = jnp.where(low, near[3], near[2]), jnp.where(low, near[2], near[3])
        pick = lambda p, q: jnp.where(high, q, p)
        return jnp.stack([pick(a, c), pick(b, d), pick(c, a), pick(d, b)])

    def gather_z_all(self, both):
        return lax.all_gather(both, self.axes[0], axis=0, tiled=False)

    def gather_lo(self, pair, *behind):
        got = [after(self.swap(v, axis), *behind) for v, axis in zip(pair, ("x", "y"))]
        return [jnp.stack([v, g]) for v, g in zip(pair, got)]

    def gather_hi(self, pair, *behind):
        return [[v, after(self.swap(v, axis), *behind)] for v, axis in zip(pair, ("y", "x"))]

    def gather_core(self, full, *behind):
        return [half + [after(self.swap(b, "core"), *behind) for b in half] for half in full]

    def gather_down(self, pair):
        return jnp.stack([jnp.stack(half) for half in self.gather_hi(self.gather_lo(pair))]).reshape(-1, 128)

    def scatter_z(self, value):
        return lax.psum_scatter(value, self.axes[0], scatter_dimension=0, tiled=False)

    def send(self, values, axes):
        return [self.swap(v, axis) for v, axis in zip(values, axes)]

    def send_back(self, value):
        part = lambda by: lax.dynamic_index_in_dim(value, self.z ^ by, 0, False)
        return [self.swap(part(by), "z", by) for by in (1, 2, 3)]

    def add_back(self, value, got):
        total = lax.dynamic_index_in_dim(value, self.z, 0, False).astype(f32)
        for g in got:
            total = total + g.astype(f32)
        return total

    def reduce_z_all(self, pair):
        n1 = pair[0].shape[1]
        both = jnp.concatenate(pair, axis=1)
        total = lax.psum_scatter(both, self.axes[0], scatter_dimension=0, tiled=False).astype(f32)
        return total[:n1], total[n1:]


def pack(shards, halves):
    *attn, gate, up, dn = shards
    dp = pad_rows(dn)
    return [strips_of(attn, halves), (pad_hidden(gate), pad_hidden(up)), (dp[:, :128], dp[:, 128:])]


def boxes_any(weights, halves):
    *attn, gate, up, dn = weights

    def cut(w, rows, cols):
        return w.reshape(4, 2, rows, 2, 2, cols).transpose(0, 1, 3, 4, 2, 5)

    def boxes(one, two):
        first = [one[:, y, :, core].transpose(1, 0, 2, 3) for core in range(2) for y in range(2)]
        second = [two[:, :, x, core].transpose(1, 0, 2, 3) for core in range(2) for x in range(2)]
        return first, second

    a = boxes(*strips_of([cut(w, D // ROWS, w.shape[1] // COLS) for w in attn], halves))
    hidden = lambda w: pad_hidden(w).reshape(2, 2, FC, 4, 2, 128).transpose(3, 4, 0, 1, 2, 5)
    d = cut(pad_rows(dn), FBP, 256)
    one = d[..., :128].transpose(3, 0, 1, 2, 4, 5)
    two = d[..., 128:].transpose(3, 0, 2, 1, 4, 5)
    d = jnp.stack([one, two], axis=2).reshape(2, 4, FFP, 128)
    return [a, boxes(hidden(gate), hidden(up)), [d[0], d[1]]]


def unpad_hidden(g):
    k = g.shape[1]
    return g.reshape(-1, FBP, k)[:, :FB].reshape(-1, k).T


def unpad_rows(g):
    n = g.shape[1]
    return g.reshape(-1, FBP, n)[:, :FB].reshape(-1, n)


def whole_grad(own, send, swapped):
    p = jnp.stack([own, send])
    if swapped:
        p = jnp.swapaxes(p, 1, 2)
    core, x, y, z, n, w = p.shape
    return p.transpose(3, 2, 1, 0, 4, 5).reshape(z * y, x * core, n, w)


def join_strips(one, two, halves):
    out = []
    for which in range(1 + max(w for half in halves for w, _ in half)):
        got = {}
        for src, strips in ((one, halves[0]), (two, halves[1])):
            for j, (w, at) in enumerate(strips):
                if w == which:
                    got[at] = src[..., j * 128 : j * 128 + 128, :]
        out.append(jnp.concatenate([got[a] for a in sorted(got)], axis=-1))
    return out


def sum_parts(a, gu, d, halves):
    return join_strips(*a, halves) + [unpad_hidden(gu[0]), unpad_hidden(gu[1]), unpad_rows(jnp.concatenate(d, axis=1))]


def scatter_any(w):
    part = lax.psum_scatter(w, "row", scatter_dimension=0, tiled=True)
    return lax.psum_scatter(part, "col", scatter_dimension=1, tiled=True).astype(f32)


def natural(blocks):
    r, c, n, w = blocks.shape
    return blocks.transpose(0, 2, 1, 3).reshape(r * n, c * w)


def sum_any(pd, pgu, pa, halves):
    pairs = lambda p: (whole_grad(*p[:2], False), whole_grad(*p[2:], True))
    one, two = jnp.split(jnp.stack(pd).reshape(2, 4, 2, 2, 2, FBP, 128), 2, axis=2)
    dn = jnp.concatenate([one[:, :, 0], jnp.swapaxes(two[:, :, 0], 2, 3)], axis=-1)
    dn = dn.transpose(1, 2, 3, 0, 4, 5).reshape(ROWS, COLS, FBP, 256)
    dn = scatter_any(unpad_rows(natural(dn)))
    gu = [scatter_any(unpad_hidden(g.transpose(1, 2, 0, 3).reshape(FFP, D))) for g in pairs(pgu)]
    blocks = join_strips(*pairs(pa), halves)
    if len(blocks) == 3:
        blocks = [blocks[0][..., :64], blocks[0][..., 64:]] + blocks[1:]
    return [scatter_any(natural(b)) for b in blocks] + gu + [dn]


def join_qk(q, k, parts):
    n = q.shape[0]
    both = jnp.concatenate([q.reshape(n, parts, -1), k.reshape(n, parts, -1)], axis=2)
    return both.reshape(n, -1)

def route_plan(dest_slot, block_tokens, rows, cols):
    row_count = lax.axis_size(rows)
    col_count = lax.axis_size(cols)
    per_peer = block_tokens // row_count
    row_at = lax.axis_index(rows)
    col_at = lax.axis_index(cols)
    slot_table = dest_slot.reshape(row_count, col_count, block_tokens)
    column = lax.dynamic_index_in_dim(slot_table, col_at, 1, False)
    own_slots = lax.dynamic_index_in_dim(column, row_at, 0, False)
    send_order = jnp.argsort(own_slots)
    arrived = jnp.sort(column, axis=1)
    incoming = lax.dynamic_slice_in_dim(arrived, row_at * per_peer, per_peer, 1)
    local_slots = incoming.reshape(-1) - (row_at * col_count + col_at) * block_tokens
    placing = jnp.argsort(local_slots)
    return (send_order, local_slots, placing)


def exchange(value, axis):
    n, width = value.shape
    row_count = lax.axis_size(axis)
    got = lax.all_to_all(value.reshape(row_count, n // row_count, width), axis, split_axis=0, concat_axis=0, tiled=True)
    return got.reshape(n, width)


def gather_all(shards):
    return [lax.all_gather(lax.all_gather(w, "col", axis=1, tiled=True), "row", axis=0, tiled=True) for w in shards]


def body(names, tokens, cotangent, dest_slot, lengths, pad_mask, *params):
    ring = Ring(names) if len(names) == 4 else None
    rows, cols = (names[:2], names[2:]) if ring else names
    gain_a1, bq, bk, bv, bo_w, gain_m1, wg1, wu1, wd1 = params[:9]
    gain_a2, wq, wk, wv, wo2, gain_m2, wg2, wu2, wd2 = params[9:]
    shards1, shards2 = [bq, bk, bv, bo_w, wg1, wu1, wd1], [wq, wk, wv, wo2, wg2, wu2, wd2]
    send_order, local_slots, placing = route_plan(dest_slot, T, rows, cols)
    restore = jnp.argsort(send_order)
    outgoing = after(tokens[send_order], restore, placing) if ring else tokens[send_order]
    cot_going = cotangent[send_order]
    if ring:
        me = jnp.stack([lax.axis_index(names[1]), lax.axis_index(cols)]).astype(i32)
        packs = pack([join_qk(bq, bk, 1)] + shards1[2:], HALVES_ONE) + pack(shards2, HALVES_TWO)
        flat = [jnp.concatenate(p, axis=0) for p in packs]
        mid_d2 = ring.gather_down(packs[5])
        split = lambda k, v: [v[:, : packs[k][0].shape[0]], v[:, packs[k][0].shape[0] :]]
        each = lambda pair, *arrays: [after(v, *arrays) for v in pair]
        far = lambda halves: [half[1] for half in halves]
        near_a1 = ring.gather_z(flat[0])
        hi_a1 = ring.gather_hi(ring.gather_lo(each(split(0, near_a1), mid_d2)))
        near_gu1 = ring.gather_z(after(flat[1], near_a1))
        lo_gu1 = ring.gather_lo(each(split(1, near_gu1), *far(hi_a1)))
        outgoing = after(outgoing, near_gu1, *far(hi_a1))
        arrived = exchange(outgoing, rows)
        start = arrived[placing]
    else:
        me = jnp.zeros((2,), i32)
        one, two = gather_all(shards1), gather_all(shards2)
        full = boxes_any([join_qk(one[0], one[1], COLS)] + one[2:], HALVES_ONE) + boxes_any(two, HALVES_TWO)
        start = exchange(outgoing, rows)[placing]
    position = jnp.arange(T, dtype=i32)
    segment, end = jnp.zeros((T,), i32), jnp.zeros((), i32)
    for j in range(lengths.shape[1]):
        end = end + lengths[0, j]
        segment = segment + (position >= end).astype(i32)
    seg_row, seg_col = segment.reshape(1, T), segment.reshape(T, 1)
    live_row, live_col = pad_mask.reshape(1, T), pad_mask.reshape(T, 1)

    tied = after if ring else (lambda value, *arrays: value)
    if ring:
        full_a1 = ring.gather_core(hi_a1)
        start = after(start, *lo_gu1)
    else:
        full_a1 = full[0]
    w_qk, w_v, w_o = attn_weights(full_a1, HALVES_ONE)
    xa1, qk1, v1 = norm_proj(me, start, gain_a1, [w_qk, w_v])
    if ring:
        near_d1 = ring.gather_z(after(flat[2], arrived), qk1)
    o1, ou1, rden1 = based_fwd(tied(qk1, *([near_d1] if ring else [])), v1, seg_row, seg_col, live_row)
    if ring:
        hi_gu1 = ring.gather_hi(lo_gu1, o1)
        near_a2 = ring.gather_z(after(flat[3], near_d1), o1)
    hm1, xf1 = attn_out(me, start, tied(o1, *(far(hi_gu1) + [near_a2] if ring else [])), w_o, gain_m1)
    if ring:
        full_gu1 = ring.gather_core(hi_gu1, xf1)
        lo_d1 = ring.gather_lo(each(split(2, near_d1), *far(hi_gu1)), xf1)
        xf1_late = after(xf1, *lo_d1)
    else:
        full_gu1, xf1_late = full[1], xf1
    w_g, w_u = gate_weights(full_gu1)
    g1, u1, hid1 = gate_up(me, xf1_late, w_g, w_u)
    if ring:
        hi_d1 = ring.gather_hi(lo_d1, hid1)
        lo_a2 = ring.gather_lo(each(split(3, near_a2), *lo_d1), hid1)
        near_gu2 = ring.gather_z(after(flat[4], near_a2), hid1)
        own_d1 = jnp.stack([jnp.stack(half) for half in hi_d1]).transpose(3, 0, 1, 2, 4, 5).reshape(4, FFP, 128)
        full_d1 = [own_d1, ring.swap(own_d1, "core")]
        hid1_late = after(hid1, *lo_a2)
        all_d2 = ring.gather_z_all(after(mid_d2, near_gu2))
        cot_going = after(cot_going, near_gu2)
    else:
        full_d1, hid1_late = full[2], hid1
    cot = exchange(cot_going, rows)[placing]
    w_d = DownRows(full_d1)
    h1 = down(me, hm1, hid1_late, w_d)
    if ring:
        hi_a2 = ring.gather_hi(lo_a2, h1)
        full_a2 = ring.gather_core(hi_a2)
        lo_gu2 = each(split(4, near_gu2), *far(hi_a2))
    else:
        full_a2 = full[3]
    v_q, v_k, v_v, v_o = attn_weights(full_a2, HALVES_TWO)
    xa2, q2, k2, v2 = norm_proj(me, h1, gain_a2, [v_q, v_k, v_v])
    if ring:
        lo_gu2 = ring.gather_lo(lo_gu2, q2)
    o2 = window_fwd(tied(q2, *(lo_gu2 if ring else [])), k2, v2, seg_row, seg_col, live_col)
    hm2, xf2 = attn_out(me, h1, o2, v_o, gain_m2)
    if ring:
        full_gu2 = ring.gather_core(ring.gather_hi(lo_gu2, xf2))
    else:
        full_gu2 = full[4]
    v_g, v_u = gate_weights(full_gu2)
    v_d = DownRows([all_d2, after(ring.swap(all_d2, "core"), xf2)] if ring else full[5])
    g2, u2, hid2 = gate_up(me, xf2, v_g, v_u)

    dg2, du2, *d2 = down_bwd(me, cot, v_d, hid2, g2, u2)
    if ring:
        r_d2 = ring.send(d2[1:], ("core",))
    h2 = down(me, hm2, hid2, v_d)
    outgoing = h2.astype(bf16)[local_slots]
    gu2 = gate_up_bwd(me, xf2, dg2, du2)
    if ring:
        dg2, du2, gu2, r_d2, outgoing = sync(dg2, du2, gu2, r_d2, outgoing)
        z_d2 = ring.scatter_z(d2[0] + r_d2[0])
        r_gu2 = ring.send(gu2[1::2], ("core", "core"))
    output = exchange(outgoing, rows)
    gm2, bo2, dor2, gg_m2 = mlp_dx(me, dg2, du2, v_g, v_u, hm2, gain_m2, cot, v_o, bf16)
    if ring:
        gm2, bo2, dor2, gg_m2, r_gu2 = sync(gm2, bo2, dor2, gg_m2, r_gu2)
        keep_gu2, go = add_core(gu2, r_gu2)
        r_gu2 = ring.send(go, ("x", "y"))
    dq2, dk2, dv2 = window_bwd(q2, k2, v2, dor2, seg_row, seg_col, live_col)
    *a2, gh1, gg_a2 = attn_bwd(me, xa2, [dq2, dk2, dv2], [v_q, v_k, v_v], o2, bo2, h1, gain_a2, gm2, HALVES_TWO)
    if ring:
        a2, gh1, gg_a2, r_gu2, z_d2, output = sync(a2, gh1, gg_a2, r_gu2, z_d2, output)
        keep_gu2, go = add_two(keep_gu2, r_gu2)
        r_gu2 = ring.send(go, ("y", "x"))
        r_a2 = ring.send(a2[1::2], ("core", "core"))
    dg1, du1, *d1 = down_bwd(me, gh1, w_d, hid1, g1, u1)
    if ring:
        dg1, du1, d1, r_gu2, r_a2 = sync(dg1, du1, d1, r_gu2, r_a2)
        z_gu2 = ring.scatter_z(jnp.concatenate(add_one(keep_gu2, r_gu2), axis=1))
        keep_a2, go = add_core(a2, r_a2)
        r_a2 = ring.send(go, ("x", "y"))
        r_d1 = ring.send(d1[1:], ("core",))
    gu1 = gate_up_bwd(me, xf1, dg1, du1)
    if ring:
        gu1, r_a2, r_d1 = sync(gu1, r_a2, r_d1)
        keep_a2, go = add_two(keep_a2, r_a2)
        r_a2 = ring.send(go, ("y", "x"))
        r_gu1 = ring.send(gu1[1::2], ("core", "core"))
        z_d1 = ring.scatter_z(d1[0] + r_d1[0])
    gm1, bo1, dou1, gg_m1 = mlp_dx(me, dg1, du1, w_g, w_u, hm1, gain_m1, gh1, w_o, f32)
    if ring:
        gm1, bo1, dou1, gg_m1, r_a2, r_gu1 = sync(gm1, bo1, dou1, gg_m1, r_a2, r_gu1)
        n_a2 = keep_a2[0].shape[1]
        z_a2 = ring.scatter_z(jnp.concatenate(add_one(keep_a2, r_a2), axis=1))
        keep_gu1, go = add_core(gu1, r_gu1)
        r_gu1 = ring.send(go, ("x", "y"))
    dqk1, dv1 = based_bwd(qk1, v1, dou1, ou1, rden1, seg_row, seg_col, live_col)
    if ring:
        dqk1, dv1, r_gu1 = sync(dqk1, dv1, r_gu1)
        keep_gu1, go = add_two(keep_gu1, r_gu1)
        r_gu1 = ring.send(go, ("y", "x"))
    *a1, g0, gg_a1 = attn_bwd(me, xa1, [dqk1, dv1], [w_qk, w_v], o1, bo1, start, gain_a1, gm1, HALVES_ONE)
    output = output[restore]
    gains = jnp.concatenate([gg_a1, gg_m1, gg_a2, gg_m2], axis=0)
    if ring:
        a1, g0, gains, r_gu1, z_gu2, z_d1 = sync(a1, g0, gains, r_gu1, z_gu2, z_d1)
        gu1 = jnp.concatenate(add_one(keep_gu1, r_gu1), axis=1)
        r_a1 = ring.send(a1[1::2], ("core", "core"))
        r_gains = ring.send([gains], ("core",))
        keep_d1, go = far_rows(jnp.stack([z_d1, z_d2]))
        r_d1 = ring.send(go, ("y", "x"))
        r_z = ring.send_back(gu1)
        r_a1, r_gains, r_d1, g0 = sync(r_a1, r_gains, r_d1, g0)
        outgoing = g0.astype(bf16)[local_slots]
        r_z, outgoing, z_a2 = sync(r_z, outgoing, z_a2)
        arrived = exchange(outgoing, rows)
        keep_a1, go = add_core(a1, r_a1)
        r_a1 = ring.send(go, ("x", "y"))
        gains = gains + r_gains[0]
        r_gains = ring.send([gains], ("x",))
        keep_d1, go = near_rows(add_one(keep_d1, r_d1))
        r_d1 = ring.send(go, ("x", "y"))
        r_a1, r_gains, r_d1 = sync(r_a1, r_gains, r_d1)
        keep_a1, go = add_two(keep_a1, r_a1)
        r_a1 = ring.send(go, ("y", "x"))
        gains = gains + r_gains[0]
        r_gains = ring.send([gains], ("y",))
        sum_d1, sum_d2 = ([v[k] for v in add_one(keep_d1, r_d1)] for k in range(2))
        last_gu1 = ring.add_back(gu1, r_z)
        r_a1, r_gains, arrived = sync(r_a1, r_gains, arrived)
        a1 = jnp.concatenate(add_one(keep_a1, r_a1), axis=1)
        last_a1 = ring.add_back(a1, ring.send_back(a1))
        gains = gains + r_gains[0]
        far_z = [ring.swap(gains, "z", by) for by in (1, 2, 3)]
        gains = (gains + far_z[0]) + (far_z[1] + far_z[2])
        cut = lambda v, n: [v[:n].astype(f32), v[n:].astype(f32)]
        sum_gu1, sum_a1 = cut(last_gu1, FC), cut(last_a1, 128 * len(HALVES_ONE[0]))
        sum_gu2, sum_a2 = cut(z_gu2, FC), cut(z_a2, n_a2)
        tokens_grad = arrived
        wide = lambda halves: [h.astype(f32) for h in halves]
        sum_d1, sum_d2 = wide(sum_d1), wide(sum_d2)
        rest = sum_parts(sum_a2, sum_gu2, sum_d2, HALVES_TWO)
        sums1, sums2 = sum_parts(sum_a1, sum_gu1, sum_d1, HALVES_ONE), rest
        sums1 = [sums1[0][:, :64], sums1[0][:, 64:]] + sums1[1:]
        tokens_grad = tokens_grad[restore]
    else:
        sums1 = sum_any(d1, gu1, a1, HALVES_ONE)
        sums2 = sum_any(d2, gu2, a2, HALVES_TWO)
        gains = lax.psum(gains, ("row", "col"))
        tokens_grad = exchange(g0.astype(bf16)[local_slots], rows)[restore]
    return (
        output, tokens_grad,
        gains[0], *sums1[:4], gains[1], *sums1[4:],
        gains[2], *sums2[:4], gains[3], *sums2[4:],
    )


def solution(mesh):
    names, rows, cols = ("row", "col"), "row", "col"
    if (mesh.shape["row"], mesh.shape["col"]) == (ROWS, COLS):
        names = ("z", "y", "x", "core")
        rows, cols = names[:2], names[2:]
        mesh = Mesh(mesh.devices.reshape(4, 2, 2, 2), names)
    block, weight = P(names, None), P(rows, cols)
    layer_in = (P(),) + (weight,) * 4 + (P(),) + (weight,) * 3
    return jax.shard_map(
        functools.partial(body, names),
        mesh=mesh,
        in_specs=(block, block, P(), block, P(names)) + layer_in * 2,
        out_specs=(block, block) + layer_in * 2,
        check_vma=False,
    )
```
